32 devices in a mesh: grp: 2 (over x), row: 8 (over z, y), col: 2 (over core).
Axes of the slice: x: 2, y: 2, z: 4, core: 2. Of those that a mesh axis runs over, the one named last changes fastest.
Arguments:
- pair_rep: bfloat16 [512, 256, 128], P(('grp', 'row'), 'col'), parts along dimension 0, may hold values from -6 to 6
- cotangent: bfloat16 [512, 256, 128], P(('grp', 'row'), 'col'), parts along dimension 0, may hold values from -6 to 6
- residue_mask: int32 [512], P('grp'), parts along dimension 0, may hold values 0 or 1
- chain_ids: int32 [512], P('grp'), parts along dimension 0, may hold values from 0 to 5, never falling along the last dimension, each value on 1 to 64 neighbouring positions
- proj_weight: bfloat16 [2, 128, 640], replicated, may hold values from -0.5 to 0.5
- out_weight: bfloat16 [2, 128, 128], replicated, may hold values from -0.5 to 0.5
- input_gain: float32 [2, 128], replicated, may hold values from 0.25 to 1.75
- input_bias: float32 [2, 128], replicated, may hold values from -3 to 3
- hidden_gain: float32 [2, 128], replicated, may hold values from 0.25 to 1.75
- hidden_bias: float32 [2, 128], replicated, may hold values from -3 to 3
- chain_bias: float32 [2, 128], replicated, may hold values from -4 to 4
Outputs:
- grad_pair: bfloat16 [512, 256, 128], P(('grp', 'row'), 'col'), parts along dimension 0
- grad_proj: float32 [4, 128, 640], P('grp'), parts along dimension 0
- grad_output_weight: float32 [4, 128, 128], P('grp'), parts along dimension 0
- grad_input_norm: float32 [4, 2, 128], P('grp'), parts along dimension 0
- grad_hidden_norm: float32 [4, 2, 128], P('grp'), parts along dimension 0
- grad_chain: float32 [4, 128], P('grp'), parts along dimension 0
The draws below stay inside these ranges and needn't reach their ends.
There are 2 independent parts, one for each index of `grp`. The reference program is written for one: setup_inputs(seed, part) draws one part's arguments, and reference() takes and returns one part's arrays. A program takes and returns all parts, laid end to end along the dimension named above; an argument that names none is the same for every part. Nothing has to cross between parts.
Inputs may be any that keep to these rules, and one draw needn't show every extreme that they name: `chain_ids`: chain numbers never fall along the residues.
All inputs are finite; a program needn't handle non-finite values.
Results may differ from the reference program's by a relative error of at most 0.018.
Values may be sent and summed in bfloat16 or wider, within the bound.
No kernel may reach another device: no remote copies, remote signals or barrier semaphores. Data moves between devices by JAX's collectives and lax.ppermute only.
A program may use at most 128 MiB of HBM per device.

```python
import math
import jax
import jax.numpy as jnp
import numpy as np
from jax import lax

N = 256
C = 128
HID = 128
CHAINS = 6


def with_ends(array, own_key, least, largest):
    shape = array.shape
    place = [jax.random.randint(jax.random.fold_in(own_key, axis), (), 0, shape[axis]) for axis in range(len(shape))]
    array = array.at[tuple(place)].set(least)
    longest = shape.index(max(shape))
    place[longest] = (place[longest] + 1) % shape[longest]
    return array.at[tuple(place)].set(largest)


def block_scale(rng, dims, pieces, smallest, top_value):
    gain, own = 1.0, jax.random.fold_in(rng, 6)
    for axis_at, blocks in pieces:
        heights = jnp.exp(jax.random.uniform(jax.random.fold_in(own, axis_at), (blocks,), jnp.float32, smallest / len(pieces), top_value / len(pieces)))
        gain = gain * jnp.repeat(heights, dims[axis_at] // blocks).reshape([-1 if axis == axis_at else 1 for axis in range(len(dims))])
    return gain


def length_profile(amount, total, limit, slope):
    loads = [(1 << 20) // math.isqrt(standing ** slope) + 1 for standing in range(2, amount + 1)]
    spare, given = total - limit - (amount - 1), [1] * (amount - 1)
    while spare > 0:
        free = [i for i in range(amount - 1) if given[i] < limit]
        mass, budget = sum([loads[i] for i in free]), spare
        for i in free:
            more = min(limit - given[i], max(1, budget * loads[i] // mass), spare)
            given[i] = given[i] + more
            spare = spare - more
    return np.array([limit] + given)


def uneven_parts(key, number_of, total, most, slope):
    if number_of == 2:
        one = jax.random.randint(key, (), max(1, total - most), min(most, total - 1) + 1)
        return jnp.stack([one, total - one])
    tallies = jnp.asarray(length_profile(number_of, total, most, slope), jnp.int32)
    couples = (number_of - 1) // 2
    giver, receiver = tallies[1:1 + 2 * couples:2], tallies[2:2 + 2 * couples:2]
    margin = jnp.minimum(giver - 1, most - receiver)
    moved = jax.random.randint(jax.random.fold_in(key, 1), (couples,), 0, 1 << 20) % (margin + 1)
    tallies = tallies.at[1:1 + 2 * couples:2].set(giver - moved).at[2:2 + 2 * couples:2].set(receiver + moved)
    return tallies[jax.random.permutation(jax.random.fold_in(key, 2), number_of)]


def gaussian(own_key, extent, deviation, most, pieces=(), held_as=jnp.bfloat16):
    gain = block_scale(own_key, extent, pieces, -0.22, 0.18) if pieces else 1.0
    entries = jax.random.normal(own_key, extent, jnp.float32) * deviation * gain
    return jnp.minimum(jnp.maximum(entries, -most), most).astype(held_as)


def setup_inputs(seed: int = 0, part: int = 0) -> dict:
    key_list = jax.random.split(jax.random.key(seed), 12)
    part_keys = jax.random.split(jax.random.fold_in(key_list[11], part), 12)
    return {
        "pair_rep": gaussian(part_keys[0], (N, N, C), 1.0, 6.0, ((0, 8), (1, 2))),
        "cotangent": gaussian(part_keys[1], (N, N, C), 1.0, 6.0, ((0, 8), (1, 2))),
        "residue_mask": with_ends((jax.random.randint(part_keys[2], (N,), 0, 8) < 7).astype(jnp.int32), jax.random.fold_in(part_keys[2], 1), 0, 1),
        "chain_ids": jnp.searchsorted(jnp.cumsum(uneven_parts(part_keys[3], CHAINS, N, N // 4, 2)), jnp.arange(N), side="right").astype(jnp.int32),
        "proj_weight": gaussian(key_list[4], (2, C, 4 * HID + C), C ** -0.5, 0.5),
        "out_weight": gaussian(key_list[5], (2, HID, C), HID ** -0.5, 0.5),
        "input_gain": jnp.clip(1.0 + 0.15 * jax.random.normal(key_list[6], (2, C), jnp.float32), 0.25, 1.75),
        "input_bias": gaussian(key_list[7], (2, C), 0.5, 3.0, (), jnp.float32),
        "hidden_gain": jnp.clip(1.0 + 0.15 * jax.random.normal(key_list[8], (2, HID), jnp.float32), 0.25, 1.75),
        "hidden_bias": gaussian(key_list[9], (2, HID), 0.5, 3.0, (), jnp.float32),
        "chain_bias": gaussian(key_list[10], (2, C), 1.0, 4.0, (), jnp.float32),
    }


EPSILON = 1e-05

def norm_forward(values, norm_gain, norm_bias):
    average = lax.optimization_barrier(jnp.mean(values, -1, keepdims=True))
    centred = values - average
    inv_std = lax.rsqrt(lax.optimization_barrier(jnp.mean(centred * centred, -1, keepdims=True)) + EPSILON)
    normed = centred * inv_std
    return (normed, inv_std, normed * norm_gain + norm_bias)

def norm_backward(grad_scaled, normed, inv_std, norm_gain):
    grad_normed = grad_scaled * norm_gain
    first_mean = lax.optimization_barrier(jnp.mean(grad_normed, -1, keepdims=True))
    second_mean = lax.optimization_barrier(jnp.mean(grad_normed * normed, -1, keepdims=True))
    grad_values = (grad_normed - first_mean - normed * second_mean) * inv_std
    return (grad_values, lax.optimization_barrier(jnp.sum(grad_scaled * normed, 0)), lax.optimization_barrier(jnp.sum(grad_scaled, 0)))

def edge_forward(cells, weight, norm_gain, norm_bias, pair_mask, same_chain, chain_vec, hidden):
    normed, inv_std, scaled = norm_forward(cells, norm_gain, norm_bias)
    lowered = scaled.astype(jnp.bfloat16)
    projected = jnp.dot(lowered, weight, preferred_element_type=jnp.float32)
    left_edge = projected[:, :hidden] * jax.nn.sigmoid(projected[:, hidden:2 * hidden]) * pair_mask[:, None]
    right_edge = projected[:, 2 * hidden:3 * hidden] * jax.nn.sigmoid(projected[:, 3 * hidden:4 * hidden]) * pair_mask[:, None]
    logits = projected[:, 4 * hidden:] + same_chain[:, None] * chain_vec
    return (left_edge.astype(jnp.bfloat16), right_edge.astype(jnp.bfloat16), logits, (normed, inv_std, lowered, projected))

def edge_backward(grad_left, grad_right, grad_logits, stored, weight, norm_gain, pair_mask, same_chain, hidden):
    normed, inv_std, lowered, projected = stored
    left_sig = jax.nn.sigmoid(projected[:, hidden:2 * hidden])
    right_sig = jax.nn.sigmoid(projected[:, 3 * hidden:4 * hidden])
    masked_left = grad_left * pair_mask[:, None]
    masked_right = grad_right * pair_mask[:, None]
    grad_projected = jnp.concatenate([masked_left * left_sig, masked_left * projected[:, :hidden] * left_sig * (1.0 - left_sig), masked_right * right_sig, masked_right * projected[:, 2 * hidden:3 * hidden] * right_sig * (1.0 - right_sig), grad_logits], 1).astype(jnp.bfloat16)
    grad_weight = jnp.dot(lowered.T, grad_projected, preferred_element_type=jnp.float32)
    grad_scaled = jnp.dot(grad_projected, weight.T, preferred_element_type=jnp.float32)
    grad_cells, grad_gain, grad_bias = norm_backward(grad_scaled, normed, inv_std, norm_gain)
    grad_chain = lax.optimization_barrier(jnp.sum(grad_logits * same_chain[:, None], 0))
    return (grad_cells, grad_weight, grad_gain, grad_bias, grad_chain)

def mix_forward(product_cells, logits, weight, norm_gain, norm_bias):
    normed, inv_std, scaled = norm_forward(product_cells.astype(jnp.float32), norm_gain, norm_bias)
    lowered = scaled.astype(jnp.bfloat16)
    mixed = jnp.dot(lowered, weight, preferred_element_type=jnp.float32)
    gate_vals = jax.nn.sigmoid(logits)
    return (gate_vals * mixed, (normed, inv_std, lowered, mixed, gate_vals))

def mix_backward(upstream, stored, weight, norm_gain):
    normed, inv_std, lowered, mixed, gate_vals = stored
    grad_logits = upstream * mixed * gate_vals * (1.0 - gate_vals)
    grad_mixed = (upstream * gate_vals).astype(jnp.bfloat16)
    grad_weight = jnp.dot(lowered.T, grad_mixed, preferred_element_type=jnp.float32)
    grad_scaled = jnp.dot(grad_mixed, weight.T, preferred_element_type=jnp.float32)
    grad_product, grad_gain, grad_bias = norm_backward(grad_scaled, normed, inv_std, norm_gain)
    return (grad_product.astype(jnp.bfloat16), grad_logits, grad_weight, grad_gain, grad_bias)
FORWARD_FORMS = ('cik,cjk->cij', 'cki,ckj->cij')

def tri_product(formula, first_edge, second_edge):
    return jnp.einsum(formula, first_edge.astype(jnp.float32), second_edge.astype(jnp.float32), precision=lax.Precision.HIGHEST).astype(jnp.bfloat16)

def reference(pair_rep, cotangent, residue_mask, chain_ids, proj_weight, out_weight, input_gain, input_bias, hidden_gain, hidden_bias, chain_bias):
    length, _, width = pair_rep.shape
    hidden = out_weight.shape[1]
    pair_mask = (residue_mask[:, None] * residue_mask[None, :]).astype(jnp.float32).reshape(-1)
    same_chain = (chain_ids[:, None] == chain_ids[None, :]).astype(jnp.float32).reshape(-1)
    cells = pair_rep.reshape(-1, width).astype(jnp.float32)

    def to_channels(edge):
        return edge.reshape(length, length, hidden).transpose(2, 0, 1)

    def to_cells(channels):
        return channels.transpose(1, 2, 0).reshape(-1, hidden)
    records = []
    for layer_no in range(2):
        left_edge, right_edge, logits, edge_store = edge_forward(cells, proj_weight[layer_no], input_gain[layer_no], input_bias[layer_no], pair_mask, same_chain, chain_bias[layer_no], hidden)
        left_chan = to_channels(left_edge)
        right_chan = to_channels(right_edge)
        product = tri_product(FORWARD_FORMS[layer_no], left_chan, right_chan)
        mixed_out, mix_store = mix_forward(to_cells(product), logits, out_weight[layer_no], hidden_gain[layer_no], hidden_bias[layer_no])
        records.append((left_chan, right_chan, edge_store, mix_store))
        cells = cells + mixed_out
    upstream = cotangent.reshape(-1, width).astype(jnp.float32)
    grads = [None, None]
    for layer_no in (1, 0):
        left_chan, right_chan, edge_store, mix_store = records[layer_no]
        grad_prod, grad_logits, grad_outw, grad_hgain, grad_hbias = mix_backward(upstream, mix_store, out_weight[layer_no], hidden_gain[layer_no])
        grad_chan = to_channels(grad_prod)
        if layer_no == 0:
            grad_left = tri_product('cij,cjk->cik', grad_chan, right_chan)
            grad_right = tri_product('cij,cik->cjk', grad_chan, left_chan)
        else:
            grad_left = tri_product('ckj,cij->cki', right_chan, grad_chan)
            grad_right = tri_product('cki,cij->ckj', left_chan, grad_chan)
        grad_cells, grad_weight, grad_gain, grad_bias, grad_chain = edge_backward(to_cells(grad_left).astype(jnp.float32), to_cells(grad_right).astype(jnp.float32), grad_logits, edge_store, proj_weight[layer_no], input_gain[layer_no], pair_mask, same_chain, hidden)
        upstream = upstream + grad_cells
        grads[layer_no] = (grad_weight, grad_outw, jnp.stack([grad_gain, grad_bias]), jnp.stack([grad_hgain, grad_hbias]), grad_chain)
    factor = 1.0 / length
    stacked = [jnp.stack([grads[0][member], grads[1][member]]) * factor for member in range(5)]
    grad_pair = upstream.reshape(length, length, width).astype(jnp.bfloat16)
    return (grad_pair, stacked[0], stacked[1], stacked[2], stacked[3], stacked[4])
```

```python
import functools

import jax
import jax.numpy as jnp
from jax import lax
from jax.experimental import pallas as pl
from jax.experimental.pallas import tpu as pltpu
from jax.sharding import PartitionSpec as P

EPSILON = 1e-05
AXES = ("row", "col")
F32 = jnp.float32
BF16 = jnp.bfloat16
VMEM_BYTES = 50 * 1024 * 1024


def dot(a, b, ca, cb):
    return lax.dot_general(a, b, (((ca,), (cb,)), ((), ())), preferred_element_type=F32)


def sigmoid(x):
    return 0.5 * jnp.tanh(0.5 * x) + 0.5


def columns(vectors, width):
    c = vectors.shape[1]
    square = jnp.broadcast_to(vectors, (c, c)).T
    return jnp.concatenate([square] * (width // c), 1)


def norm(x):
    centred = x - jnp.mean(x, 0, keepdims=True)
    inv = lax.rsqrt(jnp.mean(centred * centred, 0, keepdims=True) + EPSILON)
    return centred * inv, inv


def norm_grad(grad_scaled, normed, inv, gain):
    g = grad_scaled * gain
    first = jnp.mean(g, 0, keepdims=True)
    second = jnp.mean(g * normed, 0, keepdims=True)
    return (g - first - normed * second) * inv


def unpack(block, cpd):
    devices, rows, cols = block.shape
    values = block.astype(F32)
    parts = []
    for a in range(rows // cpd):
        if cpd % 8 == 0:
            parts.append(values[:, a * cpd : (a + 1) * cpd, :].reshape(devices * cpd, cols))
        else:
            parts.append(
                jnp.concatenate([values[d, a * cpd : (a + 1) * cpd, :] for d in range(devices)], 0)
            )
    return jnp.concatenate(parts, 1)


def pack(tile, cpd, cols):
    channels, lanes = tile.shape
    devices = channels // cpd
    parts = [tile[:, a * cols : (a + 1) * cols] for a in range(lanes // cols)]
    if cpd % 8 == 0:
        return jnp.concatenate([p.reshape(devices, cpd, cols) for p in parts], 1).astype(BF16)
    return jnp.stack(
        [
            jnp.concatenate([p[d * cpd : (d + 1) * cpd, :] for p in parts], 0)
            for d in range(devices)
        ]
    ).astype(BF16)


def fold(tile, width):
    return sum(tile[:, a : a + width] for a in range(0, tile.shape[1], width))


def project(cells, wt_ref, gain, bias, hidden, blocks):
    normed, inv = norm(cells)
    lowered = (normed * gain + bias).astype(BF16)
    projected = dot(wt_ref[: blocks * hidden, :], lowered, 1, 0)
    return normed, inv, lowered, projected


def emit_edges(cells, wt_ref, gain, bias, chain, mask, same, hidden, cpd, cols):
    _, _, _, projected = project(cells, wt_ref, gain, bias, hidden, 5)
    part = [projected[n * hidden : (n + 1) * hidden] for n in range(5)]
    left = part[0] * sigmoid(part[1]) * mask
    right = part[2] * sigmoid(part[3]) * mask
    gate = sigmoid(part[4] + same * chain)
    return pack(left, cpd, cols), pack(right, cpd, cols), gate


def edge_first_kernel(
    cpd, q, mask_smem, chain_smem, start_smem, pair_ref, cot_ref, maskc_ref, chainc_ref, wt_ref,
    gain_ref, bias_ref, chain_ref, edges_ref, z_ref, up_ref, gate_ref, flags_ref, vec,
):
    tiles, channels, lanes = z_ref.shape
    hidden = wt_ref.shape[0] // 5
    cols = lanes // q
    step = pl.program_id(0)

    @pl.when(step == 0)
    def _():
        vec[0] = columns(gain_ref[0:1, :], lanes)
        vec[1] = columns(bias_ref[0:1, :], lanes)
        vec[2] = columns(chain_ref[0:1, :], lanes)

    for t in range(tiles):
        z_parts, u_parts, m_parts, s_parts = [], [], [], []
        for a in range(q):
            row = t * q + a
            z_parts.append(pair_ref[row].astype(F32).T)
            u_parts.append(cot_ref[row].astype(F32).T)
            whole = start_smem[0] + step * (tiles * q) + row
            m_parts.append(maskc_ref[pl.ds(start_smem[1], 1), :] * mask_smem[whole])
            s_parts.append((chainc_ref[pl.ds(start_smem[1], 1), :] == chain_smem[whole]).astype(F32))
        cells = jnp.concatenate(z_parts, 1)
        mask = jnp.concatenate(m_parts, 1).astype(F32)
        same = jnp.concatenate(s_parts, 1)
        left, right, gate = emit_edges(
            cells, wt_ref, vec[0], vec[1], vec[2], mask, same, hidden, cpd, cols
        )
        edges_ref[:, 0, t * q * cpd : (t + 1) * q * cpd, :] = left
        edges_ref[:, 1, t * q * cpd : (t + 1) * q * cpd, :] = right
        z_ref[t] = cells.astype(BF16)
        up_ref[t] = jnp.concatenate(u_parts, 1).astype(BF16)
        gate_ref[t] = gate
        flags_ref[t] = jnp.concatenate([mask, same], 0)


def mix_edge_kernel(
    cpd, q, layer, prod_ref, z_ref, gate_ref, flags_ref, owt_ref, hgain_ref, hbias_ref, wt_ref,
    gain_ref, bias_ref, chain_ref, edges_ref, znext_ref, gatenext_ref, vec,
):
    tiles, channels, lanes = z_ref.shape
    hidden = wt_ref.shape[0] // 5
    cols = lanes // q
    rows = q * cpd

    @pl.when(pl.program_id(0) == 0)
    def _():
        vec[0] = columns(hgain_ref[layer : layer + 1, :], lanes)
        vec[1] = columns(hbias_ref[layer : layer + 1, :], lanes)
        vec[2] = columns(gain_ref[layer + 1 : layer + 2, :], lanes)
        vec[3] = columns(bias_ref[layer + 1 : layer + 2, :], lanes)
        vec[4] = columns(chain_ref[layer + 1 : layer + 2, :], lanes)

    for t in range(tiles):
        mask, same = flags_ref[t, 0:1, :], flags_ref[t, 1:2, :]
        hnormed, _ = norm(unpack(prod_ref[:, t * rows : (t + 1) * rows, :], cpd))
        hscaled = (hnormed * vec[0] + vec[1]).astype(BF16)
        cells = z_ref[t].astype(F32) + gate_ref[t] * dot(owt_ref[...], hscaled, 1, 0)
        left, right, gate = emit_edges(
            cells, wt_ref, vec[2], vec[3], vec[4], mask, same, hidden, cpd, cols
        )
        edges_ref[:, 0, t * rows : (t + 1) * rows, :] = left
        edges_ref[:, 1, t * rows : (t + 1) * rows, :] = right
        znext_ref[t] = cells
        gatenext_ref[t] = gate


def mix_back(upstream, product, gate, same, ow_ref, owt_ref, hgain, hbias, acc_ow, acc_hg, acc_hb, acc_ch):
    width = acc_hg.shape[1]
    hnormed, hinv = norm(product)
    hscaled = (hnormed * hgain + hbias).astype(BF16)
    mixed = dot(owt_ref[...], hscaled, 1, 0)
    grad_gate = upstream * gate
    grad_logits = grad_gate * mixed * (1.0 - gate)
    grad_mixed = grad_gate.astype(BF16)
    acc_ow[...] += dot(hscaled, grad_mixed, 1, 1)
    grad_hscaled = dot(ow_ref[...], grad_mixed, 1, 0)
    acc_hg[...] += fold(grad_hscaled * hnormed, width)
    acc_hb[...] += fold(grad_hscaled, width)
    acc_ch[...] += fold(grad_logits * same, width)
    return norm_grad(grad_hscaled, hnormed, hinv, hgain), grad_logits


def row_of(acc):
    return jnp.sum(acc.T, 0, keepdims=True)


def finish_mix(out_ref, acc_ow, acc_hg, acc_hb, acc_ch):
    hidden = acc_ow.shape[0]
    out_ref[:hidden, :] = acc_ow[...]
    rows = [row_of(acc_hg[...]), row_of(acc_hb[...]), row_of(acc_ch[...])]
    rows.append(jnp.zeros((out_ref.shape[0] - hidden - 3, hidden), F32))
    out_ref[hidden:, :] = jnp.concatenate(rows, 0)


def mix_back_kernel(
    cpd, q, layer, prod_ref, up_ref, gate_ref, flags_ref, ow_ref, owt_ref, hgain_ref, hbias_ref,
    gp_ref, glog_ref, terms_ref, vec, acc_ow, acc_hg, acc_hb, acc_ch,
):
    tiles, channels, lanes = up_ref.shape
    cols = lanes // q
    rows = q * cpd

    @pl.when(pl.program_id(0) == 0)
    def _():
        vec[0] = columns(hgain_ref[layer : layer + 1, :], lanes)
        vec[1] = columns(hbias_ref[layer : layer + 1, :], lanes)
        for acc in (acc_ow, acc_hg, acc_hb, acc_ch):
            acc[...] = jnp.zeros_like(acc)

    for t in range(tiles):
        grad_product, grad_logits = mix_back(
            up_ref[t].astype(F32),
            unpack(prod_ref[:, t * rows : (t + 1) * rows, :], cpd),
            gate_ref[t], flags_ref[t, 1:2, :], ow_ref, owt_ref, vec[0], vec[1],
            acc_ow, acc_hg, acc_hb, acc_ch,
        )
        gp_ref[:, t * rows : (t + 1) * rows, :] = pack(grad_product, cpd, cols)
        glog_ref[t] = grad_logits.astype(BF16)

    @pl.when(pl.program_id(0) == pl.num_programs(0) - 1)
    def _():
        finish_mix(terms_ref, acc_ow, acc_hg, acc_hb, acc_ch)


def edge_back(
    cells, upstream, grad_left, grad_right, glog, mask, wt_ref, w_ref, gain, bias, hidden, acc_w, acc_g, acc_b
):
    width = acc_g.shape[1]
    normed, inv, lowered, projected = project(cells, wt_ref, gain, bias, hidden, 4)
    part = [projected[n * hidden : (n + 1) * hidden] for n in range(4)]
    blocks = []
    for grad, value, logit in ((grad_left, part[0], part[1]), (grad_right, part[2], part[3])):
        sig = sigmoid(logit)
        opened = grad * mask * sig
        blocks += [opened.astype(BF16), (opened * value * (1.0 - sig)).astype(BF16)]
    grad_projected = jnp.concatenate(blocks + [glog], 0)
    acc_w[...] += dot(lowered, grad_projected, 1, 1)
    grad_scaled = dot(w_ref[...], grad_projected, 1, 0)
    acc_g[...] += fold(grad_scaled * normed, width)
    acc_b[...] += fold(grad_scaled, width)
    return upstream + norm_grad(grad_scaled, normed, inv, gain)


def finish_edge(out_ref, mix_ref, acc_w, acc_g, acc_b):
    hidden = acc_w.shape[0]
    for n in range(5):
        out_ref[n * hidden : (n + 1) * hidden, :] = acc_w[:, n * hidden : (n + 1) * hidden].astype(BF16)
    out_ref[5 * hidden : 6 * hidden, :] = mix_ref[:hidden, :].astype(BF16)
    rows = [
        row_of(acc_g[...]), row_of(acc_b[...]), mix_ref[hidden : hidden + 3, :],
        jnp.zeros((out_ref.shape[0] - 6 * hidden - 5, hidden), F32),
    ]
    out_ref[6 * hidden :, :] = jnp.concatenate(rows, 0).astype(BF16)


def edge_mix_back_kernel(
    cpd, q, layer, grads_ref, z_ref, glog_ref, up_ref, flags_ref, wt_ref, w_ref, gain_ref, bias_ref,
    terms_in_ref, prod_ref, gate_ref, ow_ref, owt_ref, hgain_ref, hbias_ref,
    upnext_ref, gp_ref, glognext_ref, all_ref, terms_ref,
    vec, acc_w, acc_g, acc_b, acc_ow, acc_hg, acc_hb, acc_ch,
):
    tiles, channels, lanes = z_ref.shape
    hidden = wt_ref.shape[0] // 5
    cols = lanes // q
    rows = q * cpd

    @pl.when(pl.program_id(0) == 0)
    def _():
        vec[0] = columns(gain_ref[layer : layer + 1, :], lanes)
        vec[1] = columns(bias_ref[layer : layer + 1, :], lanes)
        vec[2] = columns(hgain_ref[layer - 1 : layer, :], lanes)
        vec[3] = columns(hbias_ref[layer - 1 : layer, :], lanes)
        for acc in (acc_w, acc_g, acc_b, acc_ow, acc_hg, acc_hb, acc_ch):
            acc[...] = jnp.zeros_like(acc)

    for t in range(tiles):
        here = slice(t * rows, (t + 1) * rows)
        upstream = edge_back(
            z_ref[t], up_ref[t].astype(F32), unpack(grads_ref[:, 0, here, :], cpd),
            unpack(grads_ref[:, 1, here, :], cpd), glog_ref[t], flags_ref[t, 0:1, :],
            wt_ref, w_ref, vec[0], vec[1], hidden, acc_w, acc_g, acc_b,
        )
        upnext_ref[t] = upstream
        grad_product, grad_logits = mix_back(
            upstream, unpack(prod_ref[:, here, :], cpd), gate_ref[t], flags_ref[t, 1:2, :],
            ow_ref, owt_ref, vec[2], vec[3], acc_ow, acc_hg, acc_hb, acc_ch,
        )
        gp_ref[:, here, :] = pack(grad_product, cpd, cols)
        glognext_ref[t] = grad_logits.astype(BF16)

    @pl.when(pl.program_id(0) == pl.num_programs(0) - 1)
    def _():
        finish_edge(all_ref, terms_in_ref, acc_w, acc_g, acc_b)
        finish_mix(terms_ref, acc_ow, acc_hg, acc_hb, acc_ch)


def edge_back_kernel(
    cpd, q, layer, grads_ref, z_ref, glog_ref, up_ref, flags_ref, wt_ref, w_ref, gain_ref, bias_ref,
    terms_in_ref, pair_ref, all_ref, vec, acc_w, acc_g, acc_b,
):
    tiles, channels, lanes = z_ref.shape
    hidden = wt_ref.shape[0] // 5
    cols = lanes // q
    rows = q * cpd

    @pl.when(pl.program_id(0) == 0)
    def _():
        vec[0] = columns(gain_ref[layer : layer + 1, :], lanes)
        vec[1] = columns(bias_ref[layer : layer + 1, :], lanes)
        for acc in (acc_w, acc_g, acc_b):
            acc[...] = jnp.zeros_like(acc)

    for t in range(tiles):
        here = slice(t * rows, (t + 1) * rows)
        upstream = edge_back(
            z_ref[t].astype(F32), up_ref[t], unpack(grads_ref[:, 0, here, :], cpd),
            unpack(grads_ref[:, 1, here, :], cpd), glog_ref[t], flags_ref[t, 0:1, :],
            wt_ref, w_ref, vec[0], vec[1], hidden, acc_w, acc_g, acc_b,
        )
        for a in range(q):
            pair_ref[t * q + a] = upstream[:, a * cols : (a + 1) * cols].T.astype(BF16)

    @pl.when(pl.program_id(0) == pl.num_programs(0) - 1)
    def _():
        finish_edge(all_ref, terms_in_ref, acc_w, acc_g, acc_b)


def cell_call(kernel, steps, ins, outs, scratch, prefetch=(), flops=0):
    def spec(shape, how):
        if how is None:
            return pl.BlockSpec(shape, lambda *s: (0,) * len(shape))
        block = tuple(n // steps if axis == how else n for axis, n in enumerate(shape))
        return pl.BlockSpec(
            block, lambda *s: tuple(s[0] if axis == how else 0 for axis in range(len(shape)))
        )

    moved = sum(a.size * a.dtype.itemsize for a, _ in ins)
    moved += sum(functools.reduce(lambda x, y: x * y, s, 1) * jnp.dtype(t).itemsize for (s, t), _ in outs)
    return pl.pallas_call(
        kernel,
        grid_spec=pltpu.PrefetchScalarGridSpec(
            num_scalar_prefetch=len(prefetch),
            grid=(steps,),
            in_specs=[spec(a.shape, how) for a, how in ins],
            out_specs=[spec(s, how) for (s, _), how in outs],
            scratch_shapes=scratch,
        ),
        out_shape=[jax.ShapeDtypeStruct(s, t) for (s, t), _ in outs],
        compiler_params=pltpu.CompilerParams(vmem_limit_bytes=VMEM_BYTES),
        cost_estimate=pl.CostEstimate(flops=flops, bytes_accessed=int(moved), transcendentals=0),
    )(*prefetch, *[a for a, _ in ins])


def widen(src_ref, dst):
    devices, cols = src_ref.shape[0], src_ref.shape[-1]
    per = dst.shape[0] // devices
    for d in range(devices):
        dst[d * per : (d + 1) * per, :] = src_ref[d].astype(F32).reshape(per, cols)


def narrow(src, dst_ref):
    devices = dst_ref.shape[0]
    per = src.shape[0] // devices
    for d in range(devices):
        dst_ref[d] = src[d * per : (d + 1) * per, :].astype(BF16).reshape(dst_ref.shape[1:])


def get_channel(src, ch, sub, subs, dims):
    row_devs, col_devs, rows, cpd, cols = dims
    halves = []
    for s in range(col_devs):
        parts = []
        for r in range(row_devs):
            base = ((r * col_devs + s) * subs + sub) * rows * cpd
            parts.append(src[pl.ds(base + ch, rows, stride=cpd), :])
        halves.append(jnp.concatenate(parts, 0))
    return jnp.concatenate(halves, 1).astype(BF16)


def put_channel(dst, value, ch, sub, subs, dims):
    row_devs, col_devs, rows, cpd, cols = dims
    for s in range(col_devs):
        for r in range(row_devs):
            base = ((r * col_devs + s) * subs + sub) * rows * cpd
            dst[pl.ds(base + ch, rows, stride=cpd), :] = value[
                r * rows : (r + 1) * rows, s * cols : (s + 1) * cols
            ]


def product_kernel(dims, outgoing, edges_ref, out_ref, edges, result):
    widen(edges_ref, edges)
    for ch in range(dims[3]):
        left = get_channel(edges, ch, 0, 2, dims)
        right = get_channel(edges, ch, 1, 2, dims)
        value = dot(left, right, 1, 1) if outgoing else dot(left, right, 0, 0)
        put_channel(result, value, ch, 0, 1, dims)
    narrow(result, out_ref)


def product_grad_kernel(dims, outgoing, edges_ref, grad_ref, out_ref, edges, grad, result):
    widen(edges_ref, edges)
    widen(grad_ref, grad)
    for ch in range(dims[3]):
        left = get_channel(edges, ch, 0, 2, dims)
        right = get_channel(edges, ch, 1, 2, dims)
        gp = get_channel(grad, ch, 0, 1, dims)
        if outgoing:
            grad_left = dot(gp, right, 1, 0)
            grad_right = dot(gp, left, 0, 0)
        else:
            grad_left = dot(right, gp, 1, 1)
            grad_right = dot(left, gp, 1, 0)
        put_channel(result, grad_left, ch, 0, 2, dims)
        put_channel(result, grad_right, ch, 1, 2, dims)
    narrow(result, out_ref)


def channel_call(kernel, ins, out_shape, flops):
    cols = out_shape[-1]

    def rows_of(shape):
        return functools.reduce(lambda x, y: x * y, shape[:-1], 1)

    moved = sum(a.size * 2 for a in ins) + 2 * cols * rows_of(out_shape)
    return pl.pallas_call(
        kernel,
        in_specs=[pl.BlockSpec(memory_space=pltpu.VMEM)] * len(ins),
        out_specs=pl.BlockSpec(memory_space=pltpu.VMEM),
        out_shape=jax.ShapeDtypeStruct(out_shape, BF16),
        scratch_shapes=[pltpu.VMEM((rows_of(a.shape), cols), F32) for a in ins]
        + [pltpu.VMEM((rows_of(out_shape), cols), F32)],
        compiler_params=pltpu.CompilerParams(vmem_limit_bytes=VMEM_BYTES),
        cost_estimate=pl.CostEstimate(flops=flops, bytes_accessed=int(moved), transcendentals=0),
    )(*ins)


def exchange(array):
    return lax.all_to_all(array, AXES, split_axis=0, concat_axis=0, tiled=True)


def shards(
    pair_rep, cotangent, residue_mask, chain_ids, proj_weight, out_weight,
    input_gain, input_bias, hidden_gain, hidden_bias, chain_bias,
):
    rows, cols, width = pair_rep.shape
    hidden = out_weight.shape[1]
    row_devs, col_devs = lax.axis_size("row"), lax.axis_size("col")
    devices = row_devs * col_devs
    length = rows * row_devs
    cpd = hidden // devices
    q = max(1, 16 // cpd)
    tiles = rows // q
    lanes = q * cols
    steps = max(1, tiles // 2)
    dims = (row_devs, col_devs, rows, cpd, cols)
    side = rows * cpd

    starts = jnp.stack([lax.axis_index("row") * rows, lax.axis_index("col")]).astype(jnp.int32)
    wt = jnp.swapaxes(proj_weight, 1, 2)
    owt = jnp.swapaxes(out_weight, 1, 2)
    tile = (tiles, width, lanes)
    edge_shape = (devices, 2, side, cols)
    cell_shape = (devices, side, cols)
    vec = lambda n: pltpu.VMEM((n, width, lanes), F32)
    acc = lambda n: pltpu.VMEM((width, n), F32)
    cell_flops = 2 * rows * cols * width * hidden
    tri_flops = 2 * cpd * length**3

    def product(edges, outgoing):
        return channel_call(
            functools.partial(product_kernel, dims, outgoing), [edges], cell_shape, tri_flops
        )

    def product_grad(edges, grad, outgoing):
        return channel_call(
            functools.partial(product_grad_kernel, dims, outgoing), [edges, grad], edge_shape, 2 * tri_flops
        )

    edges0, z0, up, gate0, flags = cell_call(
        functools.partial(edge_first_kernel, cpd, q),
        steps,
        [
            (pair_rep, 0), (cotangent, 0), (residue_mask.reshape(col_devs, cols), None),
            (chain_ids.reshape(col_devs, cols), None), (wt[0], None),
            (input_gain, None), (input_bias, None), (chain_bias, None),
        ],
        [
            ((edge_shape, BF16), 2), ((tile, BF16), 0), ((tile, BF16), 0), ((tile, F32), 0),
            (((tiles, 2, lanes), F32), 0),
        ],
        [vec(3)],
        prefetch=(residue_mask, chain_ids, starts),
        flops=5 * cell_flops,
    )
    edges0 = exchange(edges0)
    prod0 = exchange(product(edges0, True))
    edges1, z1, gate1 = cell_call(
        functools.partial(mix_edge_kernel, cpd, q, 0),
        steps,
        [
            (prod0, 1), (z0, 0), (gate0, 0), (flags, 0), (owt[0], None), (hidden_gain, None),
            (hidden_bias, None), (wt[1], None), (input_gain, None), (input_bias, None), (chain_bias, None),
        ],
        [((edge_shape, BF16), 2), ((tile, F32), 0), ((tile, F32), 0)],
        [vec(5)],
        flops=6 * cell_flops,
    )
    edges1 = exchange(edges1)
    prod1 = exchange(product(edges1, False))
    terms_shape = (hidden + 8, hidden)
    grad1, glog1, terms1 = cell_call(
        functools.partial(mix_back_kernel, cpd, q, 1),
        steps,
        [
            (prod1, 1), (up, 0), (gate1, 0), (flags, 0), (out_weight[1], None), (owt[1], None),
            (hidden_gain, None), (hidden_bias, None),
        ],
        [((cell_shape, BF16), 1), ((tile, BF16), 0), ((terms_shape, F32), None)],
        [vec(2), acc(hidden), acc(cols), acc(cols), acc(cols)],
        flops=3 * cell_flops,
    )
    grads1 = exchange(product_grad(edges1, exchange(grad1), False))
    per_device = -(-(6 * hidden + 5) * 2 // (devices * 16)) * 16
    all_shape = (devices * per_device // 2, hidden)
    up0, grad0, glog0, all1, terms0 = cell_call(
        functools.partial(edge_mix_back_kernel, cpd, q, 1),
        steps,
        [
            (grads1, 2), (z1, 0), (glog1, 0), (up, 0), (flags, 0), (wt[1], None), (proj_weight[1], None),
            (input_gain, None), (input_bias, None), (terms1, None), (prod0, 1), (gate0, 0),
            (out_weight[0], None), (owt[0], None), (hidden_gain, None), (hidden_bias, None),
        ],
        [
            ((tile, F32), 0), ((cell_shape, BF16), 1), ((tile, BF16), 0), ((all_shape, BF16), None),
            ((terms_shape, F32), None),
        ],
        [vec(4), acc(5 * hidden), acc(cols), acc(cols), acc(hidden), acc(cols), acc(cols), acc(cols)],
        flops=17 * cell_flops,
    )
    grads0 = exchange(product_grad(edges0, exchange(grad0), True))
    grad_pair, all0 = cell_call(
        functools.partial(edge_back_kernel, cpd, q, 0),
        steps,
        [
            (grads0, 2), (z0, 0), (glog0, 0), (up0, 0), (flags, 0), (wt[0], None), (proj_weight[0], None),
            (input_gain, None), (input_bias, None), (terms0, None),
        ],
        [((pair_rep.shape, BF16), 0), ((all_shape, BF16), None)],
        [vec(2), acc(5 * hidden), acc(cols), acc(cols)],
        flops=14 * cell_flops,
    )
    mine = exchange(jnp.stack([all0, all1]).reshape(devices, per_device, hidden))
    mine = (jnp.sum(mine.astype(F32), 0) * (1.0 / length)).astype(BF16)
    total = lax.all_gather(mine, AXES, axis=0, tiled=True).reshape(2, -1, hidden).astype(F32)
    proj = total[:, : 5 * hidden].reshape(2, 5, width, hidden).transpose(0, 2, 1, 3)
    vectors = total[:, 6 * hidden : 6 * hidden + 5]
    return (
        grad_pair,
        proj.reshape(2, width, 5 * hidden),
        total[:, 5 * hidden : 6 * hidden],
        vectors[:, 0:2],
        vectors[:, 2:4],
        vectors[:, 4],
    )


def solution(mesh):
    cells = P(("grp", "row"), "col", None)
    return jax.shard_map(
        shards,
        mesh=mesh,
        in_specs=(cells, cells, P("grp"), P("grp")) + (P(),) * 7,
        out_specs=(
            cells, P("grp", None, None), P("grp", None, None), P("grp", None, None),
            P("grp", None, None), P("grp", None),
        ),
        check_vma=False,
    )
```

```python
import functools

import jax
import jax.numpy as jnp
from jax import lax
from jax.experimental import pallas as pl
from jax.experimental.pallas import tpu as pltpu
from jax.sharding import PartitionSpec as P

EPSILON = 1e-05
AXES = ("row", "col")
F32 = jnp.float32
BF16 = jnp.bfloat16
VMEM_BYTES = 50 * 1024 * 1024


def dot(a, b, ca, cb):
    return lax.dot_general(a, b, (((ca,), (cb,)), ((), ())), preferred_element_type=F32)


def sigmoid(x):
    return 0.5 * jnp.tanh(0.5 * x) + 0.5


def columns(vectors, width):
    c = vectors.shape[1]
    square = jnp.broadcast_to(vectors, (c, c)).T
    return jnp.concatenate([square] * (width // c), 1)


def norm(x):
    centred = x - jnp.mean(x, 0, keepdims=True)
    inv = lax.rsqrt(jnp.mean(centred * centred, 0, keepdims=True) + EPSILON)
    return centred * inv, inv


def norm_grad(grad_scaled, normed, inv, gain):
    g = grad_scaled * gain
    first = jnp.mean(g, 0, keepdims=True)
    second = jnp.mean(g * normed, 0, keepdims=True)
    return (g - first - normed * second) * inv


def unpack(block, cpd):
    devices, rows, cols = block.shape
    values = block.astype(F32)
    parts = []
    for a in range(rows // cpd):
        if cpd % 8 == 0:
            parts.append(values[:, a * cpd : (a + 1) * cpd, :].reshape(devices * cpd, cols))
        else:
            parts.append(
                jnp.concatenate([values[d, a * cpd : (a + 1) * cpd, :] for d in range(devices)], 0)
            )
    return jnp.concatenate(parts, 1)


def pack(tile, cpd, cols):
    channels, lanes = tile.shape
    devices = channels // cpd
    parts = [tile[:, a * cols : (a + 1) * cols] for a in range(lanes // cols)]
    if cpd % 8 == 0:
        return jnp.concatenate([p.reshape(devices, cpd, cols) for p in parts], 1).astype(BF16)
    return jnp.stack(
        [
            jnp.concatenate([p[d * cpd : (d + 1) * cpd, :] for p in parts], 0)
            for d in range(devices)
        ]
    ).astype(BF16)


def fold(tile, width):
    return sum(tile[:, a : a + width] for a in range(0, tile.shape[1], width))


def project(cells, wt_ref, gain, bias, first, last):
    normed, _ = norm(cells)
    lowered = (normed * gain + bias).astype(BF16)
    hidden = wt_ref.shape[0] // 5
    projected = dot(wt_ref[first * hidden : last * hidden, :], lowered, 1, 0)
    return [projected[n * hidden : (n + 1) * hidden] for n in range(last - first)]


def emit_edges(edges_ref, here, cells, wt_ref, gain, bias, mask, cpd, cols):
    part = project(cells, wt_ref, gain, bias, 0, 4)
    edges_ref[:, 0, here, :] = pack(part[0] * sigmoid(part[1]) * mask, cpd, cols)
    edges_ref[:, 1, here, :] = pack(part[2] * sigmoid(part[3]) * mask, cpd, cols)


def first_step(fill):
    pl.when(pl.program_id(0) == 0)(fill)


def last_step(fill):
    pl.when(pl.program_id(0) == pl.num_programs(0) - 1)(fill)


def load_columns(vec, *rows):
    @first_step
    def _():
        for n, (ref, layer) in enumerate(rows):
            vec[n] = columns(ref[layer : layer + 1, :], vec.shape[2])


def clear(*accs):
    @first_step
    def _():
        for acc in accs:
            acc[...] = jnp.zeros_like(acc)


def turned(ref, t, q):
    return jnp.concatenate([ref[t * q + a].astype(F32).T for a in range(q)], 1)


def row_flags(row, mask_smem, chain_smem, start_smem, maskc_ref, chainc_ref):
    whole = start_smem[0] + row
    here = pl.ds(start_smem[1], 1)
    mask = (maskc_ref[here, :] * mask_smem[whole]).astype(F32)
    return mask, (chainc_ref[here, :] == chain_smem[whole]).astype(F32)


def edge_first_kernel(
    cpd, q, mask_smem, chain_smem, start_smem, pair_ref, maskc_ref, chainc_ref, wt_ref, gain_ref, bias_ref,
    edges_ref, vec,
):
    rows, cols, _ = pair_ref.shape
    load_columns(vec, (gain_ref, 0), (bias_ref, 0))
    for t in range(rows // q):
        first = pl.program_id(0) * rows + t * q
        mask = jnp.concatenate(
            [
                row_flags(first + a, mask_smem, chain_smem, start_smem, maskc_ref, chainc_ref)[0]
                for a in range(q)
            ],
            1,
        )
        here = slice(t * q * cpd, (t + 1) * q * cpd)
        emit_edges(edges_ref, here, turned(pair_ref, t, q), wt_ref, vec[0], vec[1], mask, cpd, cols)


def keep_factors(fac_ref, gate_ref, t, cells, wt_ref, gain, bias, chain, mask, same):
    hidden = wt_ref.shape[0] // 5
    part = project(cells, wt_ref, gain, bias, 0, 5)
    for n in (0, 2):
        sig = sigmoid(part[n + 1]) * mask
        fac_ref[t, n * hidden : (n + 1) * hidden, :] = sig.astype(BF16)
        fac_ref[t, (n + 1) * hidden : (n + 2) * hidden, :] = (
            part[n] * sig * (1.0 - sig)
        ).astype(BF16)
    gate_ref[t] = sigmoid(part[4] + same * chain)


def first_keep_kernel(
    q, mask_smem, chain_smem, start_smem, pair_ref, cot_ref, maskc_ref, chainc_ref, wt_ref, gain_ref,
    bias_ref, chain_ref, z_ref, up_ref, gate_ref, flags_ref, fac_ref, vec,
):
    load_columns(vec, (gain_ref, 0), (bias_ref, 0), (chain_ref, 0))
    tiles = z_ref.shape[0]
    for t in range(tiles):
        flags = [
            row_flags(
                (pl.program_id(0) * tiles + t) * q + a, mask_smem, chain_smem, start_smem, maskc_ref, chainc_ref
            )
            for a in range(q)
        ]
        mask = jnp.concatenate([f[0] for f in flags], 1)
        same = jnp.concatenate([f[1] for f in flags], 1)
        cells = turned(pair_ref, t, q)
        z_ref[t] = cells.astype(BF16)
        up_ref[t] = turned(cot_ref, t, q).astype(BF16)
        flags_ref[t] = jnp.concatenate([mask, same], 0)
        keep_factors(fac_ref, gate_ref, t, cells, wt_ref, vec[0], vec[1], vec[2], mask, same)


def keep_kernel(layer, z_ref, flags_ref, wt_ref, gain_ref, bias_ref, chain_ref, gate_ref, fac_ref, vec):
    load_columns(vec, (gain_ref, layer), (bias_ref, layer), (chain_ref, layer))
    for t in range(z_ref.shape[0]):
        keep_factors(
            fac_ref, gate_ref, t, z_ref[t], wt_ref, vec[0], vec[1], vec[2],
            flags_ref[t, 0:1, :], flags_ref[t, 1:2, :],
        )


def mix_edge_kernel(
    cpd, q, layer, prod_ref, z_ref, gate_ref, flags_ref, owt_ref, hgain_ref, hbias_ref, wt_ref,
    gain_ref, bias_ref, edges_ref, znext_ref, vec,
):
    tiles, _, lanes = z_ref.shape
    rows = q * cpd
    load_columns(vec, (hgain_ref, layer), (hbias_ref, layer), (gain_ref, layer + 1), (bias_ref, layer + 1))
    for t in range(tiles):
        here = slice(t * rows, (t + 1) * rows)
        hnormed, _ = norm(unpack(prod_ref[:, here, :], cpd))
        hscaled = (hnormed * vec[0] + vec[1]).astype(BF16)
        cells = z_ref[t].astype(F32) + gate_ref[t] * dot(owt_ref[...], hscaled, 1, 0)
        znext_ref[t] = cells
        emit_edges(
            edges_ref, here, cells, wt_ref, vec[2], vec[3], flags_ref[t, 0:1, :], cpd, lanes // q
        )


def mix_grad(upstream, product, gate, ow_ref, hgain):
    hnormed, hinv = norm(product)
    grad_hscaled = dot(ow_ref[...], (upstream * gate).astype(BF16), 1, 0)
    return norm_grad(grad_hscaled, hnormed, hinv, hgain)


def mix_back_kernel(cpd, q, layer, prod_ref, up_ref, gate_ref, ow_ref, hgain_ref, gp_ref, vec):
    tiles, _, lanes = up_ref.shape
    rows = q * cpd
    load_columns(vec, (hgain_ref, layer))
    for t in range(tiles):
        here = slice(t * rows, (t + 1) * rows)
        grad = mix_grad(
            up_ref[t].astype(F32), unpack(prod_ref[:, here, :], cpd), gate_ref[t], ow_ref, vec[0]
        )
        gp_ref[:, here, :] = pack(grad, cpd, lanes // q)


def mix_terms(upstream, product, gate, same, ow_ref, owt_ref, hgain, hbias, acc_ow, acc_hg, acc_hb, acc_ch):
    width = acc_hg.shape[1]
    hnormed, _ = norm(product)
    hscaled = (hnormed * hgain + hbias).astype(BF16)
    mixed = dot(owt_ref[...], hscaled, 1, 0)
    grad_gate = upstream * gate
    grad_logits = grad_gate * mixed * (1.0 - gate)
    grad_mixed = grad_gate.astype(BF16)
    acc_ow[...] += dot(hscaled, grad_mixed, 1, 1)
    grad_hscaled = dot(ow_ref[...], grad_mixed, 1, 0)
    acc_hg[...] += fold(grad_hscaled * hnormed, width)
    acc_hb[...] += fold(grad_hscaled, width)
    acc_ch[...] += fold(grad_logits * same, width)
    return grad_logits


def row_of(acc):
    return jnp.sum(acc.T, 0, keepdims=True)


def mix_terms_kernel(
    cpd, q, layer, prod_ref, up_ref, gate_ref, flags_ref, ow_ref, owt_ref, hgain_ref, hbias_ref,
    glog_ref, terms_ref, vec, acc_ow, acc_hg, acc_hb, acc_ch,
):
    rows = q * cpd
    load_columns(vec, (hgain_ref, layer), (hbias_ref, layer))
    clear(acc_ow, acc_hg, acc_hb, acc_ch)
    for t in range(up_ref.shape[0]):
        grad_logits = mix_terms(
            up_ref[t].astype(F32), unpack(prod_ref[:, t * rows : (t + 1) * rows, :], cpd),
            gate_ref[t], flags_ref[t, 1:2, :], ow_ref, owt_ref, vec[0], vec[1],
            acc_ow, acc_hg, acc_hb, acc_ch,
        )
        glog_ref[t] = grad_logits.astype(BF16)

    @last_step
    def _():
        hidden = acc_ow.shape[0]
        terms_ref[:hidden, :] = acc_ow[...]
        vectors = [row_of(acc_hg[...]), row_of(acc_hb[...]), row_of(acc_ch[...])]
        vectors.append(jnp.zeros((terms_ref.shape[0] - hidden - 3, hidden), F32))
        terms_ref[hidden:, :] = jnp.concatenate(vectors, 0)


def project_grad(grads, fac_ref, t, gproj_ref):
    hidden = fac_ref.shape[1] // 4
    for n in range(4):
        block = slice(n * hidden, (n + 1) * hidden)
        gproj_ref[t, block, :] = (grads[n // 2] * fac_ref[t, block, :].astype(F32)).astype(BF16)


def input_grad(cells, gproj_ref, glog_ref, t, w_ref, gain):
    hidden = gproj_ref.shape[1] // 4
    normed, inv = norm(cells)
    grad_scaled = dot(w_ref[:, : 4 * hidden], gproj_ref[t], 1, 0) + dot(
        w_ref[:, 4 * hidden :], glog_ref[t], 1, 0
    )
    return norm_grad(grad_scaled, normed, inv, gain)


def edge_mix_back_kernel(
    cpd, q, layer, left_ref, right_ref, fac_ref, z_ref, glog_ref, up_ref, w_ref, gain_ref,
    prod_ref, gate_ref, ow_ref, hgain_ref, upnext_ref, gp_ref, gproj_ref, vec,
):
    tiles, _, lanes = z_ref.shape
    rows = q * cpd
    load_columns(vec, (gain_ref, layer), (hgain_ref, layer - 1))
    for t in range(tiles):
        here = slice(t * rows, (t + 1) * rows)
        grads = (unpack(left_ref[:, here, :], cpd), unpack(right_ref[:, here, :], cpd))
        project_grad(grads, fac_ref, t, gproj_ref)
        upstream = up_ref[t].astype(F32) + input_grad(z_ref[t], gproj_ref, glog_ref, t, w_ref, vec[0])
        upnext_ref[t] = upstream
        grad = mix_grad(upstream, unpack(prod_ref[:, here, :], cpd), gate_ref[t], ow_ref, vec[1])
        gp_ref[:, here, :] = pack(grad, cpd, lanes // q)


def edge_terms(cells, gproj_ref, glog_ref, t, gain, bias, acc_w):
    hidden = gproj_ref.shape[1] // 4
    normed, _ = norm(cells)
    lowered = (normed * gain + bias).astype(BF16)
    ones = jnp.ones((16, cells.shape[1]), BF16)
    sides = jnp.concatenate([lowered, normed.astype(BF16), ones], 0)
    acc_w[:, : 4 * hidden] += dot(sides, gproj_ref[t], 1, 1)
    acc_w[:, 4 * hidden :] += dot(sides, glog_ref[t], 1, 1)


def finish_edge(out_ref, acc_w, w_ref):
    width = w_ref.shape[0]
    for n in range(acc_w.shape[1] // width):
        out_ref[n * width : (n + 1) * width, :] = acc_w[:width, n * width : (n + 1) * width].astype(BF16)
    weight = w_ref[...].astype(F32)
    gain = row_of(fold(weight * acc_w[width : 2 * width, :], width))
    bias = row_of(fold(weight * acc_w[2 * width : 2 * width + 1, :], width))
    return [gain, bias]


def finish_rows(out_ref, first, vectors):
    pad = jnp.zeros((out_ref.shape[0] - first - sum(v.shape[0] for v in vectors), out_ref.shape[1]), F32)
    out_ref[first:, :] = jnp.concatenate(vectors + [pad], 0).astype(BF16)


def late_terms_kernel(
    cpd, q, layer, z_ref, gproj_ref, glog_ref, w_ref, gain_ref, bias_ref, terms_ref,
    prod_ref, up_ref, gate_ref, flags_ref, ow_ref, owt_ref, hgain_ref, hbias_ref,
    glognext_ref, all_ref, vec, acc_w, acc_ow, acc_hg, acc_hb, acc_ch,
):
    rows = q * cpd
    load_columns(vec, (gain_ref, layer), (bias_ref, layer), (hgain_ref, layer - 1), (hbias_ref, layer - 1))
    clear(acc_w, acc_ow, acc_hg, acc_hb, acc_ch)
    for t in range(z_ref.shape[0]):
        edge_terms(z_ref[t], gproj_ref, glog_ref, t, vec[0], vec[1], acc_w)
        grad_logits = mix_terms(
            up_ref[t], unpack(prod_ref[:, t * rows : (t + 1) * rows, :], cpd), gate_ref[t],
            flags_ref[t, 1:2, :], ow_ref, owt_ref, vec[2], vec[3], acc_ow, acc_hg, acc_hb, acc_ch,
        )
        glognext_ref[t] = grad_logits.astype(BF16)

    @last_step
    def _():
        hidden = acc_ow.shape[0]
        vectors = finish_edge(all_ref, acc_w, w_ref)
        all_ref[5 * hidden : 6 * hidden, :] = terms_ref[:hidden, :].astype(BF16)
        all_ref[6 * hidden : 7 * hidden, :] = acc_ow[...].astype(BF16)
        vectors += [terms_ref[hidden : hidden + 3, :]]
        vectors += [row_of(acc_hg[...]), row_of(acc_hb[...]), row_of(acc_ch[...])]
        finish_rows(all_ref, 7 * hidden, vectors)


def last_terms_kernel(
    cpd, q, layer, left_ref, right_ref, fac_ref, z_ref, glog_ref, w_ref, gain_ref, bias_ref,
    gproj_ref, all_ref, vec, acc_w,
):
    rows = q * cpd
    load_columns(vec, (gain_ref, layer), (bias_ref, layer))
    clear(acc_w)
    for t in range(z_ref.shape[0]):
        here = slice(t * rows, (t + 1) * rows)
        grads = (unpack(left_ref[:, here, :], cpd), unpack(right_ref[:, here, :], cpd))
        project_grad(grads, fac_ref, t, gproj_ref)
        edge_terms(z_ref[t].astype(F32), gproj_ref, glog_ref, t, vec[0], vec[1], acc_w)

    @last_step
    def _():
        finish_rows(all_ref, acc_w.shape[1], finish_edge(all_ref, acc_w, w_ref))


def pair_grad_kernel(q, layer, gproj_ref, glog_ref, z_ref, up_ref, w_ref, gain_ref, pair_ref, vec):
    tiles, _, lanes = z_ref.shape
    cols = lanes // q
    load_columns(vec, (gain_ref, layer))
    for t in range(tiles):
        upstream = up_ref[t] + input_grad(z_ref[t].astype(F32), gproj_ref, glog_ref, t, w_ref, vec[0])
        for a in range(q):
            pair_ref[t * q + a] = upstream[:, a * cols : (a + 1) * cols].T.astype(BF16)


def spread_kernel(factor, early_ref, late_ref, out_ref):
    early = (jnp.sum(early_ref[...].astype(F32), 0) * factor).astype(BF16)
    late = (jnp.sum(late_ref[...].astype(F32), 0) * factor).astype(BF16)
    out_ref[...] = jnp.broadcast_to(jnp.concatenate([early, late], 0)[None], out_ref.shape)


def unpack_kernel(early_rows, got_ref, proj_ref, ow_ref, inorm_ref, hnorm_ref, chain_ref):
    width = ow_ref.shape[1]
    early = got_ref[:, :early_rows, :].astype(F32).reshape(-1, width)
    late = got_ref[:, early_rows:, :].astype(F32).reshape(-1, width)
    for n in range(5):
        rows, lanes = slice(n * width, (n + 1) * width), slice(n * width, (n + 1) * width)
        proj_ref[0, :, lanes] = late[rows]
        proj_ref[1, :, lanes] = early[rows]
    ow_ref[1] = early[5 * width : 6 * width]
    ow_ref[0] = early[6 * width : 7 * width]
    inorm_ref[0] = late[5 * width : 5 * width + 2]
    vectors = early[7 * width : 7 * width + 8]
    inorm_ref[1] = vectors[0:2]
    hnorm_ref[1] = vectors[2:4]
    hnorm_ref[0] = vectors[5:7]
    chain_ref[...] = jnp.concatenate([vectors[7:8], vectors[4:5]], 0)


def cell_call(kernel, steps, ins, outs, scratch, prefetch=(), flops=0):
    def spec(shape, how):
        if how is None:
            return pl.BlockSpec(shape, lambda *s: (0,) * len(shape))
        axis, first, size = how if isinstance(how, tuple) else (how, 0, shape[how] // steps)
        block = tuple(size if n == axis else length for n, length in enumerate(shape))
        return pl.BlockSpec(
            block, lambda *s: tuple(s[0] + first if n == axis else 0 for n in range(len(shape)))
        )

    moved = sum(a.size * a.dtype.itemsize for a, _ in ins)
    moved += sum(functools.reduce(lambda x, y: x * y, s, 1) * jnp.dtype(t).itemsize for (s, t), _ in outs)
    return pl.pallas_call(
        kernel,
        grid_spec=pltpu.PrefetchScalarGridSpec(
            num_scalar_prefetch=len(prefetch),
            grid=(steps,),
            in_specs=[spec(a.shape, how) for a, how in ins],
            out_specs=[spec(s, how) for (s, _), how in outs],
            scratch_shapes=scratch,
        ),
        out_shape=[jax.ShapeDtypeStruct(s, t) for (s, t), _ in outs],
        compiler_params=pltpu.CompilerParams(vmem_limit_bytes=VMEM_BYTES),
        cost_estimate=pl.CostEstimate(flops=flops, bytes_accessed=int(moved), transcendentals=0),
    )(*prefetch, *[a for a, _ in ins])


def widen(src_ref, dst):
    devices, cols = src_ref.shape[0], src_ref.shape[-1]
    per = dst.shape[0] // devices
    for d in range(devices):
        dst[d * per : (d + 1) * per, :] = src_ref[d].astype(F32).reshape(per, cols)


def narrow(src, dst_ref):
    devices = dst_ref.shape[0]
    per = src.shape[0] // devices
    for d in range(devices):
        dst_ref[d, :per, :] = src[d * per : (d + 1) * per, :].astype(BF16)


def get_channel(src, ch, sub, subs, dims):
    row_devs, col_devs, rows, cpd, cols = dims
    halves = []
    for s in range(col_devs):
        parts = []
        for r in range(row_devs):
            base = ((r * col_devs + s) * subs + sub) * rows * cpd
            parts.append(src[pl.ds(base + ch, rows, stride=cpd), :])
        halves.append(jnp.concatenate(parts, 0))
    return jnp.concatenate(halves, 1).astype(BF16)


def put_channel(dst, value, ch, sub, subs, dims):
    row_devs, col_devs, rows, cpd, cols = dims
    for s in range(col_devs):
        for r in range(row_devs):
            base = ((r * col_devs + s) * subs + sub) * rows * cpd
            dst[pl.ds(base + ch, rows, stride=cpd), :] = value[
                r * rows : (r + 1) * rows, s * cols : (s + 1) * cols
            ]


def product_kernel(dims, outgoing, edges_ref, out_ref, edges, result):
    widen(edges_ref, edges)
    for ch in range(dims[3]):
        left = get_channel(edges, ch, 0, 2, dims)
        right = get_channel(edges, ch, 1, 2, dims)
        value = dot(left, right, 1, 1) if outgoing else dot(left, right, 0, 0)
        put_channel(result, value, ch, 0, 1, dims)
    narrow(result, out_ref)


def assemble_kernel(dims, edges_ref, out_ref, edges):
    widen(edges_ref, edges)
    for ch in range(dims[3]):
        for sub in range(2):
            out_ref[ch, sub] = get_channel(edges, ch, sub, 2, dims)


def product_grad_kernel(dims, outgoing, sides_ref, grad_ref, *rest):
    out_ref, grad, result = rest[-3:]
    widen(grad_ref, grad)
    for ch in range(dims[3]):
        left, right = sides_ref[ch, 0], sides_ref[ch, 1]
        gp = get_channel(grad, ch, 0, 1, dims)
        if outgoing:
            grad_left = dot(gp, right, 1, 0)
            grad_right = dot(gp, left, 0, 0)
        else:
            grad_left = dot(right, gp, 1, 1)
            grad_right = dot(left, gp, 1, 0)
        put_channel(result, grad_left, ch, 0, 2, dims)
        put_channel(result, grad_right, ch, 1, 2, dims)
    narrow(result, out_ref)
    for terms_ref in rest[:-3]:
        out_ref[:, out_ref.shape[1] - terms_ref.shape[1] :, :] = terms_ref[...]


def whole_call(kernel, ins, outs, scratch, flops):
    moved = sum(a.size * a.dtype.itemsize for a in ins)
    moved += sum(functools.reduce(lambda x, y: x * y, s, 1) * jnp.dtype(t).itemsize for s, t in outs)
    specs = [pl.BlockSpec(memory_space=pltpu.VMEM)] * len(outs)
    shapes = [jax.ShapeDtypeStruct(s, t) for s, t in outs]
    return pl.pallas_call(
        kernel,
        in_specs=[pl.BlockSpec(memory_space=pltpu.VMEM)] * len(ins),
        out_specs=specs if len(outs) > 1 else specs[0],
        out_shape=shapes if len(outs) > 1 else shapes[0],
        scratch_shapes=scratch,
        compiler_params=pltpu.CompilerParams(vmem_limit_bytes=VMEM_BYTES),
        cost_estimate=pl.CostEstimate(flops=flops, bytes_accessed=int(moved), transcendentals=0),
    )(*ins)


def exchange(array):
    return lax.all_to_all(array, AXES, split_axis=0, concat_axis=0, tiled=True)


def after(array, *others):
    return lax.optimization_barrier((array, *others))[0]


def shards(
    pair_rep, cotangent, residue_mask, chain_ids, proj_weight, out_weight,
    input_gain, input_bias, hidden_gain, hidden_bias, chain_bias,
):
    rows, cols, width = pair_rep.shape
    hidden = out_weight.shape[1]
    row_devs, col_devs = lax.axis_size("row"), lax.axis_size("col")
    devices = row_devs * col_devs
    length = rows * row_devs
    cpd = hidden // devices
    q = max(1, 16 // cpd)
    tiles = rows // q
    lanes = q * cols
    steps = max(1, tiles // 4)
    dims = (row_devs, col_devs, rows, cpd, cols)
    side = rows * cpd

    starts = jnp.stack([lax.axis_index("row") * rows, lax.axis_index("col")]).astype(jnp.int32)
    wt = [proj_weight[n].T for n in range(2)]
    owt = [out_weight[n].T for n in range(2)]
    weight = [proj_weight[n] for n in range(2)]
    mixer = [out_weight[n] for n in range(2)]
    mask_cols, chain_cols = residue_mask.reshape(col_devs, cols), chain_ids.reshape(col_devs, cols)
    scalars = (residue_mask, chain_ids, starts)
    tile = (tiles, width, lanes)
    fac_tile = (tiles, 4 * hidden, lanes)
    edge_shape = (devices, 2, side, cols)
    cell_shape = (devices, side, cols)
    vec = lambda n: pltpu.VMEM((n, width, lanes), F32)
    acc = lambda n, m=width: pltpu.VMEM((m, n), F32)
    wide = lambda n: pltpu.VMEM((n * devices * side, cols), F32)
    cell_flops = 2 * rows * cols * width * hidden
    tri_flops = 2 * cpd * length**3
    rows_for = lambda n: -(-n // (devices * 16)) * 16
    early_rows, late_rows = rows_for(7 * hidden + 8), rows_for(5 * hidden + 2)
    terms_shape = (hidden + 8, hidden)

    def product(edges, outgoing):
        return whole_call(
            functools.partial(product_kernel, dims, outgoing), [edges], [(cell_shape, BF16)],
            [wide(2), wide(1)], tri_flops,
        )

    def assemble(edges):
        return whole_call(
            functools.partial(assemble_kernel, dims), [edges], [((cpd, 2, length, length), BF16)], [wide(2)], 0
        )

    def product_grad(sides, grad, outgoing, *terms):
        out_rows = 2 * side + sum(t.shape[1] for t in terms)
        return whole_call(
            functools.partial(product_grad_kernel, dims, outgoing), [sides, grad, *terms],
            [((devices, out_rows, cols), BF16)], [wide(1), wide(2)], 2 * tri_flops,
        )

    def halves(grads):
        per = side // steps
        return [(grads, (1, 0, per)), (grads, (1, steps, per))]

    (edges0,) = cell_call(
        functools.partial(edge_first_kernel, cpd, q), steps,
        [
            (pair_rep, 0), (mask_cols, None), (chain_cols, None), (wt[0], None), (input_gain, None),
            (input_bias, None),
        ],
        [((edge_shape, BF16), 2)], [vec(2)], prefetch=scalars, flops=4 * cell_flops,
    )
    got0 = exchange(edges0)
    z0, up, gate0, flags, fac0 = cell_call(
        functools.partial(first_keep_kernel, q), steps,
        [
            (after(pair_rep, edges0), 0), (cotangent, 0), (mask_cols, None), (chain_cols, None), (wt[0], None),
            (input_gain, None), (input_bias, None), (chain_bias, None),
        ],
        [
            ((tile, BF16), 0), ((tile, BF16), 0), ((tile, F32), 0), (((tiles, 2, lanes), F32), 0),
            ((fac_tile, BF16), 0),
        ],
        [vec(3)], prefetch=scalars, flops=5 * cell_flops,
    )
    made0 = product(got0, True)
    prod0 = exchange(made0)
    sides0 = assemble(after(got0, made0))
    edges1, z1 = cell_call(
        functools.partial(mix_edge_kernel, cpd, q, 0), steps,
        [
            (prod0, 1), (z0, 0), (gate0, 0), (flags, 0), (owt[0], None), (hidden_gain, None),
            (hidden_bias, None), (wt[1], None), (input_gain, None), (input_bias, None),
        ],
        [((edge_shape, BF16), 2), ((tile, F32), 0)], [vec(4)], flops=5 * cell_flops,
    )
    got1 = exchange(edges1)
    gate1, fac1 = cell_call(
        functools.partial(keep_kernel, 1), steps,
        [
            (z1, 0), (flags, 0), (wt[1], None), (input_gain, None), (input_bias, None), (chain_bias, None),
        ],
        [((tile, F32), 0), ((fac_tile, BF16), 0)], [vec(3)], flops=5 * cell_flops,
    )
    made1 = product(got1, False)
    prod1 = exchange(made1)
    sides1 = assemble(after(got1, made1))

    (grad1,) = cell_call(
        functools.partial(mix_back_kernel, cpd, q, 1), steps,
        [(prod1, 1), (up, 0), (gate1, 0), (mixer[1], None), (hidden_gain, None)],
        [((cell_shape, BF16), 1)], [vec(1)], flops=cell_flops,
    )
    got_grad1 = exchange(grad1)
    glog1, terms1 = cell_call(
        functools.partial(mix_terms_kernel, cpd, q, 1), steps,
        [
            (after(prod1, grad1), 1), (up, 0), (gate1, 0), (flags, 0), (mixer[1], None), (owt[1], None),
            (hidden_gain, None), (hidden_bias, None),
        ],
        [((tile, BF16), 0), ((terms_shape, F32), None)],
        [vec(2), acc(hidden), acc(cols), acc(cols), acc(cols)], flops=3 * cell_flops,
    )
    grads1 = exchange(product_grad(sides1, got_grad1, False))
    up0, grad0, gproj1 = cell_call(
        functools.partial(edge_mix_back_kernel, cpd, q, 1), steps,
        halves(grads1)
        + [
            (fac1, 0), (z1, 0), (glog1, 0), (up, 0), (weight[1], None), (input_gain, None),
            (prod0, 1), (gate0, 0), (mixer[0], None), (hidden_gain, None),
        ],
        [((tile, F32), 0), ((cell_shape, BF16), 1), ((fac_tile, BF16), 0)],
        [vec(2)], flops=6 * cell_flops,
    )
    got_grad0 = exchange(grad0)
    glog0, early = cell_call(
        functools.partial(late_terms_kernel, cpd, q, 1), steps,
        [
            (z1, 0), (after(gproj1, grad0), 0), (glog1, 0), (weight[1], None), (input_gain, None),
            (input_bias, None), (terms1, None), (prod0, 1), (up0, 0), (gate0, 0), (flags, 0),
            (mixer[0], None), (owt[0], None), (hidden_gain, None), (hidden_bias, None),
        ],
        [((tile, BF16), 0), (((devices * early_rows, hidden), BF16), None)],
        [vec(4), acc(5 * hidden, 2 * width + 16), acc(hidden), acc(cols), acc(cols), acc(cols)],
        flops=13 * cell_flops,
    )

    grads0 = exchange(
        product_grad(sides0, got_grad0, True, early.reshape(devices, early_rows, hidden))
    )
    gproj0, late = cell_call(
        functools.partial(last_terms_kernel, cpd, q, 0), steps,
        halves(grads0)
        + [
            (fac0, 0), (z0, 0), (glog0, 0), (weight[0], None), (input_gain, None), (input_bias, None),
        ],
        [((fac_tile, BF16), 0), (((devices * late_rows, hidden), BF16), None)],
        [vec(2), acc(5 * hidden, 2 * width + 16)], flops=10 * cell_flops,
    )
    late = exchange(late.reshape(devices, late_rows, hidden))
    (grad_pair,) = cell_call(
        functools.partial(pair_grad_kernel, q, 0), steps,
        [(gproj0, 0), (glog0, 0), (z0, 0), (up0, 0), (weight[0], None), (input_gain, None)],
        [((pair_rep.shape, BF16), 0)], [vec(1)], flops=5 * cell_flops,
    )
    (spread,) = cell_call(
        functools.partial(spread_kernel, 1.0 / length), 1,
        [(grads0, (1, 2 * side // early_rows, early_rows)), (late, None)],
        [(((devices, early_rows + late_rows, hidden), BF16), None)], [],
    )
    proj, out, inorm, hnorm, chain = whole_call(
        functools.partial(unpack_kernel, early_rows), [exchange(spread)],
        [
            ((2, width, 5 * hidden), F32), ((2, hidden, hidden), F32), ((2, 2, hidden), F32),
            ((2, 2, hidden), F32), ((2, hidden), F32),
        ],
        [], 0,
    )
    return grad_pair, proj, out, inorm, hnorm, chain


def solution(mesh):
    cells = P(("grp", "row"), "col", None)
    return jax.shard_map(
        shards,
        mesh=mesh,
        in_specs=(cells, cells, P("grp"), P("grp")) + (P(),) * 7,
        out_specs=(
            cells, P("grp", None, None), P("grp", None, None), P("grp", None, None),
            P("grp", None, None), P("grp", None),
        ),
        check_vma=False,
    )
```

```python
import functools

import jax
import jax.numpy as jnp
from jax import lax
from jax.experimental import pallas as pl
from jax.experimental.pallas import tpu as pltpu
from jax.sharding import PartitionSpec as P

EPSILON = 1e-05
AXES = ("row", "col")
F32 = jnp.float32
BF16 = jnp.bfloat16
VMEM_BYTES = 50 * 1024 * 1024
LARGE_VMEM_BYTES = 60 * 1024 * 1024


def dot(a, b, ca, cb):
    return lax.dot_general(a, b, (((ca,), (cb,)), ((), ())), preferred_element_type=F32)


def sigmoid(x):
    return 0.5 * jnp.tanh(0.5 * x) + 0.5


def columns(vectors, width):
    c = vectors.shape[1]
    square = jnp.broadcast_to(vectors, (c, c)).T
    return jnp.concatenate([square] * (width // c), 1)


def norm(x):
    centred = x - jnp.mean(x, 0, keepdims=True)
    inv = lax.rsqrt(jnp.mean(centred * centred, 0, keepdims=True) + EPSILON)
    return centred * inv, inv


def norm_grad(grad_scaled, normed, inv, gain):
    g = grad_scaled * gain
    first = jnp.mean(g, 0, keepdims=True)
    second = jnp.mean(g * normed, 0, keepdims=True)
    return (g - first - normed * second) * inv


def unpack(block, cpd):
    devices, rows, cols = block.shape
    values = block.astype(F32)
    parts = []
    for a in range(rows // cpd):
        if cpd % 8 == 0:
            parts.append(values[:, a * cpd : (a + 1) * cpd, :].reshape(devices * cpd, cols))
        else:
            parts.append(
                jnp.concatenate([values[d, a * cpd : (a + 1) * cpd, :] for d in range(devices)], 0)
            )
    return jnp.concatenate(parts, 1)


def pack(tile, cpd, cols):
    channels, lanes = tile.shape
    devices = channels // cpd
    parts = [tile[:, a * cols : (a + 1) * cols] for a in range(lanes // cols)]
    if cpd % 8 == 0:
        return jnp.concatenate([p.reshape(devices, cpd, cols) for p in parts], 1).astype(BF16)
    return jnp.stack(
        [
            jnp.concatenate([p[d * cpd : (d + 1) * cpd, :] for p in parts], 0)
            for d in range(devices)
        ]
    ).astype(BF16)


def fold(tile, width):
    return sum(tile[:, a : a + width] for a in range(0, tile.shape[1], width))


def project(lowered, wt_ref, first, last):
    hidden = wt_ref.shape[0] // 5
    projected = dot(wt_ref[first * hidden : last * hidden, :], lowered, 1, 0)
    return [projected[n * hidden : (n + 1) * hidden] for n in range(last - first)]


def lower(cells, gain, bias):
    normed, inv = norm(cells)
    return normed, inv, (normed * gain + bias).astype(BF16)


def emit_edges(edges_ref, here, cells, wt_ref, gain, bias, mask, cpd, cols):
    part = project(lower(cells, gain, bias)[2], wt_ref, 0, 4)
    edges_ref[:, 0, here, :] = pack(part[0] * sigmoid(part[1]) * mask, cpd, cols)
    edges_ref[:, 1, here, :] = pack(part[2] * sigmoid(part[3]) * mask, cpd, cols)


def first_step(fill):
    pl.when(pl.program_id(0) == 0)(fill)


def last_step(fill):
    pl.when(pl.program_id(0) == pl.num_programs(0) - 1)(fill)


def load_columns(vec, *rows):
    @first_step
    def _():
        for n, (ref, layer) in enumerate(rows):
            vec[n] = columns(ref[layer : layer + 1, :], vec.shape[2])


def clear(*accs):
    @first_step
    def _():
        for acc in accs:
            acc[...] = jnp.zeros_like(acc)


def turned(ref, t, q):
    return jnp.concatenate([ref[t * q + a].astype(F32).T for a in range(q)], 1)


def row_flags(row, mask_smem, chain_smem, start_smem, maskc_ref, chainc_ref):
    whole = start_smem[0] + row
    here = pl.ds(start_smem[1], 1)
    mask = (maskc_ref[here, :] * mask_smem[whole]).astype(F32)
    return mask, (chainc_ref[here, :] == chain_smem[whole]).astype(F32)


def edge_first_kernel(
    cpd, q, mask_smem, chain_smem, start_smem, pair_ref, maskc_ref, chainc_ref, w_ref, gain_ref, bias_ref,
    edges_ref, vec, turned_weight,
):
    rows, cols, width = pair_ref.shape
    load_columns(vec, (gain_ref, 0), (bias_ref, 0))

    @first_step
    def _():
        for n in range(turned_weight.shape[0] // width):
            block = slice(n * width, (n + 1) * width)
            turned_weight[block, :] = w_ref[0, :, block].astype(F32).T.astype(BF16)

    for t in range(rows // q):
        first = pl.program_id(0) * rows + t * q
        mask = jnp.concatenate(
            [
                row_flags(first + a, mask_smem, chain_smem, start_smem, maskc_ref, chainc_ref)[0]
                for a in range(q)
            ],
            1,
        )
        here = slice(t * q * cpd, (t + 1) * q * cpd)
        emit_edges(edges_ref, here, turned(pair_ref, t, q), turned_weight, vec[0], vec[1], mask, cpd, cols)


def first_keep_kernel(
    q, mask_smem, chain_smem, start_smem, pair_ref, cot_ref, maskc_ref, chainc_ref, wt_ref, gain_ref,
    bias_ref, chain_ref, z_ref, up_ref, gate_ref, flags_ref, vec,
):
    load_columns(vec, (gain_ref, 0), (bias_ref, 0), (chain_ref, 0))
    tiles = z_ref.shape[0]
    for t in range(tiles):
        flags = [
            row_flags(
                (pl.program_id(0) * tiles + t) * q + a, mask_smem, chain_smem, start_smem, maskc_ref, chainc_ref
            )
            for a in range(q)
        ]
        mask = jnp.concatenate([f[0] for f in flags], 1)
        same = jnp.concatenate([f[1] for f in flags], 1)
        cells = turned(pair_ref, t, q)
        z_ref[t] = cells.astype(BF16)
        up_ref[t] = turned(cot_ref, t, q).astype(BF16)
        flags_ref[t] = jnp.concatenate([mask, same], 0)
        (logits,) = project(lower(cells, vec[0], vec[1])[2], wt_ref, 4, 5)
        gate_ref[t] = sigmoid(logits + same * vec[2]).astype(BF16)


def keep_kernel(layer, z_ref, flags_ref, wt_ref, gain_ref, bias_ref, chain_ref, fac_ref, low_ref, nrm_ref, inv_ref, *rest):
    vec = rest[-1]
    hidden = wt_ref.shape[0] // 5
    load_columns(vec, (gain_ref, layer), (bias_ref, layer), (chain_ref, layer))
    for t in range(z_ref.shape[0]):
        mask, same = flags_ref[t, 0:1, :], flags_ref[t, 1:2, :]
        normed, inv_ref[t], lowered = lower(z_ref[t].astype(F32), vec[0], vec[1])
        low_ref[t] = lowered
        nrm_ref[t] = normed.astype(BF16)
        part = project(lowered, wt_ref, 0, 3 + len(rest))
        for n in (0, 2):
            sig = sigmoid(part[n + 1]) * mask
            fac_ref[t, n * hidden : (n + 1) * hidden, :] = sig.astype(BF16)
            fac_ref[t, (n + 1) * hidden : (n + 2) * hidden, :] = (
                part[n] * sig * (1.0 - sig)
            ).astype(BF16)
        for gate_ref in rest[:-1]:
            gate_ref[t] = sigmoid(part[4] + same * vec[2]).astype(BF16)


def keep_product_kernel(cpd, q, prod_ref, nrm_ref, inv_ref):
    rows = q * cpd
    for t in range(nrm_ref.shape[0]):
        normed, inv_ref[t] = norm(unpack(prod_ref[:, t * rows : (t + 1) * rows, :], cpd))
        nrm_ref[t] = normed.astype(BF16)


def mix_edge_kernel(
    cpd, q, layer, prod_ref, z_ref, gate_ref, flags_ref, owt_ref, hgain_ref, hbias_ref, wt_ref,
    gain_ref, bias_ref, edges_ref, znext_ref, vec,
):
    tiles, _, lanes = z_ref.shape
    rows = q * cpd
    load_columns(vec, (hgain_ref, layer), (hbias_ref, layer), (gain_ref, layer + 1), (bias_ref, layer + 1))
    for t in range(tiles):
        here = slice(t * rows, (t + 1) * rows)
        hnormed, _ = norm(unpack(prod_ref[:, here, :], cpd))
        hscaled = (hnormed * vec[0] + vec[1]).astype(BF16)
        cells = z_ref[t].astype(F32) + gate_ref[t].astype(F32) * dot(owt_ref[...], hscaled, 1, 0)
        znext_ref[t] = cells
        emit_edges(
            edges_ref, here, cells, wt_ref, vec[2], vec[3], flags_ref[t, 0:1, :], cpd, lanes // q
        )


def mix_grad(upstream, hnormed, hinv, gate_ref, t, ow_ref, hgain):
    grad_mixed = (upstream * gate_ref[t].astype(F32)).astype(BF16)
    return norm_grad(dot(ow_ref[...], grad_mixed, 1, 0), hnormed, hinv, hgain)


def mix_back_kernel(cpd, q, layer, prod_ref, up_ref, gate_ref, ow_ref, hgain_ref, gp_ref, vec):
    tiles, _, lanes = up_ref.shape
    rows = q * cpd
    load_columns(vec, (hgain_ref, layer))
    for t in range(tiles):
        here = slice(t * rows, (t + 1) * rows)
        hnormed, hinv = norm(unpack(prod_ref[:, here, :], cpd))
        grad = mix_grad(up_ref[t].astype(F32), hnormed, hinv, gate_ref, t, ow_ref, vec[0])
        gp_ref[:, here, :] = pack(grad, cpd, lanes // q)


def mix_terms(upstream, product, gate, same, ow_ref, owt_ref, hgain, hbias, acc_ow, acc_hg, acc_hb, acc_ch):
    width = acc_hg.shape[1]
    hnormed, _ = norm(product)
    hscaled = (hnormed * hgain + hbias).astype(BF16)
    mixed = dot(owt_ref[...], hscaled, 1, 0)
    grad_gate = upstream * gate
    grad_logits = grad_gate * mixed * (1.0 - gate)
    grad_mixed = grad_gate.astype(BF16)
    acc_ow[...] += dot(hscaled, grad_mixed, 1, 1)
    grad_hscaled = dot(ow_ref[...], grad_mixed, 1, 0)
    acc_hg[...] += fold(grad_hscaled * hnormed, width)
    acc_hb[...] += fold(grad_hscaled, width)
    acc_ch[...] += fold(grad_logits * same, width)
    return grad_logits


def row_of(acc):
    return jnp.sum(acc.T, 0, keepdims=True)


def mix_terms_kernel(
    cpd, q, layer, prod_ref, up_ref, gate_ref, flags_ref, ow_ref, owt_ref, hgain_ref, hbias_ref,
    glog_ref, terms_ref, vec, acc_ow, acc_hg, acc_hb, acc_ch,
):
    rows = q * cpd
    load_columns(vec, (hgain_ref, layer), (hbias_ref, layer))
    clear(acc_ow, acc_hg, acc_hb, acc_ch)
    for t in range(up_ref.shape[0]):
        grad_logits = mix_terms(
            up_ref[t].astype(F32), unpack(prod_ref[:, t * rows : (t + 1) * rows, :], cpd),
            gate_ref[t].astype(F32), flags_ref[t, 1:2, :], ow_ref, owt_ref, vec[0], vec[1],
            acc_ow, acc_hg, acc_hb, acc_ch,
        )
        glog_ref[t] = grad_logits.astype(BF16)

    @last_step
    def _():
        hidden = acc_ow.shape[0]
        terms_ref[:hidden, :] = acc_ow[...]
        vectors = [row_of(acc_hg[...]), row_of(acc_hb[...]), row_of(acc_ch[...])]
        vectors.append(jnp.zeros((terms_ref.shape[0] - hidden - 3, hidden), F32))
        terms_ref[hidden:, :] = jnp.concatenate(vectors, 0)


def project_grad(left_ref, right_ref, fac_ref, glog_ref, t, cpd, rows):
    hidden = fac_ref.shape[1] // 4
    here = slice(t * rows, (t + 1) * rows)
    grads = (unpack(left_ref[:, here, :], cpd), unpack(right_ref[:, here, :], cpd))
    blocks = [
        (grads[n // 2] * fac_ref[t, n * hidden : (n + 1) * hidden, :].astype(F32)).astype(BF16)
        for n in range(4)
    ]
    return jnp.concatenate(blocks + [glog_ref[t]], 0)


def input_grad(gproj, nrm_ref, inv_ref, t, w_ref, gain):
    return norm_grad(dot(w_ref[...], gproj, 1, 0), nrm_ref[t].astype(F32), inv_ref[t], gain)


def edge_mix_back_kernel(
    cpd, q, layer, left_ref, right_ref, fac_ref, nrm_ref, inv_ref, glog_ref, up_ref, w_ref, gain_ref,
    hnrm_ref, hinv_ref, gate_ref, ow_ref, hgain_ref, upnext_ref, gp_ref, vec,
):
    tiles, _, lanes = up_ref.shape
    rows = q * cpd
    load_columns(vec, (gain_ref, layer), (hgain_ref, layer - 1))
    for t in range(tiles):
        gproj = project_grad(left_ref, right_ref, fac_ref, glog_ref, t, cpd, rows)
        upstream = up_ref[t].astype(F32) + input_grad(gproj, nrm_ref, inv_ref, t, w_ref, vec[0])
        upnext_ref[t] = upstream
        grad = mix_grad(upstream, hnrm_ref[t].astype(F32), hinv_ref[t], gate_ref, t, ow_ref, vec[1])
        gp_ref[:, t * rows : (t + 1) * rows, :] = pack(grad, cpd, lanes // q)


def edge_terms(gproj, low_ref, nrm_ref, t, acc_w):
    ones = jnp.ones((16, gproj.shape[1]), BF16)
    acc_w[...] += dot(jnp.concatenate([low_ref[t], nrm_ref[t], ones], 0), gproj, 1, 1)


def finish_edge(out_ref, acc_w, w_ref):
    width = w_ref.shape[0]
    for n in range(acc_w.shape[1] // width):
        out_ref[n * width : (n + 1) * width, :] = acc_w[:width, n * width : (n + 1) * width].astype(BF16)
    weight = w_ref[...].astype(F32)
    gain = row_of(fold(weight * acc_w[width : 2 * width, :], width))
    bias = row_of(fold(weight * acc_w[2 * width : 2 * width + 1, :], width))
    return [gain, bias]


def finish_rows(out_ref, first, vectors):
    pad = jnp.zeros((out_ref.shape[0] - first - sum(v.shape[0] for v in vectors), out_ref.shape[1]), F32)
    out_ref[first:, :] = jnp.concatenate(vectors + [pad], 0).astype(BF16)


def late_terms_kernel(
    cpd, q, layer, left_ref, right_ref, fac_ref, low_ref, nrm_ref, glog_ref, w_ref, terms_ref,
    prod_ref, up_ref, gate_ref, flags_ref, ow_ref, owt_ref, hgain_ref, hbias_ref,
    glognext_ref, all_ref, vec, acc_w, acc_ow, acc_hg, acc_hb, acc_ch,
):
    rows = q * cpd
    load_columns(vec, (hgain_ref, layer - 1), (hbias_ref, layer - 1))
    clear(acc_w, acc_ow, acc_hg, acc_hb, acc_ch)
    for t in range(up_ref.shape[0]):
        gproj = project_grad(left_ref, right_ref, fac_ref, glog_ref, t, cpd, rows)
        edge_terms(gproj, low_ref, nrm_ref, t, acc_w)
        grad_logits = mix_terms(
            up_ref[t], unpack(prod_ref[:, t * rows : (t + 1) * rows, :], cpd), gate_ref[t].astype(F32),
            flags_ref[t, 1:2, :], ow_ref, owt_ref, vec[0], vec[1], acc_ow, acc_hg, acc_hb, acc_ch,
        )
        glognext_ref[t] = grad_logits.astype(BF16)

    @last_step
    def _():
        hidden = acc_ow.shape[0]
        vectors = finish_edge(all_ref, acc_w, w_ref)
        all_ref[5 * hidden : 6 * hidden, :] = terms_ref[:hidden, :].astype(BF16)
        all_ref[6 * hidden : 7 * hidden, :] = acc_ow[...].astype(BF16)
        vectors += [terms_ref[hidden : hidden + 3, :]]
        vectors += [row_of(acc_hg[...]), row_of(acc_hb[...]), row_of(acc_ch[...])]
        finish_rows(all_ref, 7 * hidden, vectors)


def last_terms_kernel(
    cpd, q, left_ref, right_ref, fac_ref, low_ref, nrm_ref, glog_ref, w_ref, all_ref, acc_w,
):
    clear(acc_w)
    for t in range(low_ref.shape[0]):
        gproj = project_grad(left_ref, right_ref, fac_ref, glog_ref, t, cpd, q * cpd)
        edge_terms(gproj, low_ref, nrm_ref, t, acc_w)

    @last_step
    def _():
        finish_rows(all_ref, acc_w.shape[1], finish_edge(all_ref, acc_w, w_ref))


def pair_grad_kernel(
    cpd, q, layer, left_ref, right_ref, fac_ref, nrm_ref, inv_ref, glog_ref, up_ref, w_ref, gain_ref, pair_ref, vec,
):
    tiles, _, lanes = up_ref.shape
    cols = lanes // q
    load_columns(vec, (gain_ref, layer))
    for t in range(tiles):
        gproj = project_grad(left_ref, right_ref, fac_ref, glog_ref, t, cpd, q * cpd)
        upstream = up_ref[t] + input_grad(gproj, nrm_ref, inv_ref, t, w_ref, vec[0])
        for a in range(q):
            pair_ref[t * q + a] = upstream[:, a * cols : (a + 1) * cols].T.astype(BF16)


def spread_kernel(factor, early_ref, late_ref, out_ref):
    early = (jnp.sum(early_ref[...].astype(F32), 0) * factor).astype(BF16)
    late = (jnp.sum(late_ref[...].astype(F32), 0) * factor).astype(BF16)
    out_ref[...] = jnp.broadcast_to(jnp.concatenate([early, late], 0)[None], out_ref.shape)


def unpack_kernel(early_rows, got_ref, proj_ref, ow_ref, inorm_ref, hnorm_ref, chain_ref):
    width = ow_ref.shape[1]
    early = got_ref[:, :early_rows, :].astype(F32).reshape(-1, width)
    late = got_ref[:, early_rows:, :].astype(F32).reshape(-1, width)
    for n in range(5):
        rows, lanes = slice(n * width, (n + 1) * width), slice(n * width, (n + 1) * width)
        proj_ref[0, :, lanes] = late[rows]
        proj_ref[1, :, lanes] = early[rows]
    ow_ref[1] = early[5 * width : 6 * width]
    ow_ref[0] = early[6 * width : 7 * width]
    inorm_ref[0] = late[5 * width : 5 * width + 2]
    vectors = early[7 * width : 7 * width + 8]
    inorm_ref[1] = vectors[0:2]
    hnorm_ref[1] = vectors[2:4]
    hnorm_ref[0] = vectors[5:7]
    chain_ref[...] = jnp.concatenate([vectors[7:8], vectors[4:5]], 0)


def cell_call(kernel, steps, ins, outs, scratch, prefetch=(), flops=0, vmem=VMEM_BYTES):
    def spec(shape, how):
        if how is None:
            return pl.BlockSpec(shape, lambda *s: (0,) * len(shape))
        axis, first, size = how if isinstance(how, tuple) else (how, 0, shape[how] // steps)
        block = tuple(size if n == axis else length for n, length in enumerate(shape))
        moves = shape[axis] >= size * steps
        return pl.BlockSpec(
            block,
            lambda *s: tuple((s[0] if moves else 0) + first if n == axis else 0 for n in range(len(shape))),
        )

    moved = sum(a.size * a.dtype.itemsize for a, _ in ins)
    moved += sum(functools.reduce(lambda x, y: x * y, s, 1) * jnp.dtype(t).itemsize for (s, t), _ in outs)
    return pl.pallas_call(
        kernel,
        grid_spec=pltpu.PrefetchScalarGridSpec(
            num_scalar_prefetch=len(prefetch),
            grid=(steps,),
            in_specs=[spec(a.shape, how) for a, how in ins],
            out_specs=[spec(s, how) for (s, _), how in outs],
            scratch_shapes=scratch,
        ),
        out_shape=[jax.ShapeDtypeStruct(s, t) for (s, t), _ in outs],
        compiler_params=pltpu.CompilerParams(vmem_limit_bytes=vmem),
        cost_estimate=pl.CostEstimate(flops=flops, bytes_accessed=int(moved), transcendentals=0),
    )(*prefetch, *[a for a, _ in ins])


def widen(src_ref, dst):
    devices, cols = src_ref.shape[0], src_ref.shape[-1]
    per = dst.shape[0] // devices
    for d in range(devices):
        dst[d * per : (d + 1) * per, :] = src_ref[d].astype(F32).reshape(per, cols)


def narrow(src, dst_ref):
    devices = dst_ref.shape[0]
    per = src.shape[0] // devices
    for d in range(devices):
        dst_ref[d, :per, :] = src[d * per : (d + 1) * per, :].astype(BF16)


def get_channel(src, ch, sub, subs, dims):
    row_devs, col_devs, rows, cpd, cols = dims
    halves = []
    for s in range(col_devs):
        parts = []
        for r in range(row_devs):
            base = ((r * col_devs + s) * subs + sub) * rows * cpd
            parts.append(src[pl.ds(base + ch, rows, stride=cpd), :])
        halves.append(jnp.concatenate(parts, 0))
    return jnp.concatenate(halves, 1).astype(BF16)


def put_channel(dst, value, ch, sub, subs, dims):
    row_devs, col_devs, rows, cpd, cols = dims
    for s in range(col_devs):
        for r in range(row_devs):
            base = ((r * col_devs + s) * subs + sub) * rows * cpd
            dst[pl.ds(base + ch, rows, stride=cpd), :] = value[
                r * rows : (r + 1) * rows, s * cols : (s + 1) * cols
            ]


def product_kernel(dims, outgoing, edges_ref, out_ref, edges, result):
    widen(edges_ref, edges)
    for ch in range(dims[3]):
        left = get_channel(edges, ch, 0, 2, dims)
        right = get_channel(edges, ch, 1, 2, dims)
        value = dot(left, right, 1, 1) if outgoing else dot(left, right, 0, 0)
        put_channel(result, value, ch, 0, 1, dims)
    narrow(result, out_ref)


def assemble_kernel(dims, edges_ref, out_ref, edges):
    widen(edges_ref, edges)
    for ch in range(dims[3]):
        for sub in range(2):
            out_ref[ch, sub] = get_channel(edges, ch, sub, 2, dims)


def product_grad_kernel(dims, outgoing, sides_ref, grad_ref, *rest):
    out_ref, grad, result = rest[-3:]
    widen(grad_ref, grad)
    for ch in range(dims[3]):
        left, right = sides_ref[ch, 0], sides_ref[ch, 1]
        gp = get_channel(grad, ch, 0, 1, dims)
        if outgoing:
            grad_left = dot(gp, right, 1, 0)
            grad_right = dot(gp, left, 0, 0)
        else:
            grad_left = dot(right, gp, 1, 1)
            grad_right = dot(left, gp, 1, 0)
        put_channel(result, grad_left, ch, 0, 2, dims)
        put_channel(result, grad_right, ch, 1, 2, dims)
    narrow(result, out_ref)
    for terms_ref in rest[:-3]:
        out_ref[:, out_ref.shape[1] - terms_ref.shape[1] :, :] = terms_ref[...]


def whole_call(kernel, ins, outs, scratch, flops):
    moved = sum(a.size * a.dtype.itemsize for a in ins)
    moved += sum(functools.reduce(lambda x, y: x * y, s, 1) * jnp.dtype(t).itemsize for s, t in outs)
    specs = [pl.BlockSpec(memory_space=pltpu.VMEM)] * len(outs)
    shapes = [jax.ShapeDtypeStruct(s, t) for s, t in outs]
    return pl.pallas_call(
        kernel,
        in_specs=[pl.BlockSpec(memory_space=pltpu.VMEM)] * len(ins),
        out_specs=specs if len(outs) > 1 else specs[0],
        out_shape=shapes if len(outs) > 1 else shapes[0],
        scratch_shapes=scratch,
        compiler_params=pltpu.CompilerParams(vmem_limit_bytes=VMEM_BYTES),
        cost_estimate=pl.CostEstimate(flops=flops, bytes_accessed=int(moved), transcendentals=0),
    )(*ins)


def exchange(array):
    return lax.all_to_all(array, AXES, split_axis=0, concat_axis=0, tiled=True)


def after(array, *others):
    return lax.optimization_barrier((array, *others))[0]


def shards(
    pair_rep, cotangent, residue_mask, chain_ids, proj_weight, out_weight,
    input_gain, input_bias, hidden_gain, hidden_bias, chain_bias,
):
    rows, cols, width = pair_rep.shape
    hidden = out_weight.shape[1]
    row_devs, col_devs = lax.axis_size("row"), lax.axis_size("col")
    devices = row_devs * col_devs
    length = rows * row_devs
    cpd = hidden // devices
    q = max(1, 16 // cpd)
    tiles = rows // q
    lanes = q * cols
    steps = max(1, tiles // 4)
    dims = (row_devs, col_devs, rows, cpd, cols)
    side = rows * cpd

    starts = jnp.stack([lax.axis_index("row") * rows, lax.axis_index("col")]).astype(jnp.int32)
    wt = [proj_weight[n].T for n in range(2)]
    owt = [out_weight[n].T for n in range(2)]
    weight = [proj_weight[n] for n in range(2)]
    mixer = [out_weight[n] for n in range(2)]
    mask_cols, chain_cols = residue_mask.reshape(col_devs, cols), chain_ids.reshape(col_devs, cols)
    scalars = (residue_mask, chain_ids, starts)
    tile = (tiles, width, lanes)
    fac_tile = (tiles, 4 * hidden, lanes)
    edge_shape = (devices, 2, side, cols)
    cell_shape = (devices, side, cols)
    vec = lambda n: pltpu.VMEM((n, width, lanes), F32)
    acc = lambda n, m=width: pltpu.VMEM((m, n), F32)
    wide = lambda n: pltpu.VMEM((n * devices * side, cols), F32)
    cell_flops = 2 * rows * cols * width * hidden
    tri_flops = 2 * cpd * length**3
    rows_for = lambda n: -(-n // (devices * 16)) * 16
    early_rows, late_rows = rows_for(7 * hidden + 8), rows_for(5 * hidden + 2)
    terms_shape = (hidden + 8, hidden)

    def product(edges, outgoing):
        return whole_call(
            functools.partial(product_kernel, dims, outgoing), [edges], [(cell_shape, BF16)],
            [wide(2), wide(1)], tri_flops,
        )

    def assemble(edges):
        return whole_call(
            functools.partial(assemble_kernel, dims), [edges], [((cpd, 2, length, length), BF16)], [wide(2)], 0
        )

    def product_grad(sides, grad, outgoing, *terms):
        out_rows = 2 * side + sum(t.shape[1] for t in terms)
        return whole_call(
            functools.partial(product_grad_kernel, dims, outgoing), [sides, grad, *terms],
            [((devices, out_rows, cols), BF16)], [wide(1), wide(2)], 2 * tri_flops,
        )

    def halves(grads):
        per = side // steps
        return [(grads, (1, 0, per)), (grads, (1, steps, per))]

    def keep(layer, z, with_gate):
        norm_outs = [((tile, BF16), 0), ((tile, BF16), 0), (((tiles, 1, lanes), F32), 0)]
        return cell_call(
            functools.partial(keep_kernel, layer), steps,
            [
                (z, 0), (flags, 0), (wt[layer], None), (input_gain, None), (input_bias, None), (chain_bias, None),
            ],
            [((fac_tile, BF16), 0)] + norm_outs + [((tile, BF16), 0)] * with_gate,
            [vec(3)], flops=5 * cell_flops,
        )

    (edges0,) = cell_call(
        functools.partial(edge_first_kernel, cpd, q), steps,
        [
            (pair_rep, 0), (mask_cols, None), (chain_cols, None), (proj_weight, (0, 0, 1)),
            (input_gain, None), (input_bias, None),
        ],
        [((edge_shape, BF16), 2)], [vec(2), pltpu.VMEM((5 * hidden, width), BF16)],
        prefetch=scalars, flops=4 * cell_flops, vmem=LARGE_VMEM_BYTES,
    )
    got0 = exchange(edges0)
    z0, up, gate0, flags = cell_call(
        functools.partial(first_keep_kernel, q), steps,
        [
            (after(pair_rep, edges0), 0), (cotangent, 0), (mask_cols, None), (chain_cols, None), (wt[0], None),
            (input_gain, None), (input_bias, None), (chain_bias, None),
        ],
        [((tile, BF16), 0), ((tile, BF16), 0), ((tile, BF16), 0), (((tiles, 2, lanes), F32), 0)],
        [vec(3)], prefetch=scalars, flops=2 * cell_flops,
    )
    made0 = product(after(got0, z0), True)
    prod0 = exchange(made0)
    sides0 = assemble(after(got0, made0))
    edges1, z1 = cell_call(
        functools.partial(mix_edge_kernel, cpd, q, 0), steps,
        [
            (after(prod0, sides0), 1), (z0, 0), (gate0, 0), (flags, 0), (owt[0], None), (hidden_gain, None),
            (hidden_bias, None), (wt[1], None), (input_gain, None), (input_bias, None),
        ],
        [((edge_shape, BF16), 2), ((tile, F32), 0)], [vec(4)], flops=5 * cell_flops,
    )
    got1 = exchange(edges1)
    fac1, low1, nrm1, inv1, gate1 = keep(1, after(z1, edges1), True)
    made1 = product(after(got1, gate1), False)
    prod1 = exchange(made1)
    sides1 = assemble(after(got1, made1))

    (grad1,) = cell_call(
        functools.partial(mix_back_kernel, cpd, q, 1), steps,
        [(after(prod1, sides1), 1), (up, 0), (gate1, 0), (mixer[1], None), (hidden_gain, None)],
        [((cell_shape, BF16), 1)], [vec(1)], flops=cell_flops,
    )
    got_grad1 = exchange(grad1)
    hnrm0, hinv0 = cell_call(
        functools.partial(keep_product_kernel, cpd, q), steps, [(after(prod0, grad1), 1)],
        [((tile, BF16), 0), (((tiles, 1, lanes), F32), 0)], [],
    )
    made_grads1 = product_grad(sides1, after(got_grad1, hnrm0), False)
    grads1 = exchange(made_grads1)
    glog1, terms1 = cell_call(
        functools.partial(mix_terms_kernel, cpd, q, 1), steps,
        [
            (after(prod1, made_grads1), 1), (up, 0), (gate1, 0), (flags, 0), (mixer[1], None), (owt[1], None),
            (hidden_gain, None), (hidden_bias, None),
        ],
        [((tile, BF16), 0), ((terms_shape, F32), None)],
        [vec(2), acc(hidden), acc(cols), acc(cols), acc(cols)], flops=3 * cell_flops,
    )
    up0, grad0 = cell_call(
        functools.partial(edge_mix_back_kernel, cpd, q, 1), steps,
        halves(after(grads1, glog1))
        + [
            (fac1, 0), (nrm1, 0), (inv1, 0), (glog1, 0), (up, 0), (weight[1], None), (input_gain, None),
            (hnrm0, 0), (hinv0, 0), (gate0, 0), (mixer[0], None), (hidden_gain, None),
        ],
        [((tile, F32), 0), ((cell_shape, BF16), 1)],
        [vec(2)], flops=6 * cell_flops,
    )
    got_grad0 = exchange(grad0)
    glog0, early = cell_call(
        functools.partial(late_terms_kernel, cpd, q, 1), steps,
        halves(after(grads1, grad0))
        + [
            (fac1, 0), (low1, 0), (nrm1, 0), (glog1, 0), (weight[1], None), (terms1, None), (prod0, 1),
            (up0, 0), (gate0, 0), (flags, 0), (mixer[0], None), (owt[0], None), (hidden_gain, None),
            (hidden_bias, None),
        ],
        [((tile, BF16), 0), (((devices * early_rows, hidden), BF16), None)],
        [vec(2), acc(5 * hidden, 2 * width + 16), acc(hidden), acc(cols), acc(cols), acc(cols)],
        flops=13 * cell_flops,
    )

    made_grads0 = product_grad(sides0, got_grad0, True, early.reshape(devices, early_rows, hidden))
    grads0 = exchange(made_grads0)
    fac0, low0, nrm0, inv0 = keep(0, after(z0, made_grads0), False)
    grads0 = after(grads0, nrm0)
    (late,) = cell_call(
        functools.partial(last_terms_kernel, cpd, q), steps,
        halves(grads0) + [(fac0, 0), (low0, 0), (nrm0, 0), (glog0, 0), (weight[0], None)],
        [(((devices * late_rows, hidden), BF16), None)],
        [acc(5 * hidden, 2 * width + 16)], flops=10 * cell_flops,
    )
    got_late = exchange(late.reshape(devices, late_rows, hidden))
    (grad_pair,) = cell_call(
        functools.partial(pair_grad_kernel, cpd, q, 0), steps,
        halves(after(grads0, late))
        + [(fac0, 0), (nrm0, 0), (inv0, 0), (glog0, 0), (up0, 0), (weight[0], None), (input_gain, None)],
        [((pair_rep.shape, BF16), 0)], [vec(1)], flops=5 * cell_flops,
    )
    (spread,) = cell_call(
        functools.partial(spread_kernel, 1.0 / length), 1,
        [(grads0, (1, 2 * side // early_rows, early_rows)), (got_late, None)],
        [(((devices, early_rows + late_rows, hidden), BF16), None)], [],
    )
    proj, out, inorm, hnorm, chain = whole_call(
        functools.partial(unpack_kernel, early_rows), [exchange(spread)],
        [
            ((2, width, 5 * hidden), F32), ((2, hidden, hidden), F32), ((2, 2, hidden), F32),
            ((2, 2, hidden), F32), ((2, hidden), F32),
        ],
        [], 0,
    )
    return grad_pair, proj, out, inorm, hnorm, chain


def solution(mesh):
    cells = P(("grp", "row"), "col", None)
    return jax.shard_map(
        shards,
        mesh=mesh,
        in_specs=(cells, cells, P("grp"), P("grp")) + (P(),) * 7,
        out_specs=(
            cells, P("grp", None, None), P("grp", None, None), P("grp", None, None),
            P("grp", None, None), P("grp", None),
        ),
        check_vma=False,
    )
```

```python
import functools

import jax
import jax.numpy as jnp
from jax import lax
from jax.experimental import pallas as pl
from jax.experimental.pallas import tpu as pltpu
from jax.sharding import PartitionSpec as P

EPSILON = 1e-05
AXES = ("row", "col")
F32 = jnp.float32
BF16 = jnp.bfloat16
VMEM_BYTES = 24 * 1024 * 1024
LARGE_VMEM_BYTES = 60 * 1024 * 1024


def dot(a, b, ca, cb):
    return lax.dot_general(a, b, (((ca,), (cb,)), ((), ())), preferred_element_type=F32)


def sigmoid(x):
    return 0.5 * jnp.tanh(0.5 * x) + 0.5


def columns(vectors, width):
    c = vectors.shape[1]
    square = jnp.broadcast_to(vectors, (c, c)).T
    return jnp.concatenate([square] * (width // c), 1)


def norm(x):
    centred = x - jnp.mean(x, 0, keepdims=True)
    inv = lax.rsqrt(jnp.mean(centred * centred, 0, keepdims=True) + EPSILON)
    return centred * inv, inv


def norm_grad(grad_scaled, normed, inv, gain):
    g = grad_scaled * gain
    first = jnp.mean(g, 0, keepdims=True)
    second = jnp.mean(g * normed, 0, keepdims=True)
    return (g - first - normed * second) * inv


def unpack(block, cpd):
    devices, rows, cols = block.shape
    values = block.astype(F32)
    parts = []
    for a in range(rows // cpd):
        if cpd % 8 == 0:
            parts.append(values[:, a * cpd : (a + 1) * cpd, :].reshape(devices * cpd, cols))
        else:
            parts.append(
                jnp.concatenate([values[d, a * cpd : (a + 1) * cpd, :] for d in range(devices)], 0)
            )
    return jnp.concatenate(parts, 1)


def pack(tile, cpd, cols):
    channels, lanes = tile.shape
    devices = channels // cpd
    parts = [tile[:, a * cols : (a + 1) * cols] for a in range(lanes // cols)]
    if cpd % 8 == 0:
        return jnp.concatenate([p.reshape(devices, cpd, cols) for p in parts], 1).astype(BF16)
    return jnp.stack(
        [
            jnp.concatenate([p[d * cpd : (d + 1) * cpd, :] for p in parts], 0)
            for d in range(devices)
        ]
    ).astype(BF16)


def fold(tile, width):
    return sum(tile[:, a : a + width] for a in range(0, tile.shape[1], width))


def project(lowered, wt_ref, first, last):
    hidden = wt_ref.shape[0] // 5
    projected = dot(wt_ref[first * hidden : last * hidden, :], lowered, 1, 0)
    return [projected[n * hidden : (n + 1) * hidden] for n in range(last - first)]


def lower(cells, gain, bias):
    normed, inv = norm(cells)
    return normed, inv, (normed * gain + bias).astype(BF16)


def emit_edges(edges_ref, here, cells, wt_ref, gain, bias, mask, cpd, cols):
    part = project(lower(cells, gain, bias)[2], wt_ref, 0, 4)
    edges_ref[:, 0, here, :] = pack(part[0] * sigmoid(part[1]) * mask, cpd, cols)
    edges_ref[:, 1, here, :] = pack(part[2] * sigmoid(part[3]) * mask, cpd, cols)


def first_step(fill):
    pl.when(pl.program_id(0) == 0)(fill)


def last_step(fill):
    pl.when(pl.program_id(0) == pl.num_programs(0) - 1)(fill)


def load_columns(vec, *rows):
    @first_step
    def _():
        for n, (ref, layer) in enumerate(rows):
            vec[n] = columns(ref[layer : layer + 1, :], vec.shape[2])


def clear(*accs):
    @first_step
    def _():
        for acc in accs:
            acc[...] = jnp.zeros_like(acc)


def turned(ref, t, q):
    return jnp.concatenate([ref[t * q + a].astype(F32).T for a in range(q)], 1)


def row_flags(row, mask_smem, chain_smem, start_smem, maskc_ref, chainc_ref):
    whole = start_smem[0] + row
    here = pl.ds(start_smem[1], 1)
    mask = (maskc_ref[here, :] * mask_smem[whole]).astype(F32)
    return mask, (chainc_ref[here, :] == chain_smem[whole]).astype(F32)


def edge_first_kernel(
    cpd, q, mask_smem, chain_smem, start_smem, pair_ref, maskc_ref, chainc_ref, w_ref, gain_ref, bias_ref,
    edges_ref, vec, turned_weight,
):
    rows, cols, width = pair_ref.shape
    load_columns(vec, (gain_ref, 0), (bias_ref, 0))

    @first_step
    def _():
        for n in range(turned_weight.shape[0] // width):
            block = slice(n * width, (n + 1) * width)
            turned_weight[block, :] = w_ref[0, :, block].astype(F32).T.astype(BF16)

    for t in range(rows // q):
        first = pl.program_id(0) * rows + t * q
        mask = jnp.concatenate(
            [
                row_flags(first + a, mask_smem, chain_smem, start_smem, maskc_ref, chainc_ref)[0]
                for a in range(q)
            ],
            1,
        )
        here = slice(t * q * cpd, (t + 1) * q * cpd)
        emit_edges(edges_ref, here, turned(pair_ref, t, q), turned_weight, vec[0], vec[1], mask, cpd, cols)


def first_keep_kernel(
    q, mask_smem, chain_smem, start_smem, pair_ref, cot_ref, maskc_ref, chainc_ref, wt_ref, gain_ref,
    bias_ref, chain_ref, z_ref, up_ref, gate_ref, flags_ref, vec,
):
    load_columns(vec, (gain_ref, 0), (bias_ref, 0), (chain_ref, 0))
    tiles = z_ref.shape[0]
    for t in range(tiles):
        flags = [
            row_flags(
                (pl.program_id(0) * tiles + t) * q + a, mask_smem, chain_smem, start_smem, maskc_ref, chainc_ref
            )
            for a in range(q)
        ]
        mask = jnp.concatenate([f[0] for f in flags], 1)
        same = jnp.concatenate([f[1] for f in flags], 1)
        cells = turned(pair_ref, t, q)
        z_ref[t] = cells.astype(BF16)
        up_ref[t] = turned(cot_ref, t, q).astype(BF16)
        flags_ref[t] = jnp.concatenate([mask, same], 0)
        (logits,) = project(lower(cells, vec[0], vec[1])[2], wt_ref, 4, 5)
        gate_ref[t] = sigmoid(logits + same * vec[2]).astype(BF16)


def keep_kernel(layer, z_ref, flags_ref, wt_ref, gain_ref, bias_ref, chain_ref, fac_ref, low_ref, nrm_ref, inv_ref, *rest):
    vec = rest[-1]
    hidden = wt_ref.shape[0] // 5
    load_columns(vec, (gain_ref, layer), (bias_ref, layer), (chain_ref, layer))
    for t in range(z_ref.shape[0]):
        mask, same = flags_ref[t, 0:1, :], flags_ref[t, 1:2, :]
        normed, inv_ref[t], lowered = lower(z_ref[t].astype(F32), vec[0], vec[1])
        low_ref[t] = lowered
        nrm_ref[t] = normed.astype(BF16)
        part = project(lowered, wt_ref, 0, 3 + len(rest))
        for n in (0, 2):
            sig = sigmoid(part[n + 1]) * mask
            fac_ref[t, n * hidden : (n + 1) * hidden, :] = sig.astype(BF16)
            fac_ref[t, (n + 1) * hidden : (n + 2) * hidden, :] = (
                part[n] * sig * (1.0 - sig)
            ).astype(BF16)
        for gate_ref in rest[:-1]:
            gate_ref[t] = sigmoid(part[4] + same * vec[2]).astype(BF16)


def keep_product_kernel(cpd, q, prod_ref, nrm_ref, inv_ref):
    rows = q * cpd
    for t in range(nrm_ref.shape[0]):
        normed, inv_ref[t] = norm(unpack(prod_ref[:, t * rows : (t + 1) * rows, :], cpd))
        nrm_ref[t] = normed.astype(BF16)


def mix_edge_kernel(
    cpd, q, layer, prod_ref, z_ref, gate_ref, flags_ref, owt_ref, hgain_ref, hbias_ref, wt_ref,
    gain_ref, bias_ref, edges_ref, znext_ref, vec,
):
    tiles, _, lanes = z_ref.shape
    rows = q * cpd
    load_columns(vec, (hgain_ref, layer), (hbias_ref, layer), (gain_ref, layer + 1), (bias_ref, layer + 1))
    for t in range(tiles):
        here = slice(t * rows, (t + 1) * rows)
        hnormed, _ = norm(unpack(prod_ref[:, here, :], cpd))
        hscaled = (hnormed * vec[0] + vec[1]).astype(BF16)
        cells = z_ref[t].astype(F32) + gate_ref[t].astype(F32) * dot(owt_ref[...], hscaled, 1, 0)
        znext_ref[t] = cells
        emit_edges(
            edges_ref, here, cells, wt_ref, vec[2], vec[3], flags_ref[t, 0:1, :], cpd, lanes // q
        )


def mix_grad(upstream, hnormed, hinv, gate_ref, t, ow_ref, hgain):
    grad_mixed = (upstream * gate_ref[t].astype(F32)).astype(BF16)
    return norm_grad(dot(ow_ref[...], grad_mixed, 1, 0), hnormed, hinv, hgain)


def mix_back_kernel(cpd, q, layer, prod_ref, up_ref, gate_ref, ow_ref, hgain_ref, gp_ref, vec):
    tiles, _, lanes = up_ref.shape
    rows = q * cpd
    load_columns(vec, (hgain_ref, layer))
    for t in range(tiles):
        here = slice(t * rows, (t + 1) * rows)
        hnormed, hinv = norm(unpack(prod_ref[:, here, :], cpd))
        grad = mix_grad(up_ref[t].astype(F32), hnormed, hinv, gate_ref, t, ow_ref, vec[0])
        gp_ref[:, here, :] = pack(grad, cpd, lanes // q)


def mix_terms(upstream, product, gate, same, ow_ref, owt_ref, hgain, hbias, acc_ow, acc_hg, acc_hb, acc_ch):
    width = acc_hg.shape[1]
    hnormed, _ = norm(product)
    hscaled = (hnormed * hgain + hbias).astype(BF16)
    mixed = dot(owt_ref[...], hscaled, 1, 0)
    grad_gate = upstream * gate
    grad_logits = grad_gate * mixed * (1.0 - gate)
    grad_mixed = grad_gate.astype(BF16)
    acc_ow[...] += dot(hscaled, grad_mixed, 1, 1)
    grad_hscaled = dot(ow_ref[...], grad_mixed, 1, 0)
    acc_hg[...] += fold(grad_hscaled * hnormed, width)
    acc_hb[...] += fold(grad_hscaled, width)
    acc_ch[...] += fold(grad_logits * same, width)
    return grad_logits


def row_of(acc):
    return jnp.sum(acc.T, 0, keepdims=True)


def mix_terms_kernel(
    cpd, q, layer, prod_ref, up_ref, gate_ref, flags_ref, ow_ref, owt_ref, hgain_ref, hbias_ref,
    glog_ref, terms_ref, vec, acc_ow, acc_hg, acc_hb, acc_ch,
):
    rows = q * cpd
    load_columns(vec, (hgain_ref, layer), (hbias_ref, layer))
    clear(acc_ow, acc_hg, acc_hb, acc_ch)
    for t in range(up_ref.shape[0]):
        grad_logits = mix_terms(
            up_ref[t].astype(F32), unpack(prod_ref[:, t * rows : (t + 1) * rows, :], cpd),
            gate_ref[t].astype(F32), flags_ref[t, 1:2, :], ow_ref, owt_ref, vec[0], vec[1],
            acc_ow, acc_hg, acc_hb, acc_ch,
        )
        glog_ref[t] = grad_logits.astype(BF16)

    @last_step
    def _():
        hidden = acc_ow.shape[0]
        terms_ref[:hidden, :] = acc_ow[...]
        vectors = [row_of(acc_hg[...]), row_of(acc_hb[...]), row_of(acc_ch[...])]
        vectors.append(jnp.zeros((terms_ref.shape[0] - hidden - 3, hidden), F32))
        terms_ref[hidden:, :] = jnp.concatenate(vectors, 0)


def project_grad(left_ref, right_ref, fac_ref, glog_ref, t, cpd, rows):
    hidden = fac_ref.shape[1] // 4
    here = slice(t * rows, (t + 1) * rows)
    grads = (unpack(left_ref[:, here, :], cpd), unpack(right_ref[:, here, :], cpd))
    blocks = [
        (grads[n // 2] * fac_ref[t, n * hidden : (n + 1) * hidden, :].astype(F32)).astype(BF16)
        for n in range(4)
    ]
    return jnp.concatenate(blocks + [glog_ref[t]], 0)


def input_grad(gproj, nrm_ref, inv_ref, t, w_ref, gain):
    return norm_grad(dot(w_ref[...], gproj, 1, 0), nrm_ref[t].astype(F32), inv_ref[t], gain)


def edge_mix_back_kernel(
    cpd, q, layer, left_ref, right_ref, fac_ref, nrm_ref, inv_ref, glog_ref, up_ref, w_ref, gain_ref,
    hnrm_ref, hinv_ref, gate_ref, ow_ref, hgain_ref, upnext_ref, gp_ref, vec,
):
    tiles, _, lanes = up_ref.shape
    rows = q * cpd
    load_columns(vec, (gain_ref, layer), (hgain_ref, layer - 1))
    for t in range(tiles):
        gproj = project_grad(left_ref, right_ref, fac_ref, glog_ref, t, cpd, rows)
        upstream = up_ref[t].astype(F32) + input_grad(gproj, nrm_ref, inv_ref, t, w_ref, vec[0])
        upnext_ref[t] = upstream
        grad = mix_grad(upstream, hnrm_ref[t].astype(F32), hinv_ref[t], gate_ref, t, ow_ref, vec[1])
        gp_ref[:, t * rows : (t + 1) * rows, :] = pack(grad, cpd, lanes // q)


def edge_terms(gproj, low_ref, nrm_ref, t, acc_w):
    ones = jnp.ones((16, gproj.shape[1]), BF16)
    acc_w[...] += dot(jnp.concatenate([low_ref[t], nrm_ref[t], ones], 0), gproj, 1, 1)


def finish_edge(out_ref, acc_w, w_ref):
    width = w_ref.shape[0]
    for n in range(acc_w.shape[1] // width):
        out_ref[n * width : (n + 1) * width, :] = acc_w[:width, n * width : (n + 1) * width].astype(BF16)
    weight = w_ref[...].astype(F32)
    gain = row_of(fold(weight * acc_w[width : 2 * width, :], width))
    bias = row_of(fold(weight * acc_w[2 * width : 2 * width + 1, :], width))
    return [gain, bias]


def finish_rows(out_ref, first, vectors):
    pad = jnp.zeros((out_ref.shape[0] - first - sum(v.shape[0] for v in vectors), out_ref.shape[1]), F32)
    out_ref[first:, :] = jnp.concatenate(vectors + [pad], 0).astype(BF16)


def late_terms_kernel(
    cpd, q, layer, left_ref, right_ref, fac_ref, low_ref, nrm_ref, glog_ref, w_ref, terms_ref,
    prod_ref, up_ref, gate_ref, flags_ref, ow_ref, owt_ref, hgain_ref, hbias_ref,
    glognext_ref, all_ref, vec, acc_w, acc_ow, acc_hg, acc_hb, acc_ch,
):
    rows = q * cpd
    load_columns(vec, (hgain_ref, layer - 1), (hbias_ref, layer - 1))
    clear(acc_w, acc_ow, acc_hg, acc_hb, acc_ch)
    for t in range(up_ref.shape[0]):
        gproj = project_grad(left_ref, right_ref, fac_ref, glog_ref, t, cpd, rows)
        edge_terms(gproj, low_ref, nrm_ref, t, acc_w)
        grad_logits = mix_terms(
            up_ref[t], unpack(prod_ref[:, t * rows : (t + 1) * rows, :], cpd), gate_ref[t].astype(F32),
            flags_ref[t, 1:2, :], ow_ref, owt_ref, vec[0], vec[1], acc_ow, acc_hg, acc_hb, acc_ch,
        )
        glognext_ref[t] = grad_logits.astype(BF16)

    @last_step
    def _():
        hidden = acc_ow.shape[0]
        vectors = finish_edge(all_ref, acc_w, w_ref)
        all_ref[5 * hidden : 6 * hidden, :] = terms_ref[:hidden, :].astype(BF16)
        all_ref[6 * hidden : 7 * hidden, :] = acc_ow[...].astype(BF16)
        vectors += [terms_ref[hidden : hidden + 3, :]]
        vectors += [row_of(acc_hg[...]), row_of(acc_hb[...]), row_of(acc_ch[...])]
        finish_rows(all_ref, 7 * hidden, vectors)


def last_terms_kernel(
    cpd, q, left_ref, right_ref, fac_ref, low_ref, nrm_ref, glog_ref, w_ref, all_ref, acc_w,
):
    clear(acc_w)
    for t in range(low_ref.shape[0]):
        gproj = project_grad(left_ref, right_ref, fac_ref, glog_ref, t, cpd, q * cpd)
        edge_terms(gproj, low_ref, nrm_ref, t, acc_w)

    @last_step
    def _():
        finish_rows(all_ref, acc_w.shape[1], finish_edge(all_ref, acc_w, w_ref))


def pair_grad_kernel(
    cpd, q, layer, left_ref, right_ref, fac_ref, nrm_ref, inv_ref, glog_ref, up_ref, w_ref, gain_ref, pair_ref, vec,
):
    tiles, _, lanes = up_ref.shape
    cols = lanes // q
    load_columns(vec, (gain_ref, layer))
    for t in range(tiles):
        gproj = project_grad(left_ref, right_ref, fac_ref, glog_ref, t, cpd, q * cpd)
        upstream = up_ref[t] + input_grad(gproj, nrm_ref, inv_ref, t, w_ref, vec[0])
        for a in range(q):
            pair_ref[t * q + a] = upstream[:, a * cols : (a + 1) * cols].T.astype(BF16)


def spread_kernel(got_ref, out_ref):
    total = jnp.sum(got_ref[...].astype(F32), 0).astype(BF16)
    out_ref[...] = jnp.broadcast_to(total[None], out_ref.shape)


def unpack_kernel(factor, early_ref, late_ref, proj_ref, ow_ref, inorm_ref, hnorm_ref, chain_ref):
    width = ow_ref.shape[1]
    early = early_ref[...].astype(F32) * factor
    late = late_ref[...].astype(F32).reshape(-1, width) * factor
    for n in range(5):
        rows, lanes = slice(n * width, (n + 1) * width), slice(n * width, (n + 1) * width)
        proj_ref[0, :, lanes] = late[rows]
        proj_ref[1, :, lanes] = early[rows]
    ow_ref[1] = early[5 * width : 6 * width]
    ow_ref[0] = early[6 * width : 7 * width]
    inorm_ref[0] = late[5 * width : 5 * width + 2]
    vectors = early[7 * width : 7 * width + 8]
    inorm_ref[1] = vectors[0:2]
    hnorm_ref[1] = vectors[2:4]
    hnorm_ref[0] = vectors[5:7]
    chain_ref[...] = jnp.concatenate([vectors[7:8], vectors[4:5]], 0)


def cell_call(kernel, steps, ins, outs, scratch, prefetch=(), flops=0):
    def spec(shape, how):
        if how is None:
            return pl.BlockSpec(shape, lambda *s: (0,) * len(shape))
        axis, first, size = how if isinstance(how, tuple) else (how, 0, shape[how] // steps)
        block = tuple(size if n == axis else length for n, length in enumerate(shape))
        moves = shape[axis] >= size * steps
        return pl.BlockSpec(
            block,
            lambda *s: tuple((s[0] if moves else 0) + first if n == axis else 0 for n in range(len(shape))),
        )

    moved = sum(a.size * a.dtype.itemsize for a, _ in ins)
    moved += sum(functools.reduce(lambda x, y: x * y, s, 1) * jnp.dtype(t).itemsize for (s, t), _ in outs)
    return pl.pallas_call(
        kernel,
        grid_spec=pltpu.PrefetchScalarGridSpec(
            num_scalar_prefetch=len(prefetch),
            grid=(steps,),
            in_specs=[spec(a.shape, how) for a, how in ins],
            out_specs=[spec(s, how) for (s, _), how in outs],
            scratch_shapes=scratch,
        ),
        out_shape=[jax.ShapeDtypeStruct(s, t) for (s, t), _ in outs],
        compiler_params=pltpu.CompilerParams(vmem_limit_bytes=LARGE_VMEM_BYTES),
        cost_estimate=pl.CostEstimate(flops=flops, bytes_accessed=int(moved), transcendentals=0),
    )(*prefetch, *[a for a, _ in ins])


def widen(src_ref, dst):
    devices, cols = src_ref.shape[0], src_ref.shape[-1]
    per = dst.shape[0] // devices
    for d in range(devices):
        dst[d * per : (d + 1) * per, :] = src_ref[d].astype(F32).reshape(per, cols)


def narrow(src, dst_ref):
    devices = dst_ref.shape[0]
    per = src.shape[0] // devices
    for d in range(devices):
        dst_ref[d, :per, :] = src[d * per : (d + 1) * per, :].astype(BF16)


def get_channel(src, ch, sub, subs, dims):
    row_devs, col_devs, rows, cpd, cols = dims
    halves = []
    for s in range(col_devs):
        parts = []
        for r in range(row_devs):
            base = ((r * col_devs + s) * subs + sub) * rows * cpd
            parts.append(src[pl.ds(base + ch, rows, stride=cpd), :])
        halves.append(jnp.concatenate(parts, 0))
    return jnp.concatenate(halves, 1).astype(BF16)


def put_channel(dst, value, ch, sub, subs, dims):
    row_devs, col_devs, rows, cpd, cols = dims
    for s in range(col_devs):
        for r in range(row_devs):
            base = ((r * col_devs + s) * subs + sub) * rows * cpd
            dst[pl.ds(base + ch, rows, stride=cpd), :] = value[
                r * rows : (r + 1) * rows, s * cols : (s + 1) * cols
            ]


def product_kernel(dims, outgoing, edges_ref, out_ref, edges, result):
    widen(edges_ref, edges)
    for ch in range(dims[3]):
        left = get_channel(edges, ch, 0, 2, dims)
        right = get_channel(edges, ch, 1, 2, dims)
        value = dot(left, right, 1, 1) if outgoing else dot(left, right, 0, 0)
        put_channel(result, value, ch, 0, 1, dims)
    narrow(result, out_ref)


def assemble_kernel(dims, edges_ref, out_ref, edges):
    widen(edges_ref, edges)
    for ch in range(dims[3]):
        for sub in range(2):
            out_ref[ch, sub] = get_channel(edges, ch, sub, 2, dims)


def product_grad_kernel(dims, outgoing, sides_ref, grad_ref, out_ref, grad, result):
    widen(grad_ref, grad)
    for ch in range(dims[3]):
        left, right = sides_ref[ch, 0], sides_ref[ch, 1]
        gp = get_channel(grad, ch, 0, 1, dims)
        if outgoing:
            grad_left = dot(gp, right, 1, 0)
            grad_right = dot(gp, left, 0, 0)
        else:
            grad_left = dot(right, gp, 1, 1)
            grad_right = dot(left, gp, 1, 0)
        put_channel(result, grad_left, ch, 0, 2, dims)
        put_channel(result, grad_right, ch, 1, 2, dims)
    narrow(result, out_ref)


def whole_call(kernel, ins, outs, scratch, flops):
    moved = sum(a.size * a.dtype.itemsize for a in ins)
    moved += sum(functools.reduce(lambda x, y: x * y, s, 1) * jnp.dtype(t).itemsize for s, t in outs)
    specs = [pl.BlockSpec(memory_space=pltpu.VMEM)] * len(outs)
    shapes = [jax.ShapeDtypeStruct(s, t) for s, t in outs]
    return pl.pallas_call(
        kernel,
        in_specs=[pl.BlockSpec(memory_space=pltpu.VMEM)] * len(ins),
        out_specs=specs if len(outs) > 1 else specs[0],
        out_shape=shapes if len(outs) > 1 else shapes[0],
        scratch_shapes=scratch,
        compiler_params=pltpu.CompilerParams(vmem_limit_bytes=VMEM_BYTES),
        cost_estimate=pl.CostEstimate(flops=flops, bytes_accessed=int(moved), transcendentals=0),
    )(*ins)


def exchange(array):
    return lax.all_to_all(array, AXES, split_axis=0, concat_axis=0, tiled=True)


def after(array, *others):
    return lax.optimization_barrier((array, *others))[0]


def shards(
    pair_rep, cotangent, residue_mask, chain_ids, proj_weight, out_weight,
    input_gain, input_bias, hidden_gain, hidden_bias, chain_bias,
):
    rows, cols, width = pair_rep.shape
    hidden = out_weight.shape[1]
    row_devs, col_devs = lax.axis_size("row"), lax.axis_size("col")
    devices = row_devs * col_devs
    length = rows * row_devs
    cpd = hidden // devices
    q = max(1, 16 // cpd)
    tiles = rows // q
    lanes = q * cols
    steps = max(1, tiles // 4)
    dims = (row_devs, col_devs, rows, cpd, cols)
    side = rows * cpd

    starts = jnp.stack([lax.axis_index("row") * rows, lax.axis_index("col")]).astype(jnp.int32)
    wt = [proj_weight[n].T for n in range(2)]
    owt = [out_weight[n].T for n in range(2)]
    weight = [proj_weight[n] for n in range(2)]
    mixer = [out_weight[n] for n in range(2)]
    mask_cols, chain_cols = residue_mask.reshape(col_devs, cols), chain_ids.reshape(col_devs, cols)
    scalars = (residue_mask, chain_ids, starts)
    tile = (tiles, width, lanes)
    fac_tile = (tiles, 4 * hidden, lanes)
    edge_shape = (devices, 2, side, cols)
    cell_shape = (devices, side, cols)
    vec = lambda n: pltpu.VMEM((n, width, lanes), F32)
    acc = lambda n, m=width: pltpu.VMEM((m, n), F32)
    wide = lambda n: pltpu.VMEM((n * devices * side, cols), F32)
    cell_flops = 2 * rows * cols * width * hidden
    tri_flops = 2 * cpd * length**3
    rows_for = lambda n: -(-n // (devices * 16)) * 16
    early_rows, late_rows = rows_for(7 * hidden + 8), rows_for(5 * hidden + 2)
    terms_shape = (hidden + 8, hidden)

    def product(edges, outgoing):
        return whole_call(
            functools.partial(product_kernel, dims, outgoing), [edges], [(cell_shape, BF16)],
            [wide(2), wide(1)], tri_flops,
        )

    def assemble(edges):
        return whole_call(
            functools.partial(assemble_kernel, dims), [edges], [((cpd, 2, length, length), BF16)], [wide(2)], 0
        )

    def product_grad(sides, grad, outgoing):
        return whole_call(
            functools.partial(product_grad_kernel, dims, outgoing), [sides, grad],
            [((devices, 2 * side, cols), BF16)], [wide(1), wide(2)], 2 * tri_flops,
        )

    def halves(grads):
        per = side // steps
        return [(grads, (1, 0, per)), (grads, (1, steps, per))]

    def keep(layer, z, with_gate):
        norm_outs = [((tile, BF16), 0), ((tile, BF16), 0), (((tiles, 1, lanes), F32), 0)]
        return cell_call(
            functools.partial(keep_kernel, layer), steps,
            [
                (z, 0), (flags, 0), (wt[layer], None), (input_gain, None), (input_bias, None), (chain_bias, None),
            ],
            [((fac_tile, BF16), 0)] + norm_outs + [((tile, BF16), 0)] * with_gate,
            [vec(3)], flops=5 * cell_flops,
        )

    (edges0,) = cell_call(
        functools.partial(edge_first_kernel, cpd, q), steps,
        [
            (pair_rep, 0), (mask_cols, None), (chain_cols, None), (proj_weight, (0, 0, 1)),
            (input_gain, None), (input_bias, None),
        ],
        [((edge_shape, BF16), 2)], [vec(2), pltpu.VMEM((5 * hidden, width), BF16)],
        prefetch=scalars, flops=4 * cell_flops,
    )
    got0 = exchange(edges0)
    z0, up, gate0, flags = cell_call(
        functools.partial(first_keep_kernel, q), steps,
        [
            (after(pair_rep, edges0), 0), (cotangent, 0), (mask_cols, None), (chain_cols, None), (wt[0], None),
            (input_gain, None), (input_bias, None), (chain_bias, None),
        ],
        [((tile, BF16), 0), ((tile, BF16), 0), ((tile, BF16), 0), (((tiles, 2, lanes), F32), 0)],
        [vec(3)], prefetch=scalars, flops=2 * cell_flops,
    )
    made0 = product(after(got0, z0), True)
    prod0 = exchange(made0)
    sides0 = assemble(after(got0, made0))
    edges1, z1 = cell_call(
        functools.partial(mix_edge_kernel, cpd, q, 0), steps,
        [
            (after(prod0, sides0), 1), (z0, 0), (gate0, 0), (flags, 0), (owt[0], None), (hidden_gain, None),
            (hidden_bias, None), (wt[1], None), (input_gain, None), (input_bias, None),
        ],
        [((edge_shape, BF16), 2), ((tile, F32), 0)], [vec(4)], flops=5 * cell_flops,
    )
    got1 = exchange(edges1)
    fac1, low1, nrm1, inv1, gate1 = keep(1, after(z1, edges1), True)
    made1 = product(after(got1, gate1), False)
    prod1 = exchange(made1)
    sides1 = assemble(after(got1, made1))

    (grad1,) = cell_call(
        functools.partial(mix_back_kernel, cpd, q, 1), steps,
        [(after(prod1, sides1), 1), (up, 0), (gate1, 0), (mixer[1], None), (hidden_gain, None)],
        [((cell_shape, BF16), 1)], [vec(1)], flops=cell_flops,
    )
    got_grad1 = exchange(grad1)
    hnrm0, hinv0 = cell_call(
        functools.partial(keep_product_kernel, cpd, q), steps, [(after(prod0, grad1), 1)],
        [((tile, BF16), 0), (((tiles, 1, lanes), F32), 0)], [],
    )
    made_grads1 = product_grad(sides1, after(got_grad1, hnrm0), False)
    grads1 = exchange(made_grads1)
    glog1, terms1 = cell_call(
        functools.partial(mix_terms_kernel, cpd, q, 1), steps,
        [
            (after(prod1, made_grads1), 1), (up, 0), (gate1, 0), (flags, 0), (mixer[1], None), (owt[1], None),
            (hidden_gain, None), (hidden_bias, None),
        ],
        [((tile, BF16), 0), ((terms_shape, F32), None)],
        [vec(2), acc(hidden), acc(cols), acc(cols), acc(cols)], flops=3 * cell_flops,
    )
    up0, grad0 = cell_call(
        functools.partial(edge_mix_back_kernel, cpd, q, 1), steps,
        halves(after(grads1, glog1))
        + [
            (fac1, 0), (nrm1, 0), (inv1, 0), (glog1, 0), (up, 0), (weight[1], None), (input_gain, None),
            (hnrm0, 0), (hinv0, 0), (gate0, 0), (mixer[0], None), (hidden_gain, None),
        ],
        [((tile, F32), 0), ((cell_shape, BF16), 1)],
        [vec(2)], flops=6 * cell_flops,
    )
    got_grad0 = exchange(grad0)
    glog0, early = cell_call(
        functools.partial(late_terms_kernel, cpd, q, 1), steps,
        halves(after(grads1, grad0))
        + [
            (fac1, 0), (low1, 0), (nrm1, 0), (glog1, 0), (weight[1], None), (terms1, None), (prod0, 1),
            (up0, 0), (gate0, 0), (flags, 0), (mixer[0], None), (owt[0], None), (hidden_gain, None),
            (hidden_bias, None),
        ],
        [((tile, BF16), 0), (((devices * early_rows, hidden), BF16), None)],
        [vec(2), acc(5 * hidden, 2 * width + 16), acc(hidden), acc(cols), acc(cols), acc(cols)],
        flops=13 * cell_flops,
    )

    early = lax.psum(early, AXES)
    made_grads0 = product_grad(sides0, got_grad0, True)
    grads0 = exchange(made_grads0)
    fac0, low0, nrm0, inv0 = keep(0, after(z0, made_grads0), False)
    grads0 = after(grads0, nrm0)
    (late,) = cell_call(
        functools.partial(last_terms_kernel, cpd, q), steps,
        halves(grads0) + [(fac0, 0), (low0, 0), (nrm0, 0), (glog0, 0), (weight[0], None)],
        [(((devices * late_rows, hidden), BF16), None)],
        [acc(5 * hidden, 2 * width + 16)], flops=10 * cell_flops,
    )
    got_late = exchange(late.reshape(devices, late_rows, hidden))
    (grad_pair,) = cell_call(
        functools.partial(pair_grad_kernel, cpd, q, 0), steps,
        halves(after(grads0, late))
        + [(fac0, 0), (nrm0, 0), (inv0, 0), (glog0, 0), (up0, 0), (weight[0], None), (input_gain, None)],
        [((pair_rep.shape, BF16), 0)], [vec(1)], flops=5 * cell_flops,
    )
    spread = whole_call(spread_kernel, [after(got_late, grad_pair)], [((devices, late_rows, hidden), BF16)], [], 0)
    proj, out, inorm, hnorm, chain = whole_call(
        functools.partial(unpack_kernel, 1.0 / length), [early, exchange(spread)],
        [
            ((2, width, 5 * hidden), F32), ((2, hidden, hidden), F32), ((2, 2, hidden), F32),
            ((2, 2, hidden), F32), ((2, hidden), F32),
        ],
        [], 0,
    )
    return grad_pair, proj, out, inorm, hnorm, chain


def solution(mesh):
    cells = P(("grp", "row"), "col", None)
    return jax.shard_map(
        shards,
        mesh=mesh,
        in_specs=(cells, cells, P("grp"), P("grp")) + (P(),) * 7,
        out_specs=(
            cells, P("grp", None, None), P("grp", None, None), P("grp", None, None),
            P("grp", None, None), P("grp", None),
        ),
        check_vma=False,
    )
```

```python
import functools

import jax
import jax.numpy as jnp
from jax import lax
from jax.experimental import pallas as pl
from jax.experimental.pallas import tpu as pltpu
from jax.sharding import PartitionSpec as P

EPSILON = 1e-05
AXES = ("row", "col")
F32 = jnp.float32
BF16 = jnp.bfloat16
CHANNEL_VMEM = 24 * 1024 * 1024
CELL_VMEM = 50 * 1024 * 1024
ALL_VMEM = 60 * 1024 * 1024


def dot(a, b, ca, cb):
    return lax.dot_general(a, b, (((ca,), (cb,)), ((), ())), preferred_element_type=F32)


def sigmoid(x):
    return 0.5 * jnp.tanh(0.5 * x) + 0.5


def columns(vectors, width):
    c = vectors.shape[1]
    square = jnp.broadcast_to(vectors, (c, c)).T
    return jnp.concatenate([square] * (width // c), 1)


def norm(x):
    centred = x - jnp.mean(x, 0, keepdims=True)
    inv = lax.rsqrt(jnp.mean(centred * centred, 0, keepdims=True) + EPSILON)
    return centred * inv, inv


def norm_grad(grad_scaled, normed, inv, gain):
    g = grad_scaled * gain
    first = jnp.mean(g, 0, keepdims=True)
    second = jnp.mean(g * normed, 0, keepdims=True)
    return (g - first - normed * second) * inv


def unpack(block, cpd):
    devices, rows, cols = block.shape
    values = block.astype(F32)
    parts = []
    for a in range(rows // cpd):
        if cpd % 8 == 0:
            parts.append(values[:, a * cpd : (a + 1) * cpd, :].reshape(devices * cpd, cols))
        else:
            parts.append(
                jnp.concatenate([values[d, a * cpd : (a + 1) * cpd, :] for d in range(devices)], 0)
            )
    return jnp.concatenate(parts, 1)


def pack(tile, cpd, cols):
    channels, lanes = tile.shape
    devices = channels // cpd
    parts = [tile[:, a * cols : (a + 1) * cols] for a in range(lanes // cols)]
    if cpd % 8 == 0:
        return jnp.concatenate([p.reshape(devices, cpd, cols) for p in parts], 1).astype(BF16)
    return jnp.stack(
        [
            jnp.concatenate([p[d * cpd : (d + 1) * cpd, :] for p in parts], 0)
            for d in range(devices)
        ]
    ).astype(BF16)


def fold(tile, width):
    return sum(tile[:, a : a + width] for a in range(0, tile.shape[1], width))


def project(lowered, wt_ref, first, last):
    hidden = wt_ref.shape[0] // 5
    projected = dot(wt_ref[first * hidden : last * hidden, :], lowered, 1, 0)
    return [projected[n * hidden : (n + 1) * hidden] for n in range(last - first)]


def lower(cells, gain, bias):
    normed, inv = norm(cells)
    return normed, inv, (normed * gain + bias).astype(BF16)


def emit_edges(edges_ref, here, cells, wt_ref, gain, bias, mask, cpd, cols):
    part = project(lower(cells, gain, bias)[2], wt_ref, 0, 4)
    edges_ref[:, 0, here, :] = pack(part[0] * sigmoid(part[1]) * mask, cpd, cols)
    edges_ref[:, 1, here, :] = pack(part[2] * sigmoid(part[3]) * mask, cpd, cols)


def first_step(fill):
    pl.when(pl.program_id(0) == 0)(fill)


def last_step(fill):
    pl.when(pl.program_id(0) == pl.num_programs(0) - 1)(fill)


def load_columns(vec, *rows):
    @first_step
    def _():
        for n, (ref, layer) in enumerate(rows):
            vec[n] = columns(ref[layer : layer + 1, :], vec.shape[2])


def clear(*accs):
    @first_step
    def _():
        for acc in accs:
            acc[...] = jnp.zeros_like(acc)


def turned(ref, t, q):
    return jnp.concatenate([ref[t * q + a].astype(F32).T for a in range(q)], 1)


def row_flags(row, mask_smem, chain_smem, start_smem, maskc_ref, chainc_ref):
    whole = start_smem[0] + row
    here = pl.ds(start_smem[1], 1)
    mask = (maskc_ref[here, :] * mask_smem[whole]).astype(F32)
    return mask, (chainc_ref[here, :] == chain_smem[whole]).astype(F32)


def edge_first_kernel(
    cpd, q, mask_smem, chain_smem, start_smem, pair_ref, maskc_ref, chainc_ref, w_ref, gain_ref, bias_ref,
    edges_ref, vec, turned_weight,
):
    rows, cols, width = pair_ref.shape
    load_columns(vec, (gain_ref, 0), (bias_ref, 0))

    @first_step
    def _():
        for n in range(turned_weight.shape[0] // width):
            block = slice(n * width, (n + 1) * width)
            turned_weight[block, :] = w_ref[0, :, block].astype(F32).T.astype(BF16)

    for t in range(rows // q):
        first = pl.program_id(0) * rows + t * q
        mask = jnp.concatenate(
            [
                row_flags(first + a, mask_smem, chain_smem, start_smem, maskc_ref, chainc_ref)[0]
                for a in range(q)
            ],
            1,
        )
        here = slice(t * q * cpd, (t + 1) * q * cpd)
        emit_edges(edges_ref, here, turned(pair_ref, t, q), turned_weight, vec[0], vec[1], mask, cpd, cols)


def first_keep_kernel(
    q, mask_smem, chain_smem, start_smem, pair_ref, cot_ref, maskc_ref, chainc_ref, wt_ref, gain_ref,
    bias_ref, chain_ref, z_ref, up_ref, gate_ref, flags_ref, vec,
):
    load_columns(vec, (gain_ref, 0), (bias_ref, 0), (chain_ref, 0))
    tiles = z_ref.shape[0]
    for t in range(tiles):
        flags = [
            row_flags(
                (pl.program_id(0) * tiles + t) * q + a, mask_smem, chain_smem, start_smem, maskc_ref, chainc_ref
            )
            for a in range(q)
        ]
        mask = jnp.concatenate([f[0] for f in flags], 1)
        same = jnp.concatenate([f[1] for f in flags], 1)
        cells = turned(pair_ref, t, q)
        z_ref[t] = cells.astype(BF16)
        up_ref[t] = turned(cot_ref, t, q).astype(BF16)
        flags_ref[t] = jnp.concatenate([mask, same], 0)
        (logits,) = project(lower(cells, vec[0], vec[1])[2], wt_ref, 4, 5)
        gate_ref[t] = sigmoid(logits + same * vec[2]).astype(BF16)


def keep_kernel(layer, z_ref, flags_ref, wt_ref, gain_ref, bias_ref, chain_ref, fac_ref, low_ref, nrm_ref, inv_ref, *rest):
    vec = rest[-1]
    hidden = wt_ref.shape[0] // 5
    load_columns(vec, (gain_ref, layer), (bias_ref, layer), (chain_ref, layer))
    for t in range(z_ref.shape[0]):
        mask, same = flags_ref[t, 0:1, :], flags_ref[t, 1:2, :]
        normed, inv_ref[t], lowered = lower(z_ref[t].astype(F32), vec[0], vec[1])
        low_ref[t] = lowered
        nrm_ref[t] = normed.astype(BF16)
        part = project(lowered, wt_ref, 0, 3 + len(rest))
        for n in (0, 2):
            sig = sigmoid(part[n + 1]) * mask
            fac_ref[t, n * hidden : (n + 1) * hidden, :] = sig.astype(BF16)
            fac_ref[t, (n + 1) * hidden : (n + 2) * hidden, :] = (
                part[n] * sig * (1.0 - sig)
            ).astype(BF16)
        for gate_ref in rest[:-1]:
            gate_ref[t] = sigmoid(part[4] + same * vec[2]).astype(BF16)


def keep_product_kernel(cpd, q, prod_ref, nrm_ref, inv_ref):
    rows = q * cpd
    for t in range(nrm_ref.shape[0]):
        normed, inv_ref[t] = norm(unpack(prod_ref[:, t * rows : (t + 1) * rows, :], cpd))
        nrm_ref[t] = normed.astype(BF16)


def mix_edge_kernel(
    cpd, q, layer, prod_ref, z_ref, gate_ref, flags_ref, owt_ref, hgain_ref, hbias_ref, wt_ref,
    gain_ref, bias_ref, edges_ref, znext_ref, vec,
):
    tiles, _, lanes = z_ref.shape
    rows = q * cpd
    load_columns(vec, (hgain_ref, layer), (hbias_ref, layer), (gain_ref, layer + 1), (bias_ref, layer + 1))
    for t in range(tiles):
        here = slice(t * rows, (t + 1) * rows)
        hnormed, _ = norm(unpack(prod_ref[:, here, :], cpd))
        hscaled = (hnormed * vec[0] + vec[1]).astype(BF16)
        cells = z_ref[t].astype(F32) + gate_ref[t].astype(F32) * dot(owt_ref[...], hscaled, 1, 0)
        znext_ref[t] = cells
        emit_edges(
            edges_ref, here, cells, wt_ref, vec[2], vec[3], flags_ref[t, 0:1, :], cpd, lanes // q
        )


def mix_grad(upstream, hnormed, hinv, gate_ref, t, ow_ref, hgain):
    grad_mixed = (upstream * gate_ref[t].astype(F32)).astype(BF16)
    return norm_grad(dot(ow_ref[...], grad_mixed, 1, 0), hnormed, hinv, hgain)


def mix_back_kernel(cpd, q, layer, prod_ref, up_ref, gate_ref, ow_ref, hgain_ref, gp_ref, vec):
    tiles, _, lanes = up_ref.shape
    rows = q * cpd
    load_columns(vec, (hgain_ref, layer))
    for t in range(tiles):
        here = slice(t * rows, (t + 1) * rows)
        hnormed, hinv = norm(unpack(prod_ref[:, here, :], cpd))
        grad = mix_grad(up_ref[t].astype(F32), hnormed, hinv, gate_ref, t, ow_ref, vec[0])
        gp_ref[:, here, :] = pack(grad, cpd, lanes // q)


def mix_terms(upstream, product, gate, same, ow_ref, owt_ref, hgain, hbias, acc_ow, acc_hg, acc_hb, acc_ch):
    width = acc_hg.shape[1]
    hnormed, _ = norm(product)
    hscaled = (hnormed * hgain + hbias).astype(BF16)
    mixed = dot(owt_ref[...], hscaled, 1, 0)
    grad_gate = upstream * gate
    grad_logits = grad_gate * mixed * (1.0 - gate)
    grad_mixed = grad_gate.astype(BF16)
    acc_ow[...] += dot(hscaled, grad_mixed, 1, 1)
    grad_hscaled = dot(ow_ref[...], grad_mixed, 1, 0)
    acc_hg[...] += fold(grad_hscaled * hnormed, width)
    acc_hb[...] += fold(grad_hscaled, width)
    acc_ch[...] += fold(grad_logits * same, width)
    return grad_logits


def row_of(acc):
    return jnp.sum(acc.T, 0, keepdims=True)


def mix_terms_kernel(
    cpd, q, layer, prod_ref, up_ref, gate_ref, flags_ref, ow_ref, owt_ref, hgain_ref, hbias_ref,
    glog_ref, terms_ref, vec, acc_ow, acc_hg, acc_hb, acc_ch,
):
    rows = q * cpd
    load_columns(vec, (hgain_ref, layer), (hbias_ref, layer))
    clear(acc_ow, acc_hg, acc_hb, acc_ch)
    for t in range(up_ref.shape[0]):
        grad_logits = mix_terms(
            up_ref[t].astype(F32), unpack(prod_ref[:, t * rows : (t + 1) * rows, :], cpd),
            gate_ref[t].astype(F32), flags_ref[t, 1:2, :], ow_ref, owt_ref, vec[0], vec[1],
            acc_ow, acc_hg, acc_hb, acc_ch,
        )
        glog_ref[t] = grad_logits.astype(BF16)

    @last_step
    def _():
        hidden = acc_ow.shape[0]
        terms_ref[:hidden, :] = acc_ow[...]
        vectors = [row_of(acc_hg[...]), row_of(acc_hb[...]), row_of(acc_ch[...])]
        vectors.append(jnp.zeros((terms_ref.shape[0] - hidden - 3, hidden), F32))
        terms_ref[hidden:, :] = jnp.concatenate(vectors, 0)


def project_grad(left_ref, right_ref, fac_ref, glog_ref, t, cpd, rows):
    hidden = fac_ref.shape[1] // 4
    here = slice(t * rows, (t + 1) * rows)
    grads = (unpack(left_ref[:, here, :], cpd), unpack(right_ref[:, here, :], cpd))
    blocks = [
        (grads[n // 2] * fac_ref[t, n * hidden : (n + 1) * hidden, :].astype(F32)).astype(BF16)
        for n in range(4)
    ]
    return jnp.concatenate(blocks + [glog_ref[t]], 0)


def input_grad(gproj, nrm_ref, inv_ref, t, w_ref, gain):
    return norm_grad(dot(w_ref[...], gproj, 1, 0), nrm_ref[t].astype(F32), inv_ref[t], gain)


def edge_mix_back_kernel(
    cpd, q, layer, left_ref, right_ref, fac_ref, nrm_ref, inv_ref, glog_ref, up_ref, w_ref, gain_ref,
    hnrm_ref, hinv_ref, gate_ref, ow_ref, hgain_ref, upnext_ref, gp_ref, vec,
):
    tiles, _, lanes = up_ref.shape
    rows = q * cpd
    load_columns(vec, (gain_ref, layer), (hgain_ref, layer - 1))
    for t in range(tiles):
        gproj = project_grad(left_ref, right_ref, fac_ref, glog_ref, t, cpd, rows)
        upstream = up_ref[t].astype(F32) + input_grad(gproj, nrm_ref, inv_ref, t, w_ref, vec[0])
        upnext_ref[t] = upstream
        grad = mix_grad(upstream, hnrm_ref[t].astype(F32), hinv_ref[t], gate_ref, t, ow_ref, vec[1])
        gp_ref[:, t * rows : (t + 1) * rows, :] = pack(grad, cpd, lanes // q)


def edge_terms(gproj, low_ref, nrm_ref, t, acc_w):
    ones = jnp.ones((16, gproj.shape[1]), BF16)
    acc_w[...] += dot(jnp.concatenate([low_ref[t], nrm_ref[t], ones], 0), gproj, 1, 1)


def finish_edge(out_ref, acc_w, w_ref):
    width = w_ref.shape[0]
    for n in range(acc_w.shape[1] // width):
        out_ref[n * width : (n + 1) * width, :] = acc_w[:width, n * width : (n + 1) * width].astype(BF16)
    weight = w_ref[...].astype(F32)
    gain = row_of(fold(weight * acc_w[width : 2 * width, :], width))
    bias = row_of(fold(weight * acc_w[2 * width : 2 * width + 1, :], width))
    return [gain, bias]


def finish_rows(out_ref, first, vectors):
    pad = jnp.zeros((out_ref.shape[0] - first - sum(v.shape[0] for v in vectors), out_ref.shape[1]), F32)
    out_ref[first:, :] = jnp.concatenate(vectors + [pad], 0).astype(BF16)


def late_terms_kernel(
    cpd, q, layer, left_ref, right_ref, fac_ref, low_ref, nrm_ref, glog_ref, w_ref, terms_ref,
    prod_ref, up_ref, gate_ref, flags_ref, ow_ref, owt_ref, hgain_ref, hbias_ref,
    glognext_ref, all_ref, vec, acc_w, acc_ow, acc_hg, acc_hb, acc_ch,
):
    rows = q * cpd
    load_columns(vec, (hgain_ref, layer - 1), (hbias_ref, layer - 1))
    clear(acc_w, acc_ow, acc_hg, acc_hb, acc_ch)
    for t in range(up_ref.shape[0]):
        gproj = project_grad(left_ref, right_ref, fac_ref, glog_ref, t, cpd, rows)
        edge_terms(gproj, low_ref, nrm_ref, t, acc_w)
        grad_logits = mix_terms(
            up_ref[t], unpack(prod_ref[:, t * rows : (t + 1) * rows, :], cpd), gate_ref[t].astype(F32),
            flags_ref[t, 1:2, :], ow_ref, owt_ref, vec[0], vec[1], acc_ow, acc_hg, acc_hb, acc_ch,
        )
        glognext_ref[t] = grad_logits.astype(BF16)

    @last_step
    def _():
        hidden = acc_ow.shape[0]
        vectors = finish_edge(all_ref, acc_w, w_ref)
        all_ref[5 * hidden : 6 * hidden, :] = terms_ref[:hidden, :].astype(BF16)
        all_ref[6 * hidden : 7 * hidden, :] = acc_ow[...].astype(BF16)
        vectors += [terms_ref[hidden : hidden + 3, :]]
        vectors += [row_of(acc_hg[...]), row_of(acc_hb[...]), row_of(acc_ch[...])]
        finish_rows(all_ref, 7 * hidden, vectors)


def last_terms_kernel(
    cpd, q, left_ref, right_ref, fac_ref, low_ref, nrm_ref, glog_ref, w_ref, all_ref, acc_w,
):
    clear(acc_w)
    for t in range(low_ref.shape[0]):
        gproj = project_grad(left_ref, right_ref, fac_ref, glog_ref, t, cpd, q * cpd)
        edge_terms(gproj, low_ref, nrm_ref, t, acc_w)

    @last_step
    def _():
        finish_rows(all_ref, acc_w.shape[1], finish_edge(all_ref, acc_w, w_ref))


def pair_grad_kernel(
    cpd, q, layer, left_ref, right_ref, fac_ref, nrm_ref, inv_ref, glog_ref, up_ref, w_ref, gain_ref, pair_ref, vec,
):
    tiles, _, lanes = up_ref.shape
    cols = lanes // q
    load_columns(vec, (gain_ref, layer))
    for t in range(tiles):
        gproj = project_grad(left_ref, right_ref, fac_ref, glog_ref, t, cpd, q * cpd)
        upstream = up_ref[t] + input_grad(gproj, nrm_ref, inv_ref, t, w_ref, vec[0])
        for a in range(q):
            pair_ref[t * q + a] = upstream[:, a * cols : (a + 1) * cols].T.astype(BF16)


def spread_kernel(early_ref, late_ref, out_ref):
    early = jnp.sum(early_ref[...].astype(F32), 0).astype(BF16)
    late = jnp.sum(late_ref[...].astype(F32), 0).astype(BF16)
    out_ref[...] = jnp.broadcast_to(jnp.concatenate([early, late], 0)[None], out_ref.shape)


def unpack_kernel(factor, early_rows, got_ref, proj_ref, ow_ref, inorm_ref, hnorm_ref, chain_ref):
    width = ow_ref.shape[1]
    early = got_ref[:, :early_rows, :].astype(F32).reshape(-1, width) * factor
    late = got_ref[:, early_rows:, :].astype(F32).reshape(-1, width) * factor
    for n in range(5):
        rows, lanes = slice(n * width, (n + 1) * width), slice(n * width, (n + 1) * width)
        proj_ref[0, :, lanes] = late[rows]
        proj_ref[1, :, lanes] = early[rows]
    ow_ref[1] = early[5 * width : 6 * width]
    ow_ref[0] = early[6 * width : 7 * width]
    inorm_ref[0] = late[5 * width : 5 * width + 2]
    vectors = early[7 * width : 7 * width + 8]
    inorm_ref[1] = vectors[0:2]
    hnorm_ref[1] = vectors[2:4]
    hnorm_ref[0] = vectors[5:7]
    chain_ref[...] = jnp.concatenate([vectors[7:8], vectors[4:5]], 0)


def cell_call(kernel, steps, ins, outs, scratch, prefetch=(), flops=0, vmem=CELL_VMEM):
    def spec(shape, how):
        if how is None:
            return pl.BlockSpec(shape, lambda *s: (0,) * len(shape))
        axis, first, size = how if isinstance(how, tuple) else (how, 0, shape[how] // steps)
        block = tuple(size if n == axis else length for n, length in enumerate(shape))
        moves = shape[axis] >= size * steps
        return pl.BlockSpec(
            block,
            lambda *s: tuple((s[0] if moves else 0) + first if n == axis else 0 for n in range(len(shape))),
        )

    moved = sum(a.size * a.dtype.itemsize for a, _ in ins)
    moved += sum(functools.reduce(lambda x, y: x * y, s, 1) * jnp.dtype(t).itemsize for (s, t), _ in outs)
    return pl.pallas_call(
        kernel,
        grid_spec=pltpu.PrefetchScalarGridSpec(
            num_scalar_prefetch=len(prefetch),
            grid=(steps,),
            in_specs=[spec(a.shape, how) for a, how in ins],
            out_specs=[spec(s, how) for (s, _), how in outs],
            scratch_shapes=scratch,
        ),
        out_shape=[jax.ShapeDtypeStruct(s, t) for (s, t), _ in outs],
        compiler_params=pltpu.CompilerParams(vmem_limit_bytes=vmem),
        cost_estimate=pl.CostEstimate(flops=flops, bytes_accessed=int(moved), transcendentals=0),
    )(*prefetch, *[a for a, _ in ins])


def widen(src_ref, dst):
    devices, cols = src_ref.shape[0], src_ref.shape[-1]
    per = dst.shape[0] // devices
    for d in range(devices):
        dst[d * per : (d + 1) * per, :] = src_ref[d].astype(F32).reshape(per, cols)


def narrow(src, dst_ref):
    devices = dst_ref.shape[0]
    per = src.shape[0] // devices
    for d in range(devices):
        dst_ref[d, :per, :] = src[d * per : (d + 1) * per, :].astype(BF16)


def get_channel(src, ch, sub, subs, dims):
    row_devs, col_devs, rows, cpd, cols = dims
    halves = []
    for s in range(col_devs):
        parts = []
        for r in range(row_devs):
            base = ((r * col_devs + s) * subs + sub) * rows * cpd
            parts.append(src[pl.ds(base + ch, rows, stride=cpd), :])
        halves.append(jnp.concatenate(parts, 0))
    return jnp.concatenate(halves, 1).astype(BF16)


def put_channel(dst, value, ch, sub, subs, dims):
    row_devs, col_devs, rows, cpd, cols = dims
    for s in range(col_devs):
        for r in range(row_devs):
            base = ((r * col_devs + s) * subs + sub) * rows * cpd
            dst[pl.ds(base + ch, rows, stride=cpd), :] = value[
                r * rows : (r + 1) * rows, s * cols : (s + 1) * cols
            ]


def product_kernel(dims, outgoing, edges_ref, out_ref, edges, result):
    widen(edges_ref, edges)
    for ch in range(dims[3]):
        left = get_channel(edges, ch, 0, 2, dims)
        right = get_channel(edges, ch, 1, 2, dims)
        value = dot(left, right, 1, 1) if outgoing else dot(left, right, 0, 0)
        put_channel(result, value, ch, 0, 1, dims)
    narrow(result, out_ref)


def assemble_kernel(dims, edges_ref, out_ref, edges):
    widen(edges_ref, edges)
    for ch in range(dims[3]):
        for sub in range(2):
            out_ref[ch, sub] = get_channel(edges, ch, sub, 2, dims)


def product_grad_kernel(dims, outgoing, sides_ref, grad_ref, *rest):
    out_ref, grad, result = rest[-3:]
    widen(grad_ref, grad)
    for ch in range(dims[3]):
        left, right = sides_ref[ch, 0], sides_ref[ch, 1]
        gp = get_channel(grad, ch, 0, 1, dims)
        if outgoing:
            grad_left = dot(gp, right, 1, 0)
            grad_right = dot(gp, left, 0, 0)
        else:
            grad_left = dot(right, gp, 1, 1)
            grad_right = dot(left, gp, 1, 0)
        put_channel(result, grad_left, ch, 0, 2, dims)
        put_channel(result, grad_right, ch, 1, 2, dims)
    narrow(result, out_ref)
    for terms_ref in rest[:-3]:
        out_ref[:, out_ref.shape[1] - terms_ref.shape[1] :, :] = terms_ref[...]


def whole_call(kernel, ins, outs, scratch, flops):
    moved = sum(a.size * a.dtype.itemsize for a in ins)
    moved += sum(functools.reduce(lambda x, y: x * y, s, 1) * jnp.dtype(t).itemsize for s, t in outs)
    specs = [pl.BlockSpec(memory_space=pltpu.VMEM)] * len(outs)
    shapes = [jax.ShapeDtypeStruct(s, t) for s, t in outs]
    return pl.pallas_call(
        kernel,
        in_specs=[pl.BlockSpec(memory_space=pltpu.VMEM)] * len(ins),
        out_specs=specs if len(outs) > 1 else specs[0],
        out_shape=shapes if len(outs) > 1 else shapes[0],
        scratch_shapes=scratch,
        compiler_params=pltpu.CompilerParams(vmem_limit_bytes=CHANNEL_VMEM),
        cost_estimate=pl.CostEstimate(flops=flops, bytes_accessed=int(moved), transcendentals=0),
    )(*ins)


def exchange(array):
    return lax.all_to_all(array, AXES, split_axis=0, concat_axis=0, tiled=True)


def after(array, *others):
    return lax.optimization_barrier((array, *others))[0]


def shards(
    pair_rep, cotangent, residue_mask, chain_ids, proj_weight, out_weight,
    input_gain, input_bias, hidden_gain, hidden_bias, chain_bias,
):
    rows, cols, width = pair_rep.shape
    hidden = out_weight.shape[1]
    row_devs, col_devs = lax.axis_size("row"), lax.axis_size("col")
    devices = row_devs * col_devs
    length = rows * row_devs
    cpd = hidden // devices
    q = max(1, 16 // cpd)
    tiles = rows // q
    lanes = q * cols
    steps = max(1, tiles // 4)
    dims = (row_devs, col_devs, rows, cpd, cols)
    side = rows * cpd

    starts = jnp.stack([lax.axis_index("row") * rows, lax.axis_index("col")]).astype(jnp.int32)
    wt = [proj_weight[n].T for n in range(2)]
    owt = [out_weight[n].T for n in range(2)]
    weight = [proj_weight[n] for n in range(2)]
    mixer = [out_weight[n] for n in range(2)]
    mask_cols, chain_cols = residue_mask.reshape(col_devs, cols), chain_ids.reshape(col_devs, cols)
    scalars = (residue_mask, chain_ids, starts)
    tile = (tiles, width, lanes)
    fac_tile = (tiles, 4 * hidden, lanes)
    edge_shape = (devices, 2, side, cols)
    cell_shape = (devices, side, cols)
    vec = lambda n: pltpu.VMEM((n, width, lanes), F32)
    acc = lambda n, m=width: pltpu.VMEM((m, n), F32)
    wide = lambda n: pltpu.VMEM((n * devices * side, cols), F32)
    cell_flops = 2 * rows * cols * width * hidden
    tri_flops = 2 * cpd * length**3
    rows_for = lambda n: -(-n // (devices * 16)) * 16
    early_rows, late_rows = rows_for(7 * hidden + 8), rows_for(5 * hidden + 2)
    terms_shape = (hidden + 8, hidden)

    def product(edges, outgoing):
        return whole_call(
            functools.partial(product_kernel, dims, outgoing), [edges], [(cell_shape, BF16)],
            [wide(2), wide(1)], tri_flops,
        )

    def assemble(edges):
        return whole_call(
            functools.partial(assemble_kernel, dims), [edges], [((cpd, 2, length, length), BF16)], [wide(2)], 0
        )

    def product_grad(sides, grad, outgoing, *terms):
        out_rows = 2 * side + sum(t.shape[1] for t in terms)
        return whole_call(
            functools.partial(product_grad_kernel, dims, outgoing), [sides, grad, *terms],
            [((devices, out_rows, cols), BF16)], [wide(1), wide(2)], 2 * tri_flops,
        )

    def halves(grads):
        per = side // steps
        return [(grads, (1, 0, per)), (grads, (1, steps, per))]

    def keep(layer, z, with_gate):
        norm_outs = [((tile, BF16), 0), ((tile, BF16), 0), (((tiles, 1, lanes), F32), 0)]
        return cell_call(
            functools.partial(keep_kernel, layer), steps,
            [
                (z, 0), (flags, 0), (wt[layer], None), (input_gain, None), (input_bias, None), (chain_bias, None),
            ],
            [((fac_tile, BF16), 0)] + norm_outs + [((tile, BF16), 0)] * with_gate,
            [vec(3)], flops=5 * cell_flops,
        )

    (edges0,) = cell_call(
        functools.partial(edge_first_kernel, cpd, q), steps,
        [
            (pair_rep, 0), (mask_cols, None), (chain_cols, None), (proj_weight, (0, 0, 1)),
            (input_gain, None), (input_bias, None),
        ],
        [((edge_shape, BF16), 2)], [vec(2), pltpu.VMEM((5 * hidden, width), BF16)],
        prefetch=scalars, flops=4 * cell_flops, vmem=ALL_VMEM,
    )
    got0 = exchange(edges0)
    z0, up, gate0, flags = cell_call(
        functools.partial(first_keep_kernel, q), steps,
        [
            (after(pair_rep, edges0), 0), (cotangent, 0), (mask_cols, None), (chain_cols, None), (wt[0], None),
            (input_gain, None), (input_bias, None), (chain_bias, None),
        ],
        [((tile, BF16), 0), ((tile, BF16), 0), ((tile, BF16), 0), (((tiles, 2, lanes), F32), 0)],
        [vec(3)], prefetch=scalars, flops=2 * cell_flops,
    )
    made0 = product(after(got0, z0), True)
    prod0 = exchange(made0)
    sides0 = assemble(after(got0, made0))
    edges1, z1 = cell_call(
        functools.partial(mix_edge_kernel, cpd, q, 0), steps,
        [
            (after(prod0, sides0), 1), (z0, 0), (gate0, 0), (flags, 0), (owt[0], None), (hidden_gain, None),
            (hidden_bias, None), (wt[1], None), (input_gain, None), (input_bias, None),
        ],
        [((edge_shape, BF16), 2), ((tile, F32), 0)], [vec(4)], flops=5 * cell_flops,
    )
    got1 = exchange(edges1)
    fac1, low1, nrm1, inv1, gate1 = keep(1, after(z1, edges1), True)
    made1 = product(after(got1, gate1), False)
    prod1 = exchange(made1)
    sides1 = assemble(after(got1, made1))

    (grad1,) = cell_call(
        functools.partial(mix_back_kernel, cpd, q, 1), steps,
        [(after(prod1, sides1), 1), (up, 0), (gate1, 0), (mixer[1], None), (hidden_gain, None)],
        [((cell_shape, BF16), 1)], [vec(1)], flops=cell_flops,
    )
    got_grad1 = exchange(grad1)
    hnrm0, hinv0 = cell_call(
        functools.partial(keep_product_kernel, cpd, q), steps, [(after(prod0, grad1), 1)],
        [((tile, BF16), 0), (((tiles, 1, lanes), F32), 0)], [],
    )
    made_grads1 = product_grad(sides1, after(got_grad1, hnrm0), False)
    grads1 = exchange(made_grads1)
    glog1, terms1 = cell_call(
        functools.partial(mix_terms_kernel, cpd, q, 1), steps,
        [
            (after(prod1, made_grads1), 1), (up, 0), (gate1, 0), (flags, 0), (mixer[1], None), (owt[1], None),
            (hidden_gain, None), (hidden_bias, None),
        ],
        [((tile, BF16), 0), ((terms_shape, F32), None)],
        [vec(2), acc(hidden), acc(cols), acc(cols), acc(cols)], flops=3 * cell_flops,
    )
    up0, grad0 = cell_call(
        functools.partial(edge_mix_back_kernel, cpd, q, 1), steps,
        halves(after(grads1, glog1))
        + [
            (fac1, 0), (nrm1, 0), (inv1, 0), (glog1, 0), (up, 0), (weight[1], None), (input_gain, None),
            (hnrm0, 0), (hinv0, 0), (gate0, 0), (mixer[0], None), (hidden_gain, None),
        ],
        [((tile, F32), 0), ((cell_shape, BF16), 1)],
        [vec(2)], flops=6 * cell_flops,
    )
    got_grad0 = exchange(grad0)
    glog0, early = cell_call(
        functools.partial(late_terms_kernel, cpd, q, 1), steps,
        halves(after(grads1, grad0))
        + [
            (fac1, 0), (low1, 0), (nrm1, 0), (glog1, 0), (weight[1], None), (terms1, None), (prod0, 1),
            (up0, 0), (gate0, 0), (flags, 0), (mixer[0], None), (owt[0], None), (hidden_gain, None),
            (hidden_bias, None),
        ],
        [((tile, BF16), 0), (((devices * early_rows, hidden), BF16), None)],
        [vec(2), acc(5 * hidden, 2 * width + 16), acc(hidden), acc(cols), acc(cols), acc(cols)],
        flops=13 * cell_flops,
    )

    made_grads0 = product_grad(sides0, got_grad0, True, early.reshape(devices, early_rows, hidden))
    grads0 = exchange(made_grads0)
    fac0, low0, nrm0, inv0 = keep(0, after(z0, made_grads0), False)
    grads0 = after(grads0, nrm0)
    (late,) = cell_call(
        functools.partial(last_terms_kernel, cpd, q), steps,
        halves(grads0) + [(fac0, 0), (low0, 0), (nrm0, 0), (glog0, 0), (weight[0], None)],
        [(((devices * late_rows, hidden), BF16), None)],
        [acc(5 * hidden, 2 * width + 16)], flops=10 * cell_flops, vmem=ALL_VMEM,
    )
    got_late = exchange(late.reshape(devices, late_rows, hidden))
    (grad_pair,) = cell_call(
        functools.partial(pair_grad_kernel, cpd, q, 0), steps,
        halves(after(grads0, late))
        + [(fac0, 0), (nrm0, 0), (inv0, 0), (glog0, 0), (up0, 0), (weight[0], None), (input_gain, None)],
        [((pair_rep.shape, BF16), 0)], [vec(1)], flops=5 * cell_flops, vmem=ALL_VMEM,
    )
    (spread,) = cell_call(
        spread_kernel, 1,
        [(grads0, (1, 2 * side // early_rows, early_rows)), (after(got_late, grad_pair), None)],
        [(((devices, early_rows + late_rows, hidden), BF16), None)], [], vmem=ALL_VMEM,
    )
    proj, out, inorm, hnorm, chain = whole_call(
        functools.partial(unpack_kernel, 1.0 / length, early_rows), [exchange(spread)],
        [
            ((2, width, 5 * hidden), F32), ((2, hidden, hidden), F32), ((2, 2, hidden), F32),
            ((2, 2, hidden), F32), ((2, hidden), F32),
        ],
        [], 0,
    )
    return grad_pair, proj, out, inorm, hnorm, chain


def solution(mesh):
    cells = P(("grp", "row"), "col", None)
    return jax.shard_map(
        shards,
        mesh=mesh,
        in_specs=(cells, cells, P("grp"), P("grp")) + (P(),) * 7,
        out_specs=(
            cells, P("grp", None, None), P("grp", None, None), P("grp", None, None),
            P("grp", None, None), P("grp", None),
        ),
        check_vma=False,
    )
```

```python
import functools

import jax
import jax.numpy as jnp
from jax import lax
from jax.experimental import pallas as pl
from jax.experimental.pallas import tpu as pltpu
from jax.sharding import PartitionSpec as P

EPSILON = 1e-05
AXES = ("row", "col")
F32 = jnp.float32
BF16 = jnp.bfloat16
CHANNEL_VMEM = 24 * 1024 * 1024
CELL_VMEM = 30 * 1024 * 1024
LOOP_VMEM = 32 * 1024 * 1024
ALL_VMEM = 60 * 1024 * 1024


def dot(a, b, ca, cb):
    return lax.dot_general(a, b, (((ca,), (cb,)), ((), ())), preferred_element_type=F32)


def sigmoid(x):
    return 0.5 * jnp.tanh(0.5 * x) + 0.5


def columns(vectors, width):
    c = vectors.shape[1]
    square = jnp.broadcast_to(vectors, (c, c)).T
    return jnp.concatenate([square] * (width // c), 1)


def norm(x):
    centred = x - jnp.mean(x, 0, keepdims=True)
    inv = lax.rsqrt(jnp.mean(centred * centred, 0, keepdims=True) + EPSILON)
    return centred * inv, inv


def norm_grad(grad_scaled, normed, inv, gain):
    g = grad_scaled * gain
    first = jnp.mean(g, 0, keepdims=True)
    second = jnp.mean(g * normed, 0, keepdims=True)
    return (g - first - normed * second) * inv


def unpack(block, cpd):
    devices, rows, cols = block.shape
    values = block.astype(F32)
    parts = []
    for a in range(rows // cpd):
        if cpd % 8 == 0:
            parts.append(values[:, a * cpd : (a + 1) * cpd, :].reshape(devices * cpd, cols))
        else:
            parts.append(
                jnp.concatenate([values[d, a * cpd : (a + 1) * cpd, :] for d in range(devices)], 0)
            )
    return jnp.concatenate(parts, 1)


def pack(tile, cpd, cols):
    channels, lanes = tile.shape
    devices = channels // cpd
    parts = [tile[:, a * cols : (a + 1) * cols] for a in range(lanes // cols)]
    if cpd % 8 == 0:
        return jnp.concatenate([p.reshape(devices, cpd, cols) for p in parts], 1).astype(BF16)
    return jnp.stack(
        [
            jnp.concatenate([p[d * cpd : (d + 1) * cpd, :] for p in parts], 0)
            for d in range(devices)
        ]
    ).astype(BF16)


def fold(tile, width):
    return sum(tile[:, a : a + width] for a in range(0, tile.shape[1], width))


def project(lowered, wt_ref, first, last):
    hidden = wt_ref.shape[0] // 5
    projected = dot(wt_ref[first * hidden : last * hidden, :], lowered, 1, 0)
    return [projected[n * hidden : (n + 1) * hidden] for n in range(last - first)]


def lower(cells, gain, bias):
    normed, inv = norm(cells)
    return normed, inv, (normed * gain + bias).astype(BF16)


def emit_edges(edges_ref, here, cells, wt_ref, gain, bias, mask, cpd, cols):
    part = project(lower(cells, gain, bias)[2], wt_ref, 0, 4)
    edges_ref[:, 0, here, :] = pack(part[0] * sigmoid(part[1]) * mask, cpd, cols)
    edges_ref[:, 1, here, :] = pack(part[2] * sigmoid(part[3]) * mask, cpd, cols)


STEP = []


def step_now():
    return STEP[-1] if STEP else (pl.program_id(0), pl.num_programs(0))


def first_step(fill):
    pl.when(step_now()[0] == 0)(fill)


def last_step(fill):
    index, count = step_now()
    pl.when(index == count - 1)(fill)


def looped_kernel(kernel, steps, hows, *refs):
    @pl.loop(0, steps)
    def _(step):
        views = []
        for ref, how in zip(refs, hows):
            if how is None:
                views.append(ref)
                continue
            axis, first, size = how
            here = pl.ds(pl.multiple_of((step + first) * size, size), size)
            views.append(ref.at[tuple(here if n == axis else slice(None) for n in range(axis + 1))])
        STEP.append((step, steps))
        kernel(*views, *refs[len(hows) :])
        STEP.pop()


def load_columns(vec, *rows):
    @first_step
    def _():
        for n, (ref, layer) in enumerate(rows):
            vec[n] = columns(ref[layer : layer + 1, :], vec.shape[2])


def clear(*accs):
    @first_step
    def _():
        for acc in accs:
            acc[...] = jnp.zeros_like(acc)


def turned(ref, t, q):
    return jnp.concatenate([ref[t * q + a].astype(F32).T for a in range(q)], 1)


def row_flags(row, mask_smem, chain_smem, start_smem, maskc_ref, chainc_ref):
    whole = start_smem[0] + row
    here = pl.ds(start_smem[1], 1)
    mask = (maskc_ref[here, :] * mask_smem[whole]).astype(F32)
    return mask, (chainc_ref[here, :] == chain_smem[whole]).astype(F32)


def edge_first_kernel(
    cpd, q, mask_smem, chain_smem, start_smem, pair_ref, maskc_ref, chainc_ref, w_ref, gain_ref, bias_ref,
    edges_ref, vec, turned_weight,
):
    rows, cols, width = pair_ref.shape
    load_columns(vec, (gain_ref, 0), (bias_ref, 0))

    @first_step
    def _():
        for n in range(turned_weight.shape[0] // width):
            block = slice(n * width, (n + 1) * width)
            turned_weight[block, :] = w_ref[0, :, block].astype(F32).T.astype(BF16)

    for t in range(rows // q):
        first = pl.program_id(0) * rows + t * q
        mask = jnp.concatenate(
            [
                row_flags(first + a, mask_smem, chain_smem, start_smem, maskc_ref, chainc_ref)[0]
                for a in range(q)
            ],
            1,
        )
        here = slice(t * q * cpd, (t + 1) * q * cpd)
        emit_edges(edges_ref, here, turned(pair_ref, t, q), turned_weight, vec[0], vec[1], mask, cpd, cols)


def first_keep_kernel(
    q, mask_smem, chain_smem, start_smem, pair_ref, cot_ref, maskc_ref, chainc_ref, wt_ref, gain_ref,
    bias_ref, chain_ref, z_ref, up_ref, gate_ref, flags_ref, vec,
):
    load_columns(vec, (gain_ref, 0), (bias_ref, 0), (chain_ref, 0))
    tiles = z_ref.shape[0]
    for t in range(tiles):
        flags = [
            row_flags(
                (pl.program_id(0) * tiles + t) * q + a, mask_smem, chain_smem, start_smem, maskc_ref, chainc_ref
            )
            for a in range(q)
        ]
        mask = jnp.concatenate([f[0] for f in flags], 1)
        same = jnp.concatenate([f[1] for f in flags], 1)
        cells = turned(pair_ref, t, q)
        z_ref[t] = cells.astype(BF16)
        up_ref[t] = turned(cot_ref, t, q).astype(BF16)
        flags_ref[t] = jnp.concatenate([mask, same], 0)
        (logits,) = project(lower(cells, vec[0], vec[1])[2], wt_ref, 4, 5)
        gate_ref[t] = sigmoid(logits + same * vec[2]).astype(BF16)


def keep_kernel(layer, z_ref, flags_ref, wt_ref, gain_ref, bias_ref, chain_ref, fac_ref, low_ref, nrm_ref, inv_ref, *rest):
    vec = rest[-1]
    hidden = wt_ref.shape[0] // 5
    load_columns(vec, (gain_ref, layer), (bias_ref, layer), (chain_ref, layer))
    for t in range(z_ref.shape[0]):
        mask, same = flags_ref[t, 0:1, :], flags_ref[t, 1:2, :]
        normed, inv_ref[t], lowered = lower(z_ref[t].astype(F32), vec[0], vec[1])
        low_ref[t] = lowered
        nrm_ref[t] = normed.astype(BF16)
        part = project(lowered, wt_ref, 0, 3 + len(rest))
        for n in (0, 2):
            sig = sigmoid(part[n + 1]) * mask
            fac_ref[t, n * hidden : (n + 1) * hidden, :] = sig.astype(BF16)
            fac_ref[t, (n + 1) * hidden : (n + 2) * hidden, :] = (
                part[n] * sig * (1.0 - sig)
            ).astype(BF16)
        for gate_ref in rest[:-1]:
            gate_ref[t] = sigmoid(part[4] + same * vec[2]).astype(BF16)


def keep_product_kernel(cpd, q, prod_ref, nrm_ref, inv_ref):
    rows = q * cpd
    for t in range(nrm_ref.shape[0]):
        normed, inv_ref[t] = norm(unpack(prod_ref[:, t * rows : (t + 1) * rows, :], cpd))
        nrm_ref[t] = normed.astype(BF16)


def mix_edge_kernel(
    cpd, q, layer, prod_ref, z_ref, gate_ref, flags_ref, owt_ref, hgain_ref, hbias_ref, wt_ref,
    gain_ref, bias_ref, edges_ref, znext_ref, vec,
):
    tiles, _, lanes = z_ref.shape
    rows = q * cpd
    load_columns(vec, (hgain_ref, layer), (hbias_ref, layer), (gain_ref, layer + 1), (bias_ref, layer + 1))
    for t in range(tiles):
        here = slice(t * rows, (t + 1) * rows)
        hnormed, _ = norm(unpack(prod_ref[:, here, :], cpd))
        hscaled = (hnormed * vec[0] + vec[1]).astype(BF16)
        cells = z_ref[t].astype(F32) + gate_ref[t].astype(F32) * dot(owt_ref[...], hscaled, 1, 0)
        znext_ref[t] = cells
        emit_edges(
            edges_ref, here, cells, wt_ref, vec[2], vec[3], flags_ref[t, 0:1, :], cpd, lanes // q
        )


def mix_grad(upstream, hnormed, hinv, gate_ref, t, ow_ref, hgain):
    grad_mixed = (upstream * gate_ref[t].astype(F32)).astype(BF16)
    return norm_grad(dot(ow_ref[...], grad_mixed, 1, 0), hnormed, hinv, hgain)


def mix_back_kernel(cpd, q, layer, prod_ref, up_ref, gate_ref, ow_ref, hgain_ref, gp_ref, vec):
    tiles, _, lanes = up_ref.shape
    rows = q * cpd
    load_columns(vec, (hgain_ref, layer))
    for t in range(tiles):
        here = slice(t * rows, (t + 1) * rows)
        hnormed, hinv = norm(unpack(prod_ref[:, here, :], cpd))
        grad = mix_grad(up_ref[t].astype(F32), hnormed, hinv, gate_ref, t, ow_ref, vec[0])
        gp_ref[:, here, :] = pack(grad, cpd, lanes // q)


def mix_terms(upstream, product, gate, same, ow_ref, owt_ref, hgain, hbias, acc_ow, acc_hg, acc_hb, acc_ch):
    width = acc_hg.shape[1]
    hnormed, _ = norm(product)
    hscaled = (hnormed * hgain + hbias).astype(BF16)
    mixed = dot(owt_ref[...], hscaled, 1, 0)
    grad_gate = upstream * gate
    grad_logits = grad_gate * mixed * (1.0 - gate)
    grad_mixed = grad_gate.astype(BF16)
    acc_ow[...] += dot(hscaled, grad_mixed, 1, 1)
    grad_hscaled = dot(ow_ref[...], grad_mixed, 1, 0)
    acc_hg[...] += fold(grad_hscaled * hnormed, width)
    acc_hb[...] += fold(grad_hscaled, width)
    acc_ch[...] += fold(grad_logits * same, width)
    return grad_logits


def row_of(acc):
    return jnp.sum(acc.T, 0, keepdims=True)


def mix_terms_kernel(
    cpd, q, layer, prod_ref, up_ref, gate_ref, flags_ref, ow_ref, owt_ref, hgain_ref, hbias_ref,
    glog_ref, terms_ref, vec, acc_ow, acc_hg, acc_hb, acc_ch,
):
    rows = q * cpd
    load_columns(vec, (hgain_ref, layer), (hbias_ref, layer))
    clear(acc_ow, acc_hg, acc_hb, acc_ch)
    for t in range(up_ref.shape[0]):
        grad_logits = mix_terms(
            up_ref[t].astype(F32), unpack(prod_ref[:, t * rows : (t + 1) * rows, :], cpd),
            gate_ref[t].astype(F32), flags_ref[t, 1:2, :], ow_ref, owt_ref, vec[0], vec[1],
            acc_ow, acc_hg, acc_hb, acc_ch,
        )
        glog_ref[t] = grad_logits.astype(BF16)

    @last_step
    def _():
        hidden = acc_ow.shape[0]
        terms_ref[:hidden, :] = acc_ow[...]
        vectors = [row_of(acc_hg[...]), row_of(acc_hb[...]), row_of(acc_ch[...])]
        vectors.append(jnp.zeros((terms_ref.shape[0] - hidden - 3, hidden), F32))
        terms_ref[hidden:, :] = jnp.concatenate(vectors, 0)


def project_grad(left_ref, right_ref, fac_ref, glog_ref, t, cpd, rows):
    hidden = fac_ref.shape[1] // 4
    here = slice(t * rows, (t + 1) * rows)
    grads = (unpack(left_ref[:, here, :], cpd), unpack(right_ref[:, here, :], cpd))
    blocks = [
        (grads[n // 2] * fac_ref[t, n * hidden : (n + 1) * hidden, :].astype(F32)).astype(BF16)
        for n in range(4)
    ]
    return jnp.concatenate(blocks + [glog_ref[t]], 0)


def input_grad(gproj, nrm_ref, inv_ref, t, w_ref, gain):
    return norm_grad(dot(w_ref[...], gproj, 1, 0), nrm_ref[t].astype(F32), inv_ref[t], gain)


def edge_mix_back_kernel(
    cpd, q, layer, left_ref, right_ref, fac_ref, nrm_ref, inv_ref, glog_ref, up_ref, w_ref, gain_ref,
    hnrm_ref, hinv_ref, gate_ref, ow_ref, hgain_ref, upnext_ref, gp_ref, vec,
):
    tiles, _, lanes = up_ref.shape
    rows = q * cpd
    load_columns(vec, (gain_ref, layer), (hgain_ref, layer - 1))
    for t in range(tiles):
        gproj = project_grad(left_ref, right_ref, fac_ref, glog_ref, t, cpd, rows)
        upstream = up_ref[t].astype(F32) + input_grad(gproj, nrm_ref, inv_ref, t, w_ref, vec[0])
        upnext_ref[t] = upstream
        grad = mix_grad(upstream, hnrm_ref[t].astype(F32), hinv_ref[t], gate_ref, t, ow_ref, vec[1])
        gp_ref[:, t * rows : (t + 1) * rows, :] = pack(grad, cpd, lanes // q)


def edge_terms(gproj, low_ref, nrm_ref, t, acc_w):
    ones = jnp.ones((16, gproj.shape[1]), BF16)
    acc_w[...] += dot(jnp.concatenate([low_ref[t], nrm_ref[t], ones], 0), gproj, 1, 1)


def finish_edge(out_ref, acc_w, w_ref):
    width = w_ref.shape[0]
    for n in range(acc_w.shape[1] // width):
        out_ref[n * width : (n + 1) * width, :] = acc_w[:width, n * width : (n + 1) * width].astype(BF16)
    weight = w_ref[...].astype(F32)
    gain = row_of(fold(weight * acc_w[width : 2 * width, :], width))
    bias = row_of(fold(weight * acc_w[2 * width : 2 * width + 1, :], width))
    return [gain, bias]


def finish_rows(out_ref, first, vectors):
    pad = jnp.zeros((out_ref.shape[0] - first - sum(v.shape[0] for v in vectors), out_ref.shape[1]), F32)
    out_ref[first:, :] = jnp.concatenate(vectors + [pad], 0).astype(BF16)


def late_terms_kernel(
    cpd, q, layer, left_ref, right_ref, fac_ref, low_ref, nrm_ref, glog_ref, w_ref, terms_ref,
    prod_ref, up_ref, gate_ref, flags_ref, ow_ref, owt_ref, hgain_ref, hbias_ref,
    glognext_ref, all_ref, vec, acc_w, acc_ow, acc_hg, acc_hb, acc_ch,
):
    rows = q * cpd
    load_columns(vec, (hgain_ref, layer - 1), (hbias_ref, layer - 1))
    clear(acc_w, acc_ow, acc_hg, acc_hb, acc_ch)
    for t in range(up_ref.shape[0]):
        gproj = project_grad(left_ref, right_ref, fac_ref, glog_ref, t, cpd, rows)
        edge_terms(gproj, low_ref, nrm_ref, t, acc_w)
        grad_logits = mix_terms(
            up_ref[t], unpack(prod_ref[:, t * rows : (t + 1) * rows, :], cpd), gate_ref[t].astype(F32),
            flags_ref[t, 1:2, :], ow_ref, owt_ref, vec[0], vec[1], acc_ow, acc_hg, acc_hb, acc_ch,
        )
        glognext_ref[t] = grad_logits.astype(BF16)

    @last_step
    def _():
        hidden = acc_ow.shape[0]
        vectors = finish_edge(all_ref, acc_w, w_ref)
        all_ref[5 * hidden : 6 * hidden, :] = terms_ref[:hidden, :].astype(BF16)
        all_ref[6 * hidden : 7 * hidden, :] = acc_ow[...].astype(BF16)
        vectors += [terms_ref[hidden : hidden + 3, :]]
        vectors += [row_of(acc_hg[...]), row_of(acc_hb[...]), row_of(acc_ch[...])]
        finish_rows(all_ref, 7 * hidden, vectors)


def last_terms_kernel(
    cpd, q, left_ref, right_ref, fac_ref, low_ref, nrm_ref, glog_ref, w_ref, all_ref, acc_w,
):
    clear(acc_w)
    tiles = range(low_ref.shape[0])
    gproj = [project_grad(left_ref, right_ref, fac_ref, glog_ref, t, cpd, q * cpd) for t in tiles]
    ones = jnp.ones((16, low_ref.shape[2]), BF16)
    sides = [jnp.concatenate([low_ref[t], nrm_ref[t], ones], 0) for t in tiles]
    acc_w[...] += dot(jnp.concatenate(sides, 1), jnp.concatenate(gproj, 1), 1, 1)

    @last_step
    def _():
        finish_rows(all_ref, acc_w.shape[1], finish_edge(all_ref, acc_w, w_ref))


def pair_grad_kernel(
    cpd, q, layer, left_ref, right_ref, fac_ref, nrm_ref, inv_ref, glog_ref, up_ref, w_ref, gain_ref, pair_ref, vec,
):
    tiles, _, lanes = up_ref.shape
    cols = lanes // q
    load_columns(vec, (gain_ref, layer))
    for t in range(tiles):
        gproj = project_grad(left_ref, right_ref, fac_ref, glog_ref, t, cpd, q * cpd)
        upstream = up_ref[t] + input_grad(gproj, nrm_ref, inv_ref, t, w_ref, vec[0])
        for a in range(q):
            pair_ref[t * q + a] = upstream[:, a * cols : (a + 1) * cols].T.astype(BF16)


def spread_kernel(early_ref, late_ref, out_ref):
    early = jnp.sum(early_ref[...].astype(F32), 0).astype(BF16)
    late = jnp.sum(late_ref[...].astype(F32), 0).astype(BF16)
    out_ref[...] = jnp.broadcast_to(jnp.concatenate([early, late], 0)[None], out_ref.shape)


def unpack_kernel(factor, early_rows, got_ref, proj_ref, ow_ref, inorm_ref, hnorm_ref, chain_ref):
    width = ow_ref.shape[1]
    early = got_ref[:, :early_rows, :].astype(F32).reshape(-1, width) * factor
    late = got_ref[:, early_rows:, :].astype(F32).reshape(-1, width) * factor
    for n in range(5):
        rows, lanes = slice(n * width, (n + 1) * width), slice(n * width, (n + 1) * width)
        proj_ref[0, :, lanes] = late[rows]
        proj_ref[1, :, lanes] = early[rows]
    ow_ref[1] = early[5 * width : 6 * width]
    ow_ref[0] = early[6 * width : 7 * width]
    inorm_ref[0] = late[5 * width : 5 * width + 2]
    vectors = early[7 * width : 7 * width + 8]
    inorm_ref[1] = vectors[0:2]
    hnorm_ref[1] = vectors[2:4]
    hnorm_ref[0] = vectors[5:7]
    chain_ref[...] = jnp.concatenate([vectors[7:8], vectors[4:5]], 0)


def cell_call(kernel, steps, ins, outs, scratch, prefetch=(), flops=0, vmem=CELL_VMEM):
    def spec(shape, how):
        if how is None:
            return pl.BlockSpec(shape, lambda *s: (0,) * len(shape))
        axis, first, size = how if isinstance(how, tuple) else (how, 0, shape[how] // steps)
        block = tuple(size if n == axis else length for n, length in enumerate(shape))
        moves = shape[axis] >= size * steps
        return pl.BlockSpec(
            block,
            lambda *s: tuple((s[0] if moves else 0) + first if n == axis else 0 for n in range(len(shape))),
        )

    moved = sum(a.size * a.dtype.itemsize for a, _ in ins)
    moved += sum(functools.reduce(lambda x, y: x * y, s, 1) * jnp.dtype(t).itemsize for (s, t), _ in outs)
    return pl.pallas_call(
        kernel,
        grid_spec=pltpu.PrefetchScalarGridSpec(
            num_scalar_prefetch=len(prefetch),
            grid=(steps,),
            in_specs=[spec(a.shape, how) for a, how in ins],
            out_specs=[spec(s, how) for (s, _), how in outs],
            scratch_shapes=scratch,
        ),
        out_shape=[jax.ShapeDtypeStruct(s, t) for (s, t), _ in outs],
        compiler_params=pltpu.CompilerParams(vmem_limit_bytes=vmem),
        cost_estimate=pl.CostEstimate(flops=flops, bytes_accessed=int(moved), transcendentals=0),
    )(*prefetch, *[a for a, _ in ins])


def widen(src_ref, dst):
    devices, cols = src_ref.shape[0], src_ref.shape[-1]
    per = dst.shape[0] // devices
    for d in range(devices):
        dst[d * per : (d + 1) * per, :] = src_ref[d].astype(F32).reshape(per, cols)


def narrow(src, dst_ref):
    devices = dst_ref.shape[0]
    per = src.shape[0] // devices
    for d in range(devices):
        dst_ref[d, :per, :] = src[d * per : (d + 1) * per, :].astype(BF16)


def get_channel(src, ch, sub, subs, dims):
    row_devs, col_devs, rows, cpd, cols = dims
    halves = []
    for s in range(col_devs):
        parts = []
        for r in range(row_devs):
            base = ((r * col_devs + s) * subs + sub) * rows * cpd
            parts.append(src[pl.ds(base + ch, rows, stride=cpd), :])
        halves.append(jnp.concatenate(parts, 0))
    return jnp.concatenate(halves, 1).astype(BF16)


def put_channel(dst, value, ch, sub, subs, dims):
    row_devs, col_devs, rows, cpd, cols = dims
    for s in range(col_devs):
        for r in range(row_devs):
            base = ((r * col_devs + s) * subs + sub) * rows * cpd
            dst[pl.ds(base + ch, rows, stride=cpd), :] = value[
                r * rows : (r + 1) * rows, s * cols : (s + 1) * cols
            ]


def product_kernel(dims, outgoing, edges_ref, out_ref, edges, result):
    widen(edges_ref, edges)
    for ch in range(dims[3]):
        left = get_channel(edges, ch, 0, 2, dims)
        right = get_channel(edges, ch, 1, 2, dims)
        value = dot(left, right, 1, 1) if outgoing else dot(left, right, 0, 0)
        put_channel(result, value, ch, 0, 1, dims)
    narrow(result, out_ref)


def assemble_kernel(dims, edges_ref, out_ref, edges):
    widen(edges_ref, edges)
    for ch in range(dims[3]):
        for sub in range(2):
            out_ref[ch, sub] = get_channel(edges, ch, sub, 2, dims)


def product_grad_kernel(dims, outgoing, sides_ref, grad_ref, *rest):
    out_ref, grad, result = rest[-3:]
    widen(grad_ref, grad)
    for ch in range(dims[3]):
        left, right = sides_ref[ch, 0], sides_ref[ch, 1]
        gp = get_channel(grad, ch, 0, 1, dims)
        if outgoing:
            grad_left = dot(gp, right, 1, 0)
            grad_right = dot(gp, left, 0, 0)
        else:
            grad_left = dot(right, gp, 1, 1)
            grad_right = dot(left, gp, 1, 0)
        put_channel(result, grad_left, ch, 0, 2, dims)
        put_channel(result, grad_right, ch, 1, 2, dims)
    narrow(result, out_ref)
    for terms_ref in rest[:-3]:
        out_ref[:, out_ref.shape[1] - terms_ref.shape[1] :, :] = terms_ref[...]


def loop_call(kernel, steps, ins, outs, scratch, flops=0):
    def part(shape, how):
        return how if how is None or isinstance(how, tuple) else (how, 0, shape[how] // steps)

    hows = [part(a.shape, how) for a, how in ins] + [part(shape, how) for (shape, _), how in outs]
    made = whole_call(
        functools.partial(looped_kernel, kernel, steps, hows), [a for a, _ in ins], [o for o, _ in outs],
        scratch, flops, LOOP_VMEM,
    )
    return made if len(outs) > 1 else (made,)


def whole_call(kernel, ins, outs, scratch, flops, vmem=None):
    moved = sum(a.size * a.dtype.itemsize for a in ins)
    moved += sum(functools.reduce(lambda x, y: x * y, s, 1) * jnp.dtype(t).itemsize for s, t in outs)
    specs = [pl.BlockSpec(memory_space=pltpu.VMEM)] * len(outs)
    shapes = [jax.ShapeDtypeStruct(s, t) for s, t in outs]
    return pl.pallas_call(
        kernel,
        in_specs=[pl.BlockSpec(memory_space=pltpu.VMEM)] * len(ins),
        out_specs=specs if len(outs) > 1 else specs[0],
        out_shape=shapes if len(outs) > 1 else shapes[0],
        scratch_shapes=scratch,
        compiler_params=pltpu.CompilerParams(vmem_limit_bytes=vmem or CHANNEL_VMEM),
        cost_estimate=pl.CostEstimate(flops=flops, bytes_accessed=int(moved), transcendentals=0),
    )(*ins)


def exchange(array):
    return lax.all_to_all(array, AXES, split_axis=0, concat_axis=0, tiled=True)


def after(array, *others):
    return lax.optimization_barrier((array, *others))[0]


def shards(
    pair_rep, cotangent, residue_mask, chain_ids, proj_weight, out_weight,
    input_gain, input_bias, hidden_gain, hidden_bias, chain_bias,
):
    rows, cols, width = pair_rep.shape
    hidden = out_weight.shape[1]
    row_devs, col_devs = lax.axis_size("row"), lax.axis_size("col")
    devices = row_devs * col_devs
    length = rows * row_devs
    cpd = hidden // devices
    q = max(1, 16 // cpd)
    tiles = rows // q
    lanes = q * cols
    steps = max(1, tiles // 4)
    dims = (row_devs, col_devs, rows, cpd, cols)
    side = rows * cpd

    starts = jnp.stack([lax.axis_index("row") * rows, lax.axis_index("col")]).astype(jnp.int32)
    wt = [proj_weight[n].T for n in range(2)]
    owt = [out_weight[n].T for n in range(2)]
    weight = [proj_weight[n] for n in range(2)]
    mixer = [out_weight[n] for n in range(2)]
    mask_cols, chain_cols = residue_mask.reshape(col_devs, cols), chain_ids.reshape(col_devs, cols)
    scalars = (residue_mask, chain_ids, starts)
    tile = (tiles, width, lanes)
    fac_tile = (tiles, 4 * hidden, lanes)
    edge_shape = (devices, 2, side, cols)
    cell_shape = (devices, side, cols)
    vec = lambda n: pltpu.VMEM((n, width, lanes), F32)
    acc = lambda n, m=width: pltpu.VMEM((m, n), F32)
    wide = lambda n: pltpu.VMEM((n * devices * side, cols), F32)
    cell_flops = 2 * rows * cols * width * hidden
    tri_flops = 2 * cpd * length**3
    rows_for = lambda n: -(-n // (devices * 16)) * 16
    early_rows, late_rows = rows_for(7 * hidden + 8), rows_for(5 * hidden + 2)
    terms_shape = (hidden + 8, hidden)

    def product(edges, outgoing):
        return whole_call(
            functools.partial(product_kernel, dims, outgoing), [edges], [(cell_shape, BF16)],
            [wide(2), wide(1)], tri_flops,
        )

    def assemble(edges):
        return whole_call(
            functools.partial(assemble_kernel, dims), [edges], [((cpd, 2, length, length), BF16)], [wide(2)], 0
        )

    def product_grad(sides, grad, outgoing, *terms):
        out_rows = 2 * side + sum(t.shape[1] for t in terms)
        return whole_call(
            functools.partial(product_grad_kernel, dims, outgoing), [sides, grad, *terms],
            [((devices, out_rows, cols), BF16)], [wide(1), wide(2)], 2 * tri_flops,
        )

    def halves(grads):
        per = side // steps
        return [(grads, (1, 0, per)), (grads, (1, steps, per))]

    def keep(layer, z, with_gate):
        norm_outs = [((tile, BF16), 0), ((tile, BF16), 0), (((tiles, 1, lanes), F32), 0)]
        return cell_call(
            functools.partial(keep_kernel, layer), steps,
            [
                (z, 0), (flags, 0), (wt[layer], None), (input_gain, None), (input_bias, None), (chain_bias, None),
            ],
            [((fac_tile, BF16), 0)] + norm_outs + [((tile, BF16), 0)] * with_gate,
            [vec(3)], flops=5 * cell_flops,
        )

    (edges0,) = cell_call(
        functools.partial(edge_first_kernel, cpd, q), steps,
        [
            (pair_rep, 0), (mask_cols, None), (chain_cols, None), (proj_weight, (0, 0, 1)),
            (input_gain, None), (input_bias, None),
        ],
        [((edge_shape, BF16), 2)], [vec(2), pltpu.VMEM((5 * hidden, width), BF16)],
        prefetch=scalars, flops=4 * cell_flops, vmem=ALL_VMEM,
    )
    got0 = exchange(edges0)
    z0, up, gate0, flags = cell_call(
        functools.partial(first_keep_kernel, q), steps,
        [
            (after(pair_rep, edges0), 0), (cotangent, 0), (mask_cols, None), (chain_cols, None), (wt[0], None),
            (input_gain, None), (input_bias, None), (chain_bias, None),
        ],
        [((tile, BF16), 0), ((tile, BF16), 0), ((tile, BF16), 0), (((tiles, 2, lanes), F32), 0)],
        [vec(3)], prefetch=scalars, flops=2 * cell_flops,
    )
    made0 = product(after(got0, z0), True)
    prod0 = exchange(made0)
    sides0 = assemble(after(got0, made0))
    edges1, z1 = loop_call(
        functools.partial(mix_edge_kernel, cpd, q, 0), steps,
        [
            (after(prod0, sides0), 1), (z0, 0), (gate0, 0), (flags, 0), (owt[0], None), (hidden_gain, None),
            (hidden_bias, None), (wt[1], None), (input_gain, None), (input_bias, None),
        ],
        [((edge_shape, BF16), 2), ((tile, F32), 0)], [vec(4)], flops=5 * cell_flops,
    )
    got1 = exchange(edges1)
    fac1, low1, nrm1, inv1, gate1 = keep(1, after(z1, edges1), True)
    made1 = product(after(got1, gate1), False)
    prod1 = exchange(made1)
    sides1 = assemble(after(got1, made1))

    (grad1,) = loop_call(
        functools.partial(mix_back_kernel, cpd, q, 1), steps,
        [(after(prod1, sides1), 1), (up, 0), (gate1, 0), (mixer[1], None), (hidden_gain, None)],
        [((cell_shape, BF16), 1)], [vec(1)], flops=cell_flops,
    )
    got_grad1 = exchange(grad1)
    hnrm0, hinv0 = cell_call(
        functools.partial(keep_product_kernel, cpd, q), steps, [(after(prod0, grad1), 1)],
        [((tile, BF16), 0), (((tiles, 1, lanes), F32), 0)], [],
    )
    made_grads1 = product_grad(sides1, after(got_grad1, hnrm0), False)
    grads1 = exchange(made_grads1)
    glog1, terms1 = cell_call(
        functools.partial(mix_terms_kernel, cpd, q, 1), steps,
        [
            (after(prod1, made_grads1), 1), (up, 0), (gate1, 0), (flags, 0), (mixer[1], None), (owt[1], None),
            (hidden_gain, None), (hidden_bias, None),
        ],
        [((tile, BF16), 0), ((terms_shape, F32), None)],
        [vec(2), acc(hidden), acc(cols), acc(cols), acc(cols)], flops=3 * cell_flops,
    )
    up0, grad0 = loop_call(
        functools.partial(edge_mix_back_kernel, cpd, q, 1), steps,
        halves(after(grads1, glog1))
        + [
            (fac1, 0), (nrm1, 0), (inv1, 0), (glog1, 0), (up, 0), (weight[1], None), (input_gain, None),
            (hnrm0, 0), (hinv0, 0), (gate0, 0), (mixer[0], None), (hidden_gain, None),
        ],
        [((tile, F32), 0), ((cell_shape, BF16), 1)],
        [vec(2)], flops=6 * cell_flops,
    )
    got_grad0 = exchange(grad0)
    glog0, early = cell_call(
        functools.partial(late_terms_kernel, cpd, q, 1), steps,
        halves(after(grads1, grad0))
        + [
            (fac1, 0), (low1, 0), (nrm1, 0), (glog1, 0), (weight[1], None), (terms1, None), (prod0, 1),
            (up0, 0), (gate0, 0), (flags, 0), (mixer[0], None), (owt[0], None), (hidden_gain, None),
            (hidden_bias, None),
        ],
        [((tile, BF16), 0), (((devices * early_rows, hidden), BF16), None)],
        [vec(2), acc(5 * hidden, 2 * width + 16), acc(hidden), acc(cols), acc(cols), acc(cols)],
        flops=13 * cell_flops,
    )

    made_grads0 = product_grad(sides0, got_grad0, True, early.reshape(devices, early_rows, hidden))
    grads0 = exchange(made_grads0)
    fac0, low0, nrm0, inv0 = keep(0, after(z0, made_grads0), False)
    grads0 = after(grads0, nrm0)
    (late,) = loop_call(
        functools.partial(last_terms_kernel, cpd, q), steps,
        halves(grads0) + [(fac0, 0), (low0, 0), (nrm0, 0), (glog0, 0), (weight[0], None)],
        [(((devices * late_rows, hidden), BF16), None)],
        [acc(5 * hidden, 2 * width + 16)], flops=10 * cell_flops,
    )
    got_late = exchange(late.reshape(devices, late_rows, hidden))
    (grad_pair,) = cell_call(
        functools.partial(pair_grad_kernel, cpd, q, 0), steps,
        halves(after(grads0, late))
        + [(fac0, 0), (nrm0, 0), (inv0, 0), (glog0, 0), (up0, 0), (weight[0], None), (input_gain, None)],
        [((pair_rep.shape, BF16), 0)], [vec(1)], flops=5 * cell_flops, vmem=ALL_VMEM,
    )
    (spread,) = cell_call(
        spread_kernel, 1,
        [(grads0, (1, 2 * side // early_rows, early_rows)), (after(got_late, grad_pair), None)],
        [(((devices, early_rows + late_rows, hidden), BF16), None)], [], vmem=ALL_VMEM,
    )
    proj, out, inorm, hnorm, chain = whole_call(
        functools.partial(unpack_kernel, 1.0 / length, early_rows), [exchange(spread)],
        [
            ((2, width, 5 * hidden), F32), ((2, hidden, hidden), F32), ((2, 2, hidden), F32),
            ((2, 2, hidden), F32), ((2, hidden), F32),
        ],
        [], 0,
    )
    return grad_pair, proj, out, inorm, hnorm, chain


def solution(mesh):
    cells = P(("grp", "row"), "col", None)
    return jax.shard_map(
        shards,
        mesh=mesh,
        in_specs=(cells, cells, P("grp"), P("grp")) + (P(),) * 7,
        out_specs=(
            cells, P("grp", None, None), P("grp", None, None), P("grp", None, None),
            P("grp", None, None), P("grp", None),
        ),
        check_vma=False,
    )
```

```python
import functools

import jax
import jax.numpy as jnp
from jax import lax
from jax.experimental import pallas as pl
from jax.experimental.pallas import tpu as pltpu
from jax.sharding import PartitionSpec as P

EPSILON = 1e-05
AXES = ("row", "col")
F32 = jnp.float32
BF16 = jnp.bfloat16
CHANNEL_VMEM = 24 * 1024 * 1024
CELL_VMEM = 50 * 1024 * 1024
ALL_VMEM = 60 * 1024 * 1024


def dot(a, b, ca, cb):
    return lax.dot_general(a, b, (((ca,), (cb,)), ((), ())), preferred_element_type=F32)


def sigmoid(x):
    return 0.5 * jnp.tanh(0.5 * x) + 0.5


def columns(vectors, width):
    c = vectors.shape[1]
    square = jnp.broadcast_to(vectors, (c, c)).T
    return jnp.concatenate([square] * (width // c), 1)


def norm(x):
    centred = x - jnp.mean(x, 0, keepdims=True)
    inv = lax.rsqrt(jnp.mean(centred * centred, 0, keepdims=True) + EPSILON)
    return centred * inv, inv


def norm_grad(grad_scaled, normed, inv, gain):
    g = grad_scaled * gain
    first = jnp.mean(g, 0, keepdims=True)
    second = jnp.mean(g * normed, 0, keepdims=True)
    return (g - first - normed * second) * inv


def unpack(block, cpd):
    devices, rows, cols = block.shape
    values = block.astype(F32)
    parts = []
    for a in range(rows // cpd):
        if cpd % 8 == 0:
            parts.append(values[:, a * cpd : (a + 1) * cpd, :].reshape(devices * cpd, cols))
        else:
            parts.append(
                jnp.concatenate([values[d, a * cpd : (a + 1) * cpd, :] for d in range(devices)], 0)
            )
    return jnp.concatenate(parts, 1)


def pack(tile, cpd, cols):
    channels, lanes = tile.shape
    devices = channels // cpd
    parts = [tile[:, a * cols : (a + 1) * cols] for a in range(lanes // cols)]
    if cpd % 8 == 0:
        return jnp.concatenate([p.reshape(devices, cpd, cols) for p in parts], 1).astype(BF16)
    return jnp.stack(
        [
            jnp.concatenate([p[d * cpd : (d + 1) * cpd, :] for p in parts], 0)
            for d in range(devices)
        ]
    ).astype(BF16)


def fold(tile, width):
    return sum(tile[:, a : a + width] for a in range(0, tile.shape[1], width))


def project(lowered, wt_ref, first, last):
    hidden = wt_ref.shape[0] // 5
    projected = dot(wt_ref[first * hidden : last * hidden, :], lowered, 1, 0)
    return [projected[n * hidden : (n + 1) * hidden] for n in range(last - first)]


def lower(cells, gain, bias):
    normed, inv = norm(cells)
    return normed, inv, (normed * gain + bias).astype(BF16)


def emit_edges(edges_ref, here, cells, wt_ref, gain, bias, mask, cpd, cols):
    part = project(lower(cells, gain, bias)[2], wt_ref, 0, 4)
    edges_ref[:, 0, here, :] = pack(part[0] * sigmoid(part[1]) * mask, cpd, cols)
    edges_ref[:, 1, here, :] = pack(part[2] * sigmoid(part[3]) * mask, cpd, cols)


STEP = []


def step_now():
    return STEP[-1] if STEP else (pl.program_id(0), pl.num_programs(0))


def first_step(fill):
    pl.when(step_now()[0] == 0)(fill)


def last_step(fill):
    index, count = step_now()
    pl.when(index == count - 1)(fill)


def looped_kernel(kernel, steps, in_hows, out_hows, scratches, *refs):
    n_in, n_out = len(in_hows), len(out_hows)
    ins, outs, scratch = refs[:n_in], refs[n_in : n_in + n_out], refs[n_in + n_out : n_in + n_out + scratches]
    bufs = list(refs[n_in + n_out + scratches : -3])
    whole_sems, in_sems, out_sems = refs[-3:]

    def part(ref, how, step, first):
        axis, _, size = how
        start = (step + first) * size
        here = pl.ds(start if isinstance(start, int) else pl.multiple_of(start, size), size)
        return ref.at[tuple(here if n == axis else slice(None) for n in range(axis + 1))]

    def copy_in(k, step):
        how = in_hows[k]
        if how is None:
            return pltpu.make_async_copy(ins[k], bufs[k], whole_sems.at[k])
        return pltpu.make_async_copy(
            part(ins[k], how, step, how[1]), part(bufs[k], how, step, 0), in_sems.at[k, step]
        )

    def copy_out(k, step):
        how = out_hows[k]
        return pltpu.make_async_copy(
            part(bufs[n_in + k], how, step, 0), part(outs[k], how, step, 0), out_sems.at[k, step]
        )

    wholes = [k for k in range(n_in) if in_hows[k] is None]
    parts = [k for k in range(n_in) if in_hows[k] is not None]
    moved = [k for k in range(n_out) if out_hows[k] is not None]
    for k in parts:
        copy_in(k, 0).start()
    for k in wholes:
        copy_in(k, 0).start()
    for step in range(1, steps):
        for k in parts:
            copy_in(k, step).start()
    for k in wholes:
        copy_in(k, 0).wait()

    @pl.loop(0, steps)
    def _(step):
        views = []
        for k in range(n_in):
            if in_hows[k] is None:
                views.append(bufs[k])
            else:
                copy_in(k, step).wait()
                views.append(part(bufs[k], in_hows[k], step, 0))
        for k in range(n_out):
            views.append(outs[k] if out_hows[k] is None else part(bufs[n_in + k], out_hows[k], step, 0))
        STEP.append((step, steps))
        kernel(*views, *scratch)
        STEP.pop()
        for k in moved:
            copy_out(k, step).start()

    for step in range(steps):
        for k in moved:
            copy_out(k, step).wait()


def load_columns(vec, *rows):
    @first_step
    def _():
        for n, (ref, layer) in enumerate(rows):
            vec[n] = columns(ref[layer : layer + 1, :], vec.shape[2])


def clear(*accs):
    @first_step
    def _():
        for acc in accs:
            acc[...] = jnp.zeros_like(acc)


def turned(ref, t, q):
    return jnp.concatenate([ref[t * q + a].astype(F32).T for a in range(q)], 1)


def row_flags(row, mask_smem, chain_smem, start_smem, maskc_ref, chainc_ref):
    whole = start_smem[0] + row
    here = pl.ds(start_smem[1], 1)
    mask = (maskc_ref[here, :] * mask_smem[whole]).astype(F32)
    return mask, (chainc_ref[here, :] == chain_smem[whole]).astype(F32)


def edge_first_kernel(
    cpd, q, mask_smem, chain_smem, start_smem, pair_ref, maskc_ref, chainc_ref, w_ref, gain_ref, bias_ref,
    edges_ref, vec, turned_weight,
):
    rows, cols, width = pair_ref.shape
    load_columns(vec, (gain_ref, 0), (bias_ref, 0))

    @first_step
    def _():
        for n in range(turned_weight.shape[0] // width):
            block = slice(n * width, (n + 1) * width)
            turned_weight[block, :] = w_ref[0, :, block].astype(F32).T.astype(BF16)

    for t in range(rows // q):
        first = pl.program_id(0) * rows + t * q
        mask = jnp.concatenate(
            [
                row_flags(first + a, mask_smem, chain_smem, start_smem, maskc_ref, chainc_ref)[0]
                for a in range(q)
            ],
            1,
        )
        here = slice(t * q * cpd, (t + 1) * q * cpd)
        emit_edges(edges_ref, here, turned(pair_ref, t, q), turned_weight, vec[0], vec[1], mask, cpd, cols)


def first_keep_kernel(
    q, mask_smem, chain_smem, start_smem, pair_ref, cot_ref, maskc_ref, chainc_ref, wt_ref, gain_ref,
    bias_ref, chain_ref, z_ref, up_ref, gate_ref, flags_ref, vec,
):
    load_columns(vec, (gain_ref, 0), (bias_ref, 0), (chain_ref, 0))
    tiles = z_ref.shape[0]
    for t in range(tiles):
        flags = [
            row_flags(
                (pl.program_id(0) * tiles + t) * q + a, mask_smem, chain_smem, start_smem, maskc_ref, chainc_ref
            )
            for a in range(q)
        ]
        mask = jnp.concatenate([f[0] for f in flags], 1)
        same = jnp.concatenate([f[1] for f in flags], 1)
        cells = turned(pair_ref, t, q)
        z_ref[t] = cells.astype(BF16)
        up_ref[t] = turned(cot_ref, t, q).astype(BF16)
        flags_ref[t] = jnp.concatenate([mask, same], 0)
        (logits,) = project(lower(cells, vec[0], vec[1])[2], wt_ref, 4, 5)
        gate_ref[t] = sigmoid(logits + same * vec[2]).astype(BF16)


def keep_kernel(layer, z_ref, flags_ref, wt_ref, gain_ref, bias_ref, chain_ref, fac_ref, low_ref, nrm_ref, inv_ref, *rest):
    vec = rest[-1]
    hidden = wt_ref.shape[0] // 5
    load_columns(vec, (gain_ref, layer), (bias_ref, layer), (chain_ref, layer))
    for t in range(z_ref.shape[0]):
        mask, same = flags_ref[t, 0:1, :], flags_ref[t, 1:2, :]
        normed, inv_ref[t], lowered = lower(z_ref[t].astype(F32), vec[0], vec[1])
        low_ref[t] = lowered
        nrm_ref[t] = normed.astype(BF16)
        part = project(lowered, wt_ref, 0, 3 + len(rest))
        for n in (0, 2):
            sig = sigmoid(part[n + 1]) * mask
            fac_ref[t, n * hidden : (n + 1) * hidden, :] = sig.astype(BF16)
            fac_ref[t, (n + 1) * hidden : (n + 2) * hidden, :] = (
                part[n] * sig * (1.0 - sig)
            ).astype(BF16)
        for gate_ref in rest[:-1]:
            gate_ref[t] = sigmoid(part[4] + same * vec[2]).astype(BF16)


def keep_product_kernel(cpd, q, prod_ref, nrm_ref, inv_ref):
    rows = q * cpd
    for t in range(nrm_ref.shape[0]):
        normed, inv_ref[t] = norm(unpack(prod_ref[:, t * rows : (t + 1) * rows, :], cpd))
        nrm_ref[t] = normed.astype(BF16)


def mix_edge_kernel(
    cpd, q, layer, prod_ref, z_ref, gate_ref, flags_ref, owt_ref, hgain_ref, hbias_ref, wt_ref,
    gain_ref, bias_ref, edges_ref, znext_ref, vec,
):
    tiles, _, lanes = z_ref.shape
    rows = q * cpd
    load_columns(vec, (hgain_ref, layer), (hbias_ref, layer), (gain_ref, layer + 1), (bias_ref, layer + 1))
    for t in range(tiles):
        here = slice(t * rows, (t + 1) * rows)
        hnormed, _ = norm(unpack(prod_ref[:, here, :], cpd))
        hscaled = (hnormed * vec[0] + vec[1]).astype(BF16)
        cells = z_ref[t].astype(F32) + gate_ref[t].astype(F32) * dot(owt_ref[...], hscaled, 1, 0)
        znext_ref[t] = cells
        emit_edges(
            edges_ref, here, cells, wt_ref, vec[2], vec[3], flags_ref[t, 0:1, :], cpd, lanes // q
        )


def mix_grad(upstream, hnormed, hinv, gate_ref, t, ow_ref, hgain):
    grad_mixed = (upstream * gate_ref[t].astype(F32)).astype(BF16)
    return norm_grad(dot(ow_ref[...], grad_mixed, 1, 0), hnormed, hinv, hgain)


def mix_back_kernel(cpd, q, layer, prod_ref, up_ref, gate_ref, ow_ref, hgain_ref, gp_ref, vec):
    tiles, _, lanes = up_ref.shape
    rows = q * cpd
    load_columns(vec, (hgain_ref, layer))
    for t in range(tiles):
        here = slice(t * rows, (t + 1) * rows)
        hnormed, hinv = norm(unpack(prod_ref[:, here, :], cpd))
        grad = mix_grad(up_ref[t].astype(F32), hnormed, hinv, gate_ref, t, ow_ref, vec[0])
        gp_ref[:, here, :] = pack(grad, cpd, lanes // q)


def mix_terms(upstream, product, gate, same, ow_ref, owt_ref, hgain, hbias, acc_ow, acc_hg, acc_hb, acc_ch):
    width = acc_hg.shape[1]
    hnormed, _ = norm(product)
    hscaled = (hnormed * hgain + hbias).astype(BF16)
    mixed = dot(owt_ref[...], hscaled, 1, 0)
    grad_gate = upstream * gate
    grad_logits = grad_gate * mixed * (1.0 - gate)
    grad_mixed = grad_gate.astype(BF16)
    acc_ow[...] += dot(hscaled, grad_mixed, 1, 1)
    grad_hscaled = dot(ow_ref[...], grad_mixed, 1, 0)
    acc_hg[...] += fold(grad_hscaled * hnormed, width)
    acc_hb[...] += fold(grad_hscaled, width)
    acc_ch[...] += fold(grad_logits * same, width)
    return grad_logits


def row_of(acc):
    return jnp.sum(acc.T, 0, keepdims=True)


def mix_terms_kernel(
    cpd, q, layer, prod_ref, up_ref, gate_ref, flags_ref, ow_ref, owt_ref, hgain_ref, hbias_ref,
    glog_ref, terms_ref, vec, acc_ow, acc_hg, acc_hb, acc_ch,
):
    rows = q * cpd
    load_columns(vec, (hgain_ref, layer), (hbias_ref, layer))
    clear(acc_ow, acc_hg, acc_hb, acc_ch)
    for t in range(up_ref.shape[0]):
        grad_logits = mix_terms(
            up_ref[t].astype(F32), unpack(prod_ref[:, t * rows : (t + 1) * rows, :], cpd),
            gate_ref[t].astype(F32), flags_ref[t, 1:2, :], ow_ref, owt_ref, vec[0], vec[1],
            acc_ow, acc_hg, acc_hb, acc_ch,
        )
        glog_ref[t] = grad_logits.astype(BF16)

    @last_step
    def _():
        hidden = acc_ow.shape[0]
        terms_ref[:hidden, :] = acc_ow[...]
        vectors = [row_of(acc_hg[...]), row_of(acc_hb[...]), row_of(acc_ch[...])]
        vectors.append(jnp.zeros((terms_ref.shape[0] - hidden - 3, hidden), F32))
        terms_ref[hidden:, :] = jnp.concatenate(vectors, 0)


def project_grad(left_ref, right_ref, fac_ref, glog_ref, t, cpd, rows):
    hidden = fac_ref.shape[1] // 4
    here = slice(t * rows, (t + 1) * rows)
    grads = (unpack(left_ref[:, here, :], cpd), unpack(right_ref[:, here, :], cpd))
    blocks = [
        (grads[n // 2] * fac_ref[t, n * hidden : (n + 1) * hidden, :].astype(F32)).astype(BF16)
        for n in range(4)
    ]
    return jnp.concatenate(blocks + [glog_ref[t]], 0)


def input_grad(gproj, nrm_ref, inv_ref, t, w_ref, gain):
    return norm_grad(dot(w_ref[...], gproj, 1, 0), nrm_ref[t].astype(F32), inv_ref[t], gain)


def edge_mix_back_kernel(
    cpd, q, layer, left_ref, right_ref, fac_ref, nrm_ref, inv_ref, glog_ref, up_ref, w_ref, gain_ref,
    hnrm_ref, hinv_ref, gate_ref, ow_ref, hgain_ref, upnext_ref, gp_ref, vec,
):
    tiles, _, lanes = up_ref.shape
    rows = q * cpd
    load_columns(vec, (gain_ref, layer), (hgain_ref, layer - 1))
    for t in range(tiles):
        gproj = project_grad(left_ref, right_ref, fac_ref, glog_ref, t, cpd, rows)
        upstream = up_ref[t].astype(F32) + input_grad(gproj, nrm_ref, inv_ref, t, w_ref, vec[0])
        upnext_ref[t] = upstream
        grad = mix_grad(upstream, hnrm_ref[t].astype(F32), hinv_ref[t], gate_ref, t, ow_ref, vec[1])
        gp_ref[:, t * rows : (t + 1) * rows, :] = pack(grad, cpd, lanes // q)


def edge_terms(gproj, low_ref, nrm_ref, t, acc_w):
    ones = jnp.ones((16, gproj.shape[1]), BF16)
    acc_w[...] += dot(jnp.concatenate([low_ref[t], nrm_ref[t], ones], 0), gproj, 1, 1)


def finish_edge(out_ref, acc_w, w_ref):
    width = w_ref.shape[0]
    for n in range(acc_w.shape[1] // width):
        out_ref[n * width : (n + 1) * width, :] = acc_w[:width, n * width : (n + 1) * width].astype(BF16)
    weight = w_ref[...].astype(F32)
    gain = row_of(fold(weight * acc_w[width : 2 * width, :], width))
    bias = row_of(fold(weight * acc_w[2 * width : 2 * width + 1, :], width))
    return [gain, bias]


def finish_rows(out_ref, first, vectors):
    pad = jnp.zeros((out_ref.shape[0] - first - sum(v.shape[0] for v in vectors), out_ref.shape[1]), F32)
    out_ref[first:, :] = jnp.concatenate(vectors + [pad], 0).astype(BF16)


def late_terms_kernel(
    cpd, q, layer, left_ref, right_ref, fac_ref, low_ref, nrm_ref, glog_ref, w_ref, terms_ref,
    prod_ref, up_ref, gate_ref, flags_ref, ow_ref, owt_ref, hgain_ref, hbias_ref,
    glognext_ref, all_ref, vec, acc_w, acc_ow, acc_hg, acc_hb, acc_ch,
):
    rows = q * cpd
    load_columns(vec, (hgain_ref, layer - 1), (hbias_ref, layer - 1))
    clear(acc_w, acc_ow, acc_hg, acc_hb, acc_ch)
    for t in range(up_ref.shape[0]):
        gproj = project_grad(left_ref, right_ref, fac_ref, glog_ref, t, cpd, rows)
        edge_terms(gproj, low_ref, nrm_ref, t, acc_w)
        grad_logits = mix_terms(
            up_ref[t], unpack(prod_ref[:, t * rows : (t + 1) * rows, :], cpd), gate_ref[t].astype(F32),
            flags_ref[t, 1:2, :], ow_ref, owt_ref, vec[0], vec[1], acc_ow, acc_hg, acc_hb, acc_ch,
        )
        glognext_ref[t] = grad_logits.astype(BF16)

    @last_step
    def _():
        hidden = acc_ow.shape[0]
        vectors = finish_edge(all_ref, acc_w, w_ref)
        all_ref[5 * hidden : 6 * hidden, :] = terms_ref[:hidden, :].astype(BF16)
        all_ref[6 * hidden : 7 * hidden, :] = acc_ow[...].astype(BF16)
        vectors += [terms_ref[hidden : hidden + 3, :]]
        vectors += [row_of(acc_hg[...]), row_of(acc_hb[...]), row_of(acc_ch[...])]
        finish_rows(all_ref, 7 * hidden, vectors)


def last_terms_kernel(
    cpd, q, left_ref, right_ref, fac_ref, low_ref, nrm_ref, glog_ref, w_ref, all_ref, acc_w,
):
    clear(acc_w)
    tiles = range(low_ref.shape[0])
    gproj = [project_grad(left_ref, right_ref, fac_ref, glog_ref, t, cpd, q * cpd) for t in tiles]
    ones = jnp.ones((16, low_ref.shape[2]), BF16)
    sides = [jnp.concatenate([low_ref[t], nrm_ref[t], ones], 0) for t in tiles]
    acc_w[...] += dot(jnp.concatenate(sides, 1), jnp.concatenate(gproj, 1), 1, 1)

    @last_step
    def _():
        finish_rows(all_ref, acc_w.shape[1], finish_edge(all_ref, acc_w, w_ref))


def pair_grad_kernel(
    cpd, q, layer, left_ref, right_ref, fac_ref, nrm_ref, inv_ref, glog_ref, up_ref, w_ref, gain_ref, pair_ref, vec,
):
    tiles, _, lanes = up_ref.shape
    cols = lanes // q
    load_columns(vec, (gain_ref, layer))
    for t in range(tiles):
        gproj = project_grad(left_ref, right_ref, fac_ref, glog_ref, t, cpd, q * cpd)
        upstream = up_ref[t] + input_grad(gproj, nrm_ref, inv_ref, t, w_ref, vec[0])
        for a in range(q):
            pair_ref[t * q + a] = upstream[:, a * cols : (a + 1) * cols].T.astype(BF16)


def spread_kernel(early_ref, late_ref, out_ref):
    early = jnp.sum(early_ref[...].astype(F32), 0).astype(BF16)
    late = jnp.sum(late_ref[...].astype(F32), 0).astype(BF16)
    out_ref[...] = jnp.broadcast_to(jnp.concatenate([early, late], 0)[None], out_ref.shape)


def unpack_kernel(factor, early_rows, got_ref, proj_ref, ow_ref, inorm_ref, hnorm_ref, chain_ref):
    width = ow_ref.shape[1]
    early = got_ref[:, :early_rows, :].astype(F32).reshape(-1, width) * factor
    late = got_ref[:, early_rows:, :].astype(F32).reshape(-1, width) * factor
    for n in range(5):
        rows, lanes = slice(n * width, (n + 1) * width), slice(n * width, (n + 1) * width)
        proj_ref[0, :, lanes] = late[rows]
        proj_ref[1, :, lanes] = early[rows]
    ow_ref[1] = early[5 * width : 6 * width]
    ow_ref[0] = early[6 * width : 7 * width]
    inorm_ref[0] = late[5 * width : 5 * width + 2]
    vectors = early[7 * width : 7 * width + 8]
    inorm_ref[1] = vectors[0:2]
    hnorm_ref[1] = vectors[2:4]
    hnorm_ref[0] = vectors[5:7]
    chain_ref[...] = jnp.concatenate([vectors[7:8], vectors[4:5]], 0)


def cell_call(kernel, steps, ins, outs, scratch, prefetch=(), flops=0, vmem=CELL_VMEM):
    def spec(shape, how):
        if how is None:
            return pl.BlockSpec(shape, lambda *s: (0,) * len(shape))
        axis, first, size = how if isinstance(how, tuple) else (how, 0, shape[how] // steps)
        block = tuple(size if n == axis else length for n, length in enumerate(shape))
        moves = shape[axis] >= size * steps
        return pl.BlockSpec(
            block,
            lambda *s: tuple((s[0] if moves else 0) + first if n == axis else 0 for n in range(len(shape))),
        )

    moved = sum(a.size * a.dtype.itemsize for a, _ in ins)
    moved += sum(functools.reduce(lambda x, y: x * y, s, 1) * jnp.dtype(t).itemsize for (s, t), _ in outs)
    return pl.pallas_call(
        kernel,
        grid_spec=pltpu.PrefetchScalarGridSpec(
            num_scalar_prefetch=len(prefetch),
            grid=(steps,),
            in_specs=[spec(a.shape, how) for a, how in ins],
            out_specs=[spec(s, how) for (s, _), how in outs],
            scratch_shapes=scratch,
        ),
        out_shape=[jax.ShapeDtypeStruct(s, t) for (s, t), _ in outs],
        compiler_params=pltpu.CompilerParams(vmem_limit_bytes=vmem),
        cost_estimate=pl.CostEstimate(flops=flops, bytes_accessed=int(moved), transcendentals=0),
    )(*prefetch, *[a for a, _ in ins])


def widen(src_ref, dst):
    devices, cols = src_ref.shape[0], src_ref.shape[-1]
    per = dst.shape[0] // devices
    for d in range(devices):
        dst[d * per : (d + 1) * per, :] = src_ref[d].astype(F32).reshape(per, cols)


def narrow(src, dst_ref):
    devices = dst_ref.shape[0]
    per = src.shape[0] // devices
    for d in range(devices):
        dst_ref[d, :per, :] = src[d * per : (d + 1) * per, :].astype(BF16)


def get_channel(src, ch, sub, subs, dims):
    row_devs, col_devs, rows, cpd, cols = dims
    halves = []
    for s in range(col_devs):
        parts = []
        for r in range(row_devs):
            base = ((r * col_devs + s) * subs + sub) * rows * cpd
            parts.append(src[pl.ds(base + ch, rows, stride=cpd), :])
        halves.append(jnp.concatenate(parts, 0))
    return jnp.concatenate(halves, 1).astype(BF16)


def put_channel(dst, value, ch, sub, subs, dims):
    row_devs, col_devs, rows, cpd, cols = dims
    for s in range(col_devs):
        for r in range(row_devs):
            base = ((r * col_devs + s) * subs + sub) * rows * cpd
            dst[pl.ds(base + ch, rows, stride=cpd), :] = value[
                r * rows : (r + 1) * rows, s * cols : (s + 1) * cols
            ]


def product_kernel(dims, outgoing, edges_ref, out_ref, edges, result):
    widen(edges_ref, edges)
    for ch in range(dims[3]):
        left = get_channel(edges, ch, 0, 2, dims)
        right = get_channel(edges, ch, 1, 2, dims)
        value = dot(left, right, 1, 1) if outgoing else dot(left, right, 0, 0)
        put_channel(result, value, ch, 0, 1, dims)
    narrow(result, out_ref)


def assemble_kernel(dims, edges_ref, out_ref, edges):
    widen(edges_ref, edges)
    for ch in range(dims[3]):
        for sub in range(2):
            out_ref[ch, sub] = get_channel(edges, ch, sub, 2, dims)


def product_grad_kernel(dims, outgoing, count, sides_hbm, grad_ref, *refs):
    terms, (out_hbm, grad, result, sides_ref, out_ref, side_sems, out_sems, term_sems) = refs[:count], refs[count:]
    channels, devices = sides_ref.shape[0], out_ref.shape[0]
    rows = out_ref.shape[1]

    def side_copy(ch):
        return pltpu.make_async_copy(sides_hbm.at[ch], sides_ref.at[ch], side_sems.at[ch])

    def out_copy(d):
        return pltpu.make_async_copy(out_ref.at[d], out_hbm.at[d, pl.ds(0, rows)], out_sems.at[d])

    def term_copy(n):
        extra = terms[n].shape[1]
        return pltpu.make_async_copy(terms[n], out_hbm.at[:, pl.ds(rows, extra)], term_sems.at[n])

    for ch in range(channels):
        side_copy(ch).start()
    for n in range(count):
        term_copy(n).start()
    widen(grad_ref, grad)
    for ch in range(channels):
        gp = get_channel(grad, ch, 0, 1, dims)
        side_copy(ch).wait()
        left, right = sides_ref[ch, 0], sides_ref[ch, 1]
        if outgoing:
            grad_left = dot(gp, right, 1, 0)
            grad_right = dot(gp, left, 0, 0)
        else:
            grad_left = dot(right, gp, 1, 1)
            grad_right = dot(left, gp, 1, 0)
        put_channel(result, grad_left, ch, 0, 2, dims)
        put_channel(result, grad_right, ch, 1, 2, dims)
    for d in range(devices):
        out_ref[d] = result[d * rows : (d + 1) * rows, :].astype(BF16)
        out_copy(d).start()
    for n in range(count):
        term_copy(n).wait()
    for d in range(devices):
        out_copy(d).wait()


def loop_call(kernel, steps, ins, outs, scratch, flops=0):
    def part(shape, how):
        return how if how is None or isinstance(how, tuple) else (how, 0, shape[how] // steps)

    in_hows = [part(a.shape, how) for a, how in ins]
    out_hows = [part(shape, how) for (shape, _), how in outs]

    def buffer(shape, dtype, how):
        if how is None:
            return pltpu.VMEM(shape, dtype)
        return pltpu.VMEM(tuple(how[2] * steps if n == how[0] else m for n, m in enumerate(shape)), dtype)

    buffers = [buffer(a.shape, a.dtype, how) for (a, _), how in zip(ins, in_hows)]
    for ((shape, dtype), _), how in zip(outs, out_hows):
        buffers.append(pltpu.VMEM((8, 128), F32) if how is None else buffer(shape, dtype, how))
    sems = [
        pltpu.SemaphoreType.DMA((len(ins),)), pltpu.SemaphoreType.DMA((len(ins), steps)),
        pltpu.SemaphoreType.DMA((len(outs), steps)),
    ]
    made = whole_call(
        functools.partial(looped_kernel, kernel, steps, in_hows, out_hows, len(scratch)),
        [a for a, _ in ins], [o for o, _ in outs], list(scratch) + buffers + sems, flops, CELL_VMEM,
        [pltpu.HBM] * len(ins), [pltpu.VMEM if how is None else pltpu.HBM for how in out_hows],
    )
    return made if len(outs) > 1 else (made,)


def whole_call(kernel, ins, outs, scratch, flops, vmem=None, in_spaces=None, out_spaces=None):
    moved = sum(a.size * a.dtype.itemsize for a in ins)
    moved += sum(functools.reduce(lambda x, y: x * y, s, 1) * jnp.dtype(t).itemsize for s, t in outs)
    specs = [pl.BlockSpec(memory_space=m) for m in out_spaces or [pltpu.VMEM] * len(outs)]
    shapes = [jax.ShapeDtypeStruct(s, t) for s, t in outs]
    return pl.pallas_call(
        kernel,
        in_specs=[pl.BlockSpec(memory_space=m) for m in in_spaces or [pltpu.VMEM] * len(ins)],
        out_specs=specs if len(outs) > 1 else specs[0],
        out_shape=shapes if len(outs) > 1 else shapes[0],
        scratch_shapes=scratch,
        compiler_params=pltpu.CompilerParams(vmem_limit_bytes=vmem or CHANNEL_VMEM),
        cost_estimate=pl.CostEstimate(flops=flops, bytes_accessed=int(moved), transcendentals=0),
    )(*ins)


def exchange(array):
    return lax.all_to_all(array, AXES, split_axis=0, concat_axis=0, tiled=True)


def after(array, *others):
    return lax.optimization_barrier((array, *others))[0]


def shards(
    pair_rep, cotangent, residue_mask, chain_ids, proj_weight, out_weight,
    input_gain, input_bias, hidden_gain, hidden_bias, chain_bias,
):
    rows, cols, width = pair_rep.shape
    hidden = out_weight.shape[1]
    row_devs, col_devs = lax.axis_size("row"), lax.axis_size("col")
    devices = row_devs * col_devs
    length = rows * row_devs
    cpd = hidden // devices
    q = max(1, 16 // cpd)
    tiles = rows // q
    lanes = q * cols
    steps = max(1, tiles // 4)
    dims = (row_devs, col_devs, rows, cpd, cols)
    side = rows * cpd

    starts = jnp.stack([lax.axis_index("row") * rows, lax.axis_index("col")]).astype(jnp.int32)
    wt = [proj_weight[n].T for n in range(2)]
    owt = [out_weight[n].T for n in range(2)]
    weight = [proj_weight[n] for n in range(2)]
    mixer = [out_weight[n] for n in range(2)]
    mask_cols, chain_cols = residue_mask.reshape(col_devs, cols), chain_ids.reshape(col_devs, cols)
    scalars = (residue_mask, chain_ids, starts)
    tile = (tiles, width, lanes)
    fac_tile = (tiles, 4 * hidden, lanes)
    edge_shape = (devices, 2, side, cols)
    cell_shape = (devices, side, cols)
    vec = lambda n: pltpu.VMEM((n, width, lanes), F32)
    acc = lambda n, m=width: pltpu.VMEM((m, n), F32)
    wide = lambda n: pltpu.VMEM((n * devices * side, cols), F32)
    cell_flops = 2 * rows * cols * width * hidden
    tri_flops = 2 * cpd * length**3
    rows_for = lambda n: -(-n // (devices * 16)) * 16
    early_rows, late_rows = rows_for(7 * hidden + 8), rows_for(5 * hidden + 2)
    terms_shape = (hidden + 8, hidden)

    def product(edges, outgoing):
        return whole_call(
            functools.partial(product_kernel, dims, outgoing), [edges], [(cell_shape, BF16)],
            [wide(2), wide(1)], tri_flops,
        )

    def assemble(edges):
        return whole_call(
            functools.partial(assemble_kernel, dims), [edges], [((cpd, 2, length, length), BF16)], [wide(2)], 0
        )

    def product_grad(sides, grad, outgoing, *terms):
        out_rows = 2 * side + sum(t.shape[1] for t in terms)
        return whole_call(
            functools.partial(product_grad_kernel, dims, outgoing, len(terms)), [sides, grad, *terms],
            [((devices, out_rows, cols), BF16)],
            [
                wide(1), wide(2), pltpu.VMEM(sides.shape, BF16), pltpu.VMEM((devices, 2 * side, cols), BF16),
                pltpu.SemaphoreType.DMA((cpd,)), pltpu.SemaphoreType.DMA((devices,)),
                pltpu.SemaphoreType.DMA((max(1, len(terms)),)),
            ],
            2 * tri_flops, None, [pltpu.HBM, pltpu.VMEM] + [pltpu.HBM] * len(terms), [pltpu.HBM],
        )

    def halves(grads):
        per = side // steps
        return [(grads, (1, 0, per)), (grads, (1, steps, per))]

    def keep(layer, z, with_gate):
        norm_outs = [((tile, BF16), 0), ((tile, BF16), 0), (((tiles, 1, lanes), F32), 0)]
        return cell_call(
            functools.partial(keep_kernel, layer), steps,
            [
                (z, 0), (flags, 0), (wt[layer], None), (input_gain, None), (input_bias, None), (chain_bias, None),
            ],
            [((fac_tile, BF16), 0)] + norm_outs + [((tile, BF16), 0)] * with_gate,
            [vec(3)], flops=5 * cell_flops,
        )

    (edges0,) = cell_call(
        functools.partial(edge_first_kernel, cpd, q), steps,
        [
            (pair_rep, 0), (mask_cols, None), (chain_cols, None), (proj_weight, (0, 0, 1)),
            (input_gain, None), (input_bias, None),
        ],
        [((edge_shape, BF16), 2)], [vec(2), pltpu.VMEM((5 * hidden, width), BF16)],
        prefetch=scalars, flops=4 * cell_flops, vmem=ALL_VMEM,
    )
    got0 = exchange(edges0)
    z0, up, gate0, flags = cell_call(
        functools.partial(first_keep_kernel, q), steps,
        [
            (after(pair_rep, edges0), 0), (cotangent, 0), (mask_cols, None), (chain_cols, None), (wt[0], None),
            (input_gain, None), (input_bias, None), (chain_bias, None),
        ],
        [((tile, BF16), 0), ((tile, BF16), 0), ((tile, BF16), 0), (((tiles, 2, lanes), F32), 0)],
        [vec(3)], prefetch=scalars, flops=2 * cell_flops,
    )
    made0 = product(after(got0, z0), True)
    prod0 = exchange(made0)
    sides0 = assemble(after(got0, made0))
    edges1, z1 = loop_call(
        functools.partial(mix_edge_kernel, cpd, q, 0), steps,
        [
            (after(prod0, sides0), 1), (z0, 0), (gate0, 0), (flags, 0), (owt[0], None), (hidden_gain, None),
            (hidden_bias, None), (wt[1], None), (input_gain, None), (input_bias, None),
        ],
        [((edge_shape, BF16), 2), ((tile, F32), 0)], [vec(4)], flops=5 * cell_flops,
    )
    got1 = exchange(edges1)
    fac1, low1, nrm1, inv1, gate1 = keep(1, after(z1, edges1), True)
    made1 = product(after(got1, gate1), False)
    prod1 = exchange(made1)
    sides1 = assemble(after(got1, made1))

    (grad1,) = loop_call(
        functools.partial(mix_back_kernel, cpd, q, 1), steps,
        [(after(prod1, sides1), 1), (up, 0), (gate1, 0), (mixer[1], None), (hidden_gain, None)],
        [((cell_shape, BF16), 1)], [vec(1)], flops=cell_flops,
    )
    got_grad1 = exchange(grad1)
    hnrm0, hinv0 = cell_call(
        functools.partial(keep_product_kernel, cpd, q), steps, [(after(prod0, grad1), 1)],
        [((tile, BF16), 0), (((tiles, 1, lanes), F32), 0)], [],
    )
    made_grads1 = product_grad(sides1, after(got_grad1, hnrm0), False)
    grads1 = exchange(made_grads1)
    glog1, terms1 = cell_call(
        functools.partial(mix_terms_kernel, cpd, q, 1), steps,
        [
            (after(prod1, made_grads1), 1), (up, 0), (gate1, 0), (flags, 0), (mixer[1], None), (owt[1], None),
            (hidden_gain, None), (hidden_bias, None),
        ],
        [((tile, BF16), 0), ((terms_shape, F32), None)],
        [vec(2), acc(hidden), acc(cols), acc(cols), acc(cols)], flops=3 * cell_flops,
    )
    up0, grad0 = loop_call(
        functools.partial(edge_mix_back_kernel, cpd, q, 1), steps,
        halves(after(grads1, glog1))
        + [
            (fac1, 0), (nrm1, 0), (inv1, 0), (glog1, 0), (up, 0), (weight[1], None), (input_gain, None),
            (hnrm0, 0), (hinv0, 0), (gate0, 0), (mixer[0], None), (hidden_gain, None),
        ],
        [((tile, F32), 0), ((cell_shape, BF16), 1)],
        [vec(2)], flops=6 * cell_flops,
    )
    got_grad0 = exchange(grad0)
    glog0, early = cell_call(
        functools.partial(late_terms_kernel, cpd, q, 1), steps,
        halves(after(grads1, grad0))
        + [
            (fac1, 0), (low1, 0), (nrm1, 0), (glog1, 0), (weight[1], None), (terms1, None), (prod0, 1),
            (up0, 0), (gate0, 0), (flags, 0), (mixer[0], None), (owt[0], None), (hidden_gain, None),
            (hidden_bias, None),
        ],
        [((tile, BF16), 0), (((devices * early_rows, hidden), BF16), None)],
        [vec(2), acc(5 * hidden, 2 * width + 16), acc(hidden), acc(cols), acc(cols), acc(cols)],
        flops=13 * cell_flops,
    )

    made_grads0 = product_grad(sides0, got_grad0, True, early.reshape(devices, early_rows, hidden))
    grads0 = exchange(made_grads0)
    fac0, low0, nrm0, inv0 = keep(0, after(z0, made_grads0), False)
    grads0 = after(grads0, nrm0)
    (late,) = loop_call(
        functools.partial(last_terms_kernel, cpd, q), steps,
        halves(grads0) + [(fac0, 0), (low0, 0), (nrm0, 0), (glog0, 0), (weight[0], None)],
        [(((devices * late_rows, hidden), BF16), None)],
        [acc(5 * hidden, 2 * width + 16)], flops=10 * cell_flops,
    )
    got_late = exchange(late.reshape(devices, late_rows, hidden))
    (grad_pair,) = cell_call(
        functools.partial(pair_grad_kernel, cpd, q, 0), steps,
        halves(after(grads0, late))
        + [(fac0, 0), (nrm0, 0), (inv0, 0), (glog0, 0), (up0, 0), (weight[0], None), (input_gain, None)],
        [((pair_rep.shape, BF16), 0)], [vec(1)], flops=5 * cell_flops, vmem=ALL_VMEM,
    )
    (spread,) = cell_call(
        spread_kernel, 1,
        [(grads0, (1, 2 * side // early_rows, early_rows)), (after(got_late, grad_pair), None)],
        [(((devices, early_rows + late_rows, hidden), BF16), None)], [], vmem=ALL_VMEM,
    )
    proj, out, inorm, hnorm, chain = whole_call(
        functools.partial(unpack_kernel, 1.0 / length, early_rows), [exchange(spread)],
        [
            ((2, width, 5 * hidden), F32), ((2, hidden, hidden), F32), ((2, 2, hidden), F32),
            ((2, 2, hidden), F32), ((2, hidden), F32),
        ],
        [], 0,
    )
    return grad_pair, proj, out, inorm, hnorm, chain


def solution(mesh):
    cells = P(("grp", "row"), "col", None)
    return jax.shard_map(
        shards,
        mesh=mesh,
        in_specs=(cells, cells, P("grp"), P("grp")) + (P(),) * 7,
        out_specs=(
            cells, P("grp", None, None), P("grp", None, None), P("grp", None, None),
            P("grp", None, None), P("grp", None),
        ),
        check_vma=False,
    )
```

```python
import functools

import jax
import jax.numpy as jnp
from jax import lax
from jax.experimental import pallas as pl
from jax.experimental.pallas import tpu as pltpu
from jax.sharding import PartitionSpec as P

EPSILON = 1e-05
AXES = ("row", "col")
F32 = jnp.float32
BF16 = jnp.bfloat16
CHANNEL_VMEM = 50 * 1024 * 1024
CELL_VMEM = 50 * 1024 * 1024
ALL_VMEM = 60 * 1024 * 1024


def dot(a, b, ca, cb):
    return lax.dot_general(a, b, (((ca,), (cb,)), ((), ())), preferred_element_type=F32)


def sigmoid(x):
    return 0.5 * jnp.tanh(0.5 * x) + 0.5


def columns(vectors, width):
    c = vectors.shape[1]
    square = jnp.broadcast_to(vectors, (c, c)).T
    return jnp.concatenate([square] * (width // c), 1)


def norm(x):
    centred = x - jnp.mean(x, 0, keepdims=True)
    inv = lax.rsqrt(jnp.mean(centred * centred, 0, keepdims=True) + EPSILON)
    return centred * inv, inv


def norm_grad(grad_scaled, normed, inv, gain):
    g = grad_scaled * gain
    first = jnp.mean(g, 0, keepdims=True)
    second = jnp.mean(g * normed, 0, keepdims=True)
    return (g - first - normed * second) * inv


def unpack(block, cpd):
    devices, rows, cols = block.shape
    values = block.astype(F32)
    parts = []
    for a in range(rows // cpd):
        if cpd % 8 == 0:
            parts.append(values[:, a * cpd : (a + 1) * cpd, :].reshape(devices * cpd, cols))
        else:
            parts.append(
                jnp.concatenate([values[d, a * cpd : (a + 1) * cpd, :] for d in range(devices)], 0)
            )
    return jnp.concatenate(parts, 1)


def pack(tile, cpd, cols):
    channels, lanes = tile.shape
    devices = channels // cpd
    parts = [tile[:, a * cols : (a + 1) * cols] for a in range(lanes // cols)]
    if cpd % 8 == 0:
        return jnp.concatenate([p.reshape(devices, cpd, cols) for p in parts], 1).astype(BF16)
    return jnp.stack(
        [
            jnp.concatenate([p[d * cpd : (d + 1) * cpd, :] for p in parts], 0)
            for d in range(devices)
        ]
    ).astype(BF16)


def fold(tile, width):
    return sum(tile[:, a : a + width] for a in range(0, tile.shape[1], width))


def project(lowered, wt_ref, first, last):
    hidden = wt_ref.shape[0] // 5
    projected = dot(wt_ref[first * hidden : last * hidden, :], lowered, 1, 0)
    return [projected[n * hidden : (n + 1) * hidden] for n in range(last - first)]


def lower(cells, gain, bias):
    normed, inv = norm(cells)
    return normed, inv, (normed * gain + bias).astype(BF16)


def emit_edges(edges_ref, here, cells, wt_ref, gain, bias, mask, cpd, cols):
    part = project(lower(cells, gain, bias)[2], wt_ref, 0, 4)
    edges_ref[:, 0, here, :] = pack(part[0] * sigmoid(part[1]) * mask, cpd, cols)
    edges_ref[:, 1, here, :] = pack(part[2] * sigmoid(part[3]) * mask, cpd, cols)


def first_step(fill):
    pl.when(pl.program_id(0) == 0)(fill)


def last_step(fill):
    pl.when(pl.program_id(0) == pl.num_programs(0) - 1)(fill)


def load_columns(vec, *rows):
    @first_step
    def _():
        for n, (ref, layer) in enumerate(rows):
            vec[n] = columns(ref[layer : layer + 1, :], vec.shape[2])


def clear(*accs):
    @first_step
    def _():
        for acc in accs:
            acc[...] = jnp.zeros_like(acc)


def turned(ref, t, q):
    return jnp.concatenate([ref[t * q + a].astype(F32).T for a in range(q)], 1)


def row_flags(row, device_rows, mask_smem, chain_smem, maskc_ref, chainc_ref):
    whole = lax.axis_index("row") * device_rows + row
    here = pl.ds(lax.axis_index("col"), 1)
    mask = (maskc_ref[here, :] * mask_smem[whole]).astype(F32)
    return mask, (chainc_ref[here, :] == chain_smem[whole]).astype(F32)


def edge_first_kernel(
    cpd, q, device_rows, mask_smem, chain_smem, pair_ref, maskc_ref, chainc_ref, w_ref, gain_ref, bias_ref,
    edges_ref, vec, turned_weight,
):
    rows, cols, width = pair_ref.shape
    load_columns(vec, (gain_ref, 0), (bias_ref, 0))

    @first_step
    def _():
        for n in range(turned_weight.shape[0] // width):
            block = slice(n * width, (n + 1) * width)
            turned_weight[block, :] = w_ref[0, :, block].astype(F32).T.astype(BF16)

    for t in range(rows // q):
        first = pl.program_id(0) * rows + t * q
        mask = jnp.concatenate(
            [
                row_flags(first + a, device_rows, mask_smem, chain_smem, maskc_ref, chainc_ref)[0]
                for a in range(q)
            ],
            1,
        )
        here = slice(t * q * cpd, (t + 1) * q * cpd)
        emit_edges(edges_ref, here, turned(pair_ref, t, q), turned_weight, vec[0], vec[1], mask, cpd, cols)


def first_keep_kernel(
    q, device_rows, mask_smem, chain_smem, pair_ref, cot_ref, maskc_ref, chainc_ref, wt_ref, gain_ref,
    bias_ref, chain_ref, z_ref, up_ref, gate_ref, flags_ref, vec,
):
    load_columns(vec, (gain_ref, 0), (bias_ref, 0), (chain_ref, 0))
    tiles = z_ref.shape[0]
    for t in range(tiles):
        flags = [
            row_flags(
                (pl.program_id(0) * tiles + t) * q + a, device_rows, mask_smem, chain_smem, maskc_ref, chainc_ref
            )
            for a in range(q)
        ]
        mask = jnp.concatenate([f[0] for f in flags], 1)
        same = jnp.concatenate([f[1] for f in flags], 1)
        cells = turned(pair_ref, t, q)
        z_ref[t] = cells.astype(BF16)
        up_ref[t] = turned(cot_ref, t, q).astype(BF16)
        flags_ref[t] = jnp.concatenate([mask, same], 0)
        (logits,) = project(lower(cells, vec[0], vec[1])[2], wt_ref, 4, 5)
        gate_ref[t] = sigmoid(logits + same * vec[2]).astype(BF16)


def keep_kernel(layer, z_ref, flags_ref, wt_ref, gain_ref, bias_ref, chain_ref, fac_ref, low_ref, nrm_ref, inv_ref, *rest):
    vec = rest[-1]
    hidden = wt_ref.shape[0] // 5
    load_columns(vec, (gain_ref, layer), (bias_ref, layer), (chain_ref, layer))
    for t in range(z_ref.shape[0]):
        mask, same = flags_ref[t, 0:1, :], flags_ref[t, 1:2, :]
        normed, inv_ref[t], lowered = lower(z_ref[t].astype(F32), vec[0], vec[1])
        low_ref[t] = lowered
        nrm_ref[t] = normed.astype(BF16)
        part = project(lowered, wt_ref, 0, 3 + len(rest))
        for n in (0, 2):
            sig = sigmoid(part[n + 1]) * mask
            fac_ref[t, n * hidden : (n + 1) * hidden, :] = sig.astype(BF16)
            fac_ref[t, (n + 1) * hidden : (n + 2) * hidden, :] = (
                part[n] * sig * (1.0 - sig)
            ).astype(BF16)
        for gate_ref in rest[:-1]:
            gate_ref[t] = sigmoid(part[4] + same * vec[2]).astype(BF16)


def keep_product_kernel(cpd, q, prod_ref, nrm_ref, inv_ref):
    rows = q * cpd
    for t in range(nrm_ref.shape[0]):
        normed, inv_ref[t] = norm(unpack(prod_ref[:, t * rows : (t + 1) * rows, :], cpd))
        nrm_ref[t] = normed.astype(BF16)


def mix_edge_kernel(
    cpd, q, layer, prod_ref, z_ref, gate_ref, flags_ref, owt_ref, hgain_ref, hbias_ref, wt_ref,
    gain_ref, bias_ref, edges_ref, znext_ref, vec,
):
    tiles, _, lanes = z_ref.shape
    rows = q * cpd
    load_columns(vec, (hgain_ref, layer), (hbias_ref, layer), (gain_ref, layer + 1), (bias_ref, layer + 1))
    for t in range(tiles):
        here = slice(t * rows, (t + 1) * rows)
        hnormed, _ = norm(unpack(prod_ref[:, here, :], cpd))
        hscaled = (hnormed * vec[0] + vec[1]).astype(BF16)
        cells = z_ref[t].astype(F32) + gate_ref[t].astype(F32) * dot(owt_ref[...], hscaled, 1, 0)
        znext_ref[t] = cells
        emit_edges(
            edges_ref, here, cells, wt_ref, vec[2], vec[3], flags_ref[t, 0:1, :], cpd, lanes // q
        )


def mix_grad(upstream, hnormed, hinv, gate_ref, t, ow_ref, hgain):
    grad_mixed = (upstream * gate_ref[t].astype(F32)).astype(BF16)
    return norm_grad(dot(ow_ref[...], grad_mixed, 1, 0), hnormed, hinv, hgain)


def mix_back_kernel(cpd, q, layer, prod_ref, up_ref, gate_ref, ow_ref, hgain_ref, gp_ref, vec):
    tiles, _, lanes = up_ref.shape
    rows = q * cpd
    load_columns(vec, (hgain_ref, layer))
    for t in range(tiles):
        here = slice(t * rows, (t + 1) * rows)
        hnormed, hinv = norm(unpack(prod_ref[:, here, :], cpd))
        grad = mix_grad(up_ref[t].astype(F32), hnormed, hinv, gate_ref, t, ow_ref, vec[0])
        gp_ref[:, here, :] = pack(grad, cpd, lanes // q)


def mix_terms(upstream, product, gate, same, ow_ref, owt_ref, hgain, hbias, acc_ow, acc_hg, acc_hb, acc_ch):
    width = acc_hg.shape[1]
    hnormed, _ = norm(product)
    hscaled = (hnormed * hgain + hbias).astype(BF16)
    mixed = dot(owt_ref[...], hscaled, 1, 0)
    grad_gate = upstream * gate
    grad_logits = grad_gate * mixed * (1.0 - gate)
    grad_mixed = grad_gate.astype(BF16)
    acc_ow[...] += dot(hscaled, grad_mixed, 1, 1)
    grad_hscaled = dot(ow_ref[...], grad_mixed, 1, 0)
    acc_hg[...] += fold(grad_hscaled * hnormed, width)
    acc_hb[...] += fold(grad_hscaled, width)
    acc_ch[...] += fold(grad_logits * same, width)
    return grad_logits


def row_of(acc):
    return jnp.sum(acc.T, 0, keepdims=True)


def mix_terms_kernel(
    cpd, q, layer, prod_ref, up_ref, gate_ref, flags_ref, ow_ref, owt_ref, hgain_ref, hbias_ref,
    glog_ref, terms_ref, vec, acc_ow, acc_hg, acc_hb, acc_ch,
):
    rows = q * cpd
    load_columns(vec, (hgain_ref, layer), (hbias_ref, layer))
    clear(acc_ow, acc_hg, acc_hb, acc_ch)
    for t in range(up_ref.shape[0]):
        grad_logits = mix_terms(
            up_ref[t].astype(F32), unpack(prod_ref[:, t * rows : (t + 1) * rows, :], cpd),
            gate_ref[t].astype(F32), flags_ref[t, 1:2, :], ow_ref, owt_ref, vec[0], vec[1],
            acc_ow, acc_hg, acc_hb, acc_ch,
        )
        glog_ref[t] = grad_logits.astype(BF16)

    @last_step
    def _():
        hidden = acc_ow.shape[0]
        terms_ref[:hidden, :] = acc_ow[...]
        vectors = [row_of(acc_hg[...]), row_of(acc_hb[...]), row_of(acc_ch[...])]
        vectors.append(jnp.zeros((terms_ref.shape[0] - hidden - 3, hidden), F32))
        terms_ref[hidden:, :] = jnp.concatenate(vectors, 0)


def project_grad(left_ref, right_ref, fac_ref, glog_ref, t, cpd, rows):
    hidden = fac_ref.shape[1] // 4
    here = slice(t * rows, (t + 1) * rows)
    grads = (unpack(left_ref[:, here, :], cpd), unpack(right_ref[:, here, :], cpd))
    blocks = [
        (grads[n // 2] * fac_ref[t, n * hidden : (n + 1) * hidden, :].astype(F32)).astype(BF16)
        for n in range(4)
    ]
    return jnp.concatenate(blocks + [glog_ref[t]], 0)


def input_grad(gproj, nrm_ref, inv_ref, t, w_ref, gain):
    return norm_grad(dot(w_ref[...], gproj, 1, 0), nrm_ref[t].astype(F32), inv_ref[t], gain)


def edge_mix_back_kernel(
    cpd, q, layer, left_ref, right_ref, fac_ref, nrm_ref, inv_ref, glog_ref, up_ref, w_ref, gain_ref,
    hnrm_ref, hinv_ref, gate_ref, ow_ref, hgain_ref, upnext_ref, gp_ref, vec,
):
    tiles, _, lanes = up_ref.shape
    rows = q * cpd
    load_columns(vec, (gain_ref, layer), (hgain_ref, layer - 1))
    for t in range(tiles):
        gproj = project_grad(left_ref, right_ref, fac_ref, glog_ref, t, cpd, rows)
        upstream = up_ref[t].astype(F32) + input_grad(gproj, nrm_ref, inv_ref, t, w_ref, vec[0])
        upnext_ref[t] = upstream
        grad = mix_grad(upstream, hnrm_ref[t].astype(F32), hinv_ref[t], gate_ref, t, ow_ref, vec[1])
        gp_ref[:, t * rows : (t + 1) * rows, :] = pack(grad, cpd, lanes // q)


def edge_terms(gproj, low_ref, nrm_ref, t, acc_w):
    ones = jnp.ones((16, gproj.shape[1]), BF16)
    acc_w[...] += dot(jnp.concatenate([low_ref[t], nrm_ref[t], ones], 0), gproj, 1, 1)


def finish_edge(out_ref, acc_w, w_ref):
    width = w_ref.shape[0]
    for n in range(acc_w.shape[1] // width):
        out_ref[n * width : (n + 1) * width, :] = acc_w[:width, n * width : (n + 1) * width].astype(BF16)
    weight = w_ref[...].astype(F32)
    gain = row_of(fold(weight * acc_w[width : 2 * width, :], width))
    bias = row_of(fold(weight * acc_w[2 * width : 2 * width + 1, :], width))
    return [gain, bias]


def finish_rows(out_ref, first, vectors):
    pad = jnp.zeros((out_ref.shape[0] - first - sum(v.shape[0] for v in vectors), out_ref.shape[1]), F32)
    out_ref[first:, :] = jnp.concatenate(vectors + [pad], 0).astype(BF16)


def late_terms_kernel(
    cpd, q, layer, left_ref, right_ref, fac_ref, low_ref, nrm_ref, glog_ref, w_ref, terms_ref,
    prod_ref, up_ref, gate_ref, flags_ref, ow_ref, owt_ref, hgain_ref, hbias_ref,
    glognext_ref, all_ref, vec, acc_w, acc_ow, acc_hg, acc_hb, acc_ch,
):
    rows = q * cpd
    load_columns(vec, (hgain_ref, layer - 1), (hbias_ref, layer - 1))
    clear(acc_w, acc_ow, acc_hg, acc_hb, acc_ch)
    for t in range(up_ref.shape[0]):
        gproj = project_grad(left_ref, right_ref, fac_ref, glog_ref, t, cpd, rows)
        edge_terms(gproj, low_ref, nrm_ref, t, acc_w)
        grad_logits = mix_terms(
            up_ref[t], unpack(prod_ref[:, t * rows : (t + 1) * rows, :], cpd), gate_ref[t].astype(F32),
            flags_ref[t, 1:2, :], ow_ref, owt_ref, vec[0], vec[1], acc_ow, acc_hg, acc_hb, acc_ch,
        )
        glognext_ref[t] = grad_logits.astype(BF16)

    @last_step
    def _():
        hidden = acc_ow.shape[0]
        vectors = finish_edge(all_ref, acc_w, w_ref)
        all_ref[5 * hidden : 6 * hidden, :] = terms_ref[:hidden, :].astype(BF16)
        all_ref[6 * hidden : 7 * hidden, :] = acc_ow[...].astype(BF16)
        vectors += [terms_ref[hidden : hidden + 3, :]]
        vectors += [row_of(acc_hg[...]), row_of(acc_hb[...]), row_of(acc_ch[...])]
        finish_rows(all_ref, 7 * hidden, vectors)


def last_terms_kernel(
    cpd, q, left_ref, right_ref, fac_ref, low_ref, nrm_ref, glog_ref, w_ref, all_ref, acc_w,
):
    clear(acc_w)
    tiles = range(low_ref.shape[0])
    gproj = [project_grad(left_ref, right_ref, fac_ref, glog_ref, t, cpd, q * cpd) for t in tiles]
    ones = jnp.ones((16, low_ref.shape[2]), BF16)
    sides = [jnp.concatenate([low_ref[t], nrm_ref[t], ones], 0) for t in tiles]
    acc_w[...] += dot(jnp.concatenate(sides, 1), jnp.concatenate(gproj, 1), 1, 1)

    @last_step
    def _():
        finish_rows(all_ref, acc_w.shape[1], finish_edge(all_ref, acc_w, w_ref))


def pair_grad_kernel(
    cpd, q, layer, left_ref, right_ref, fac_ref, nrm_ref, inv_ref, glog_ref, up_ref, w_ref, gain_ref, pair_ref, vec,
):
    tiles, _, lanes = up_ref.shape
    cols = lanes // q
    load_columns(vec, (gain_ref, layer))
    for t in range(tiles):
        gproj = project_grad(left_ref, right_ref, fac_ref, glog_ref, t, cpd, q * cpd)
        upstream = up_ref[t] + input_grad(gproj, nrm_ref, inv_ref, t, w_ref, vec[0])
        for a in range(q):
            pair_ref[t * q + a] = upstream[:, a * cols : (a + 1) * cols].T.astype(BF16)


def spread_kernel(early_ref, late_ref, out_ref):
    early = jnp.sum(early_ref[...].astype(F32), 0).astype(BF16)
    late = jnp.sum(late_ref[...].astype(F32), 0).astype(BF16)
    out_ref[...] = jnp.broadcast_to(jnp.concatenate([early, late], 0)[None], out_ref.shape)


def unpack_kernel(factor, early_rows, got_ref, proj_ref, ow_ref, inorm_ref, hnorm_ref, chain_ref):
    width = ow_ref.shape[1]
    early = got_ref[:, :early_rows, :].astype(F32).reshape(-1, width) * factor
    late = got_ref[:, early_rows:, :].astype(F32).reshape(-1, width) * factor
    for n in range(5):
        rows, lanes = slice(n * width, (n + 1) * width), slice(n * width, (n + 1) * width)
        proj_ref[0, :, lanes] = late[rows]
        proj_ref[1, :, lanes] = early[rows]
    ow_ref[1] = early[5 * width : 6 * width]
    ow_ref[0] = early[6 * width : 7 * width]
    inorm_ref[0] = late[5 * width : 5 * width + 2]
    vectors = early[7 * width : 7 * width + 8]
    inorm_ref[1] = vectors[0:2]
    hnorm_ref[1] = vectors[2:4]
    hnorm_ref[0] = vectors[5:7]
    chain_ref[...] = jnp.concatenate([vectors[7:8], vectors[4:5]], 0)


def cell_call(kernel, steps, ins, outs, scratch, prefetch=(), flops=0, vmem=CELL_VMEM):
    def spec(shape, how):
        if how is None:
            return pl.BlockSpec(shape, lambda *s: (0,) * len(shape))
        axis, first, size = how if isinstance(how, tuple) else (how, 0, shape[how] // steps)
        block = tuple(size if n == axis else length for n, length in enumerate(shape))
        moves = shape[axis] >= size * steps
        return pl.BlockSpec(
            block,
            lambda *s: tuple((s[0] if moves else 0) + first if n == axis else 0 for n in range(len(shape))),
        )

    moved = sum(a.size * a.dtype.itemsize for a, _ in ins)
    moved += sum(functools.reduce(lambda x, y: x * y, s, 1) * jnp.dtype(t).itemsize for (s, t), _ in outs)
    return pl.pallas_call(
        kernel,
        grid_spec=pltpu.PrefetchScalarGridSpec(
            num_scalar_prefetch=len(prefetch),
            grid=(steps,),
            in_specs=[spec(a.shape, how) for a, how in ins],
            out_specs=[spec(s, how) for (s, _), how in outs],
            scratch_shapes=scratch,
        ),
        out_shape=[jax.ShapeDtypeStruct(s, t) for (s, t), _ in outs],
        compiler_params=pltpu.CompilerParams(vmem_limit_bytes=vmem),
        cost_estimate=pl.CostEstimate(flops=flops, bytes_accessed=int(moved), transcendentals=0),
    )(*prefetch, *[a for a, _ in ins])


def widen(src_ref, dst):
    devices, cols = src_ref.shape[0], src_ref.shape[-1]
    per = dst.shape[0] // devices
    for d in range(devices):
        dst[d * per : (d + 1) * per, :] = src_ref[d].astype(F32).reshape(per, cols)


def narrow(src, dst_ref):
    devices = dst_ref.shape[0]
    per = src.shape[0] // devices
    for d in range(devices):
        dst_ref[d, :per, :] = src[d * per : (d + 1) * per, :].astype(BF16)


def get_channel(src, ch, sub, subs, dims):
    row_devs, col_devs, rows, cpd, cols = dims
    halves = []
    for s in range(col_devs):
        parts = []
        for r in range(row_devs):
            base = ((r * col_devs + s) * subs + sub) * rows * cpd
            parts.append(src[pl.ds(base + ch, rows, stride=cpd), :])
        halves.append(jnp.concatenate(parts, 0))
    return jnp.concatenate(halves, 1).astype(BF16)


def put_channel(dst, value, ch, sub, subs, dims):
    row_devs, col_devs, rows, cpd, cols = dims
    for s in range(col_devs):
        for r in range(row_devs):
            base = ((r * col_devs + s) * subs + sub) * rows * cpd
            dst[pl.ds(base + ch, rows, stride=cpd), :] = value[
                r * rows : (r + 1) * rows, s * cols : (s + 1) * cols
            ]


def product_kernel(dims, outgoing, edges_ref, out_ref, edges, result):
    widen(edges_ref, edges)
    for ch in range(dims[3]):
        left = get_channel(edges, ch, 0, 2, dims)
        right = get_channel(edges, ch, 1, 2, dims)
        value = dot(left, right, 1, 1) if outgoing else dot(left, right, 0, 0)
        put_channel(result, value, ch, 0, 1, dims)
    narrow(result, out_ref)


def assemble_kernel(dims, edges_ref, out_ref, edges):
    widen(edges_ref, edges)
    for ch in range(dims[3]):
        for sub in range(2):
            out_ref[ch, sub] = get_channel(edges, ch, sub, 2, dims)


def product_grad_kernel(dims, outgoing, sides_ref, grad_ref, *rest):
    out_ref, grad, result = rest[-3:]
    widen(grad_ref, grad)
    for ch in range(dims[3]):
        left, right = sides_ref[ch, 0], sides_ref[ch, 1]
        gp = get_channel(grad, ch, 0, 1, dims)
        if outgoing:
            grad_left = dot(gp, right, 1, 0)
            grad_right = dot(gp, left, 0, 0)
        else:
            grad_left = dot(right, gp, 1, 1)
            grad_right = dot(left, gp, 1, 0)
        put_channel(result, grad_left, ch, 0, 2, dims)
        put_channel(result, grad_right, ch, 1, 2, dims)
    narrow(result, out_ref)
    for terms_ref in rest[:-3]:
        out_ref[:, out_ref.shape[1] - terms_ref.shape[1] :, :] = terms_ref[...]


def whole_call(kernel, ins, outs, scratch, flops):
    moved = sum(a.size * a.dtype.itemsize for a in ins)
    moved += sum(functools.reduce(lambda x, y: x * y, s, 1) * jnp.dtype(t).itemsize for s, t in outs)
    specs = [pl.BlockSpec(memory_space=pltpu.VMEM)] * len(outs)
    shapes = [jax.ShapeDtypeStruct(s, t) for s, t in outs]
    return pl.pallas_call(
        kernel,
        in_specs=[pl.BlockSpec(memory_space=pltpu.VMEM)] * len(ins),
        out_specs=specs if len(outs) > 1 else specs[0],
        out_shape=shapes if len(outs) > 1 else shapes[0],
        scratch_shapes=scratch,
        compiler_params=pltpu.CompilerParams(vmem_limit_bytes=CHANNEL_VMEM),
        cost_estimate=pl.CostEstimate(flops=flops, bytes_accessed=int(moved), transcendentals=0),
    )(*ins)


def exchange(array):
    return lax.all_to_all(array, AXES, split_axis=0, concat_axis=0, tiled=True)


def after(array, *others):
    return lax.optimization_barrier((array, *others))[0]


def shards(
    pair_rep, cotangent, residue_mask, chain_ids, proj_weight, out_weight,
    input_gain, input_bias, hidden_gain, hidden_bias, chain_bias,
):
    rows, cols, width = pair_rep.shape
    hidden = out_weight.shape[1]
    row_devs, col_devs = lax.axis_size("row"), lax.axis_size("col")
    devices = row_devs * col_devs
    length = rows * row_devs
    cpd = hidden // devices
    q = max(1, 16 // cpd)
    tiles = rows // q
    lanes = q * cols
    steps = max(1, tiles // 4)
    dims = (row_devs, col_devs, rows, cpd, cols)
    side = rows * cpd

    wt = [proj_weight[n].T for n in range(2)]
    owt = [out_weight[n].T for n in range(2)]
    weight = [proj_weight[n] for n in range(2)]
    mixer = [out_weight[n] for n in range(2)]
    mask_cols, chain_cols = residue_mask.reshape(col_devs, cols), chain_ids.reshape(col_devs, cols)
    scalars = (residue_mask, chain_ids)
    tile = (tiles, width, lanes)
    fac_tile = (tiles, 4 * hidden, lanes)
    edge_shape = (devices, 2, side, cols)
    cell_shape = (devices, side, cols)
    vec = lambda n: pltpu.VMEM((n, width, lanes), F32)
    acc = lambda n, m=width: pltpu.VMEM((m, n), F32)
    wide = lambda n: pltpu.VMEM((n * devices * side, cols), F32)
    cell_flops = 2 * rows * cols * width * hidden
    tri_flops = 2 * cpd * length**3
    rows_for = lambda n: -(-n // (devices * 16)) * 16
    early_rows, late_rows = rows_for(7 * hidden + 8), rows_for(5 * hidden + 2)
    terms_shape = (hidden + 8, hidden)

    def product(edges, outgoing):
        return whole_call(
            functools.partial(product_kernel, dims, outgoing), [edges], [(cell_shape, BF16)],
            [wide(2), wide(1)], tri_flops,
        )

    def assemble(edges):
        return whole_call(
            functools.partial(assemble_kernel, dims), [edges], [((cpd, 2, length, length), BF16)], [wide(2)], 0
        )

    def product_grad(sides, grad, outgoing, *terms):
        out_rows = 2 * side + sum(t.shape[1] for t in terms)
        return whole_call(
            functools.partial(product_grad_kernel, dims, outgoing), [sides, grad, *terms],
            [((devices, out_rows, cols), BF16)], [wide(1), wide(2)], 2 * tri_flops,
        )

    def halves(grads):
        per = side // steps
        return [(grads, (1, 0, per)), (grads, (1, steps, per))]

    def keep(layer, z, with_gate):
        norm_outs = [((tile, BF16), 0), ((tile, BF16), 0), (((tiles, 1, lanes), F32), 0)]
        return cell_call(
            functools.partial(keep_kernel, layer), steps,
            [
                (z, 0), (flags, 0), (wt[layer], None), (input_gain, None), (input_bias, None), (chain_bias, None),
            ],
            [((fac_tile, BF16), 0)] + norm_outs + [((tile, BF16), 0)] * with_gate,
            [vec(3)], flops=5 * cell_flops,
        )

    (edges0,) = cell_call(
        functools.partial(edge_first_kernel, cpd, q, rows), steps,
        [
            (pair_rep, 0), (mask_cols, None), (chain_cols, None), (proj_weight, (0, 0, 1)),
            (input_gain, None), (input_bias, None),
        ],
        [((edge_shape, BF16), 2)], [vec(2), pltpu.VMEM((5 * hidden, width), BF16)],
        prefetch=scalars, flops=4 * cell_flops, vmem=ALL_VMEM,
    )
    got0 = exchange(edges0)
    z0, up, gate0, flags = cell_call(
        functools.partial(first_keep_kernel, q, rows), steps,
        [
            (after(pair_rep, edges0), 0), (cotangent, 0), (mask_cols, None), (chain_cols, None), (wt[0], None),
            (input_gain, None), (input_bias, None), (chain_bias, None),
        ],
        [((tile, BF16), 0), ((tile, BF16), 0), ((tile, BF16), 0), (((tiles, 2, lanes), F32), 0)],
        [vec(3)], prefetch=scalars, flops=2 * cell_flops,
    )
    made0 = product(after(got0, z0), True)
    prod0 = exchange(made0)
    sides0 = assemble(after(got0, made0))
    edges1, z1 = cell_call(
        functools.partial(mix_edge_kernel, cpd, q, 0), steps,
        [
            (after(prod0, sides0), 1), (z0, 0), (gate0, 0), (flags, 0), (owt[0], None), (hidden_gain, None),
            (hidden_bias, None), (wt[1], None), (input_gain, None), (input_bias, None),
        ],
        [((edge_shape, BF16), 2), ((tile, F32), 0)], [vec(4)], flops=5 * cell_flops,
    )
    got1 = exchange(edges1)
    fac1, low1, nrm1, inv1, gate1 = keep(1, after(z1, edges1), True)
    made1 = product(after(got1, gate1), False)
    prod1 = exchange(made1)
    sides1 = assemble(after(got1, made1))

    (grad1,) = cell_call(
        functools.partial(mix_back_kernel, cpd, q, 1), steps,
        [(after(prod1, sides1), 1), (up, 0), (gate1, 0), (mixer[1], None), (hidden_gain, None)],
        [((cell_shape, BF16), 1)], [vec(1)], flops=cell_flops,
    )
    got_grad1 = exchange(grad1)
    hnrm0, hinv0 = cell_call(
        functools.partial(keep_product_kernel, cpd, q), steps, [(after(prod0, grad1), 1)],
        [((tile, BF16), 0), (((tiles, 1, lanes), F32), 0)], [],
    )
    made_grads1 = product_grad(sides1, after(got_grad1, hnrm0), False)
    grads1 = exchange(made_grads1)
    glog1, terms1 = cell_call(
        functools.partial(mix_terms_kernel, cpd, q, 1), steps,
        [
            (after(prod1, made_grads1), 1), (up, 0), (gate1, 0), (flags, 0), (mixer[1], None), (owt[1], None),
            (hidden_gain, None), (hidden_bias, None),
        ],
        [((tile, BF16), 0), ((terms_shape, F32), None)],
        [vec(2), acc(hidden), acc(cols), acc(cols), acc(cols)], flops=3 * cell_flops,
    )
    up0, grad0 = cell_call(
        functools.partial(edge_mix_back_kernel, cpd, q, 1), steps,
        halves(after(grads1, glog1))
        + [
            (fac1, 0), (nrm1, 0), (inv1, 0), (glog1, 0), (up, 0), (weight[1], None), (input_gain, None),
            (hnrm0, 0), (hinv0, 0), (gate0, 0), (mixer[0], None), (hidden_gain, None),
        ],
        [((tile, F32), 0), ((cell_shape, BF16), 1)],
        [vec(2)], flops=6 * cell_flops,
    )
    got_grad0 = exchange(grad0)
    glog0, early = cell_call(
        functools.partial(late_terms_kernel, cpd, q, 1), steps,
        halves(after(grads1, grad0))
        + [
            (fac1, 0), (low1, 0), (nrm1, 0), (glog1, 0), (weight[1], None), (terms1, None), (prod0, 1),
            (up0, 0), (gate0, 0), (flags, 0), (mixer[0], None), (owt[0], None), (hidden_gain, None),
            (hidden_bias, None),
        ],
        [((tile, BF16), 0), (((devices * early_rows, hidden), BF16), None)],
        [vec(2), acc(5 * hidden, 2 * width + 16), acc(hidden), acc(cols), acc(cols), acc(cols)],
        flops=13 * cell_flops,
    )

    made_grads0 = product_grad(sides0, got_grad0, True, early.reshape(devices, early_rows, hidden))
    grads0 = exchange(made_grads0)
    fac0, low0, nrm0, inv0 = keep(0, after(z0, made_grads0), False)
    grads0 = after(grads0, nrm0)
    (late,) = cell_call(
        functools.partial(last_terms_kernel, cpd, q), steps,
        halves(grads0) + [(fac0, 0), (low0, 0), (nrm0, 0), (glog0, 0), (weight[0], None)],
        [(((devices * late_rows, hidden), BF16), None)],
        [acc(5 * hidden, 2 * width + 16)], flops=10 * cell_flops, vmem=ALL_VMEM,
    )
    got_late = exchange(late.reshape(devices, late_rows, hidden))
    (grad_pair,) = cell_call(
        functools.partial(pair_grad_kernel, cpd, q, 0), steps,
        halves(after(grads0, late))
        + [(fac0, 0), (nrm0, 0), (inv0, 0), (glog0, 0), (up0, 0), (weight[0], None), (input_gain, None)],
        [((pair_rep.shape, BF16), 0)], [vec(1)], flops=5 * cell_flops, vmem=ALL_VMEM,
    )
    (spread,) = cell_call(
        spread_kernel, 1,
        [(grads0, (1, 2 * side // early_rows, early_rows)), (after(got_late, grad_pair), None)],
        [(((devices, early_rows + late_rows, hidden), BF16), None)], [], vmem=ALL_VMEM,
    )
    proj, out, inorm, hnorm, chain = whole_call(
        functools.partial(unpack_kernel, 1.0 / length, early_rows), [exchange(spread)],
        [
            ((2, width, 5 * hidden), F32), ((2, hidden, hidden), F32), ((2, 2, hidden), F32),
            ((2, 2, hidden), F32), ((2, hidden), F32),
        ],
        [], 0,
    )
    return grad_pair, proj, out, inorm, hnorm, chain


def solution(mesh):
    cells = P(("grp", "row"), "col", None)
    return jax.shard_map(
        shards,
        mesh=mesh,
        in_specs=(cells, cells, P("grp"), P("grp")) + (P(),) * 7,
        out_specs=(
            cells, P("grp", None, None), P("grp", None, None), P("grp", None, None),
            P("grp", None, None), P("grp", None),
        ),
        check_vma=False,
    )
```

```python
import functools

import jax
import jax.numpy as jnp
from jax import lax
from jax.experimental import pallas as pl
from jax.experimental.pallas import tpu as pltpu
from jax.sharding import PartitionSpec as P

EPSILON = 1e-05
AXES = ("row", "col")
F32 = jnp.float32
BF16 = jnp.bfloat16
CHANNEL_VMEM = 50 * 1024 * 1024
CELL_VMEM = 50 * 1024 * 1024
ALL_VMEM = 60 * 1024 * 1024


def dot(a, b, ca, cb):
    return lax.dot_general(a, b, (((ca,), (cb,)), ((), ())), preferred_element_type=F32)


def sigmoid(x):
    return 0.5 * jnp.tanh(0.5 * x) + 0.5


def columns(vectors, width):
    c = vectors.shape[1]
    square = jnp.broadcast_to(vectors, (c, c)).T
    return jnp.concatenate([square] * (width // c), 1)


def norm(x):
    centred = x - jnp.mean(x, 0, keepdims=True)
    inv = lax.rsqrt(jnp.mean(centred * centred, 0, keepdims=True) + EPSILON)
    return centred * inv, inv


def norm_grad(grad_scaled, normed, inv, gain):
    g = grad_scaled * gain
    first = jnp.mean(g, 0, keepdims=True)
    second = jnp.mean(g * normed, 0, keepdims=True)
    return (g - first - normed * second) * inv


def unpack(block, cpd):
    devices, rows, cols = block.shape
    values = block.astype(F32)
    parts = []
    for a in range(rows // cpd):
        if cpd % 8 == 0:
            parts.append(values[:, a * cpd : (a + 1) * cpd, :].reshape(devices * cpd, cols))
        else:
            parts.append(
                jnp.concatenate([values[d, a * cpd : (a + 1) * cpd, :] for d in range(devices)], 0)
            )
    return jnp.concatenate(parts, 1)


def pack(tile, cpd, cols):
    channels, lanes = tile.shape
    devices = channels // cpd
    parts = [tile[:, a * cols : (a + 1) * cols] for a in range(lanes // cols)]
    if cpd % 8 == 0:
        return jnp.concatenate([p.reshape(devices, cpd, cols) for p in parts], 1).astype(BF16)
    return jnp.stack(
        [
            jnp.concatenate([p[d * cpd : (d + 1) * cpd, :] for p in parts], 0)
            for d in range(devices)
        ]
    ).astype(BF16)


def fold(tile, width):
    return sum(tile[:, a : a + width] for a in range(0, tile.shape[1], width))


def project(lowered, wt_ref, first, last):
    hidden = lowered.shape[0]
    projected = dot(wt_ref[first * hidden : last * hidden, :], lowered, 1, 0)
    return [projected[n * hidden : (n + 1) * hidden] for n in range(last - first)]


def lower(cells, gain, bias):
    normed, inv = norm(cells)
    return normed, inv, (normed * gain + bias).astype(BF16)


def emit_edges(edges_ref, here, cells, wt_ref, gain, bias, mask, cpd, cols):
    part = project(lower(cells, gain, bias)[2], wt_ref, 0, 4)
    edges_ref[:, 0, here, :] = pack(part[0] * sigmoid(part[1]) * mask, cpd, cols)
    edges_ref[:, 1, here, :] = pack(part[2] * sigmoid(part[3]) * mask, cpd, cols)


def first_step(fill):
    pl.when(pl.program_id(0) == 0)(fill)


def last_step(fill):
    pl.when(pl.program_id(0) == pl.num_programs(0) - 1)(fill)


def load_columns(vec, *rows):
    @first_step
    def _():
        for n, (ref, layer) in enumerate(rows):
            vec[n] = columns(ref[layer : layer + 1, :], vec.shape[2])


def clear(*accs):
    @first_step
    def _():
        for acc in accs:
            acc[...] = jnp.zeros_like(acc)


def turned(ref, t, q):
    return jnp.concatenate([ref[t * q + a].astype(F32).T for a in range(q)], 1)


def row_flags(row, device_rows, mask_smem, chain_smem, maskc_ref, chainc_ref):
    whole = lax.axis_index("row") * device_rows + row
    here = pl.ds(lax.axis_index("col"), 1)
    mask = (maskc_ref[here, :] * mask_smem[whole]).astype(F32)
    return mask, (chainc_ref[here, :] == chain_smem[whole]).astype(F32)


def edge_first_kernel(
    cpd, q, device_rows, mask_smem, chain_smem, pair_ref, maskc_ref, chainc_ref, w_ref, gain_ref, bias_ref,
    edges_ref, vec, turned_weight,
):
    rows, cols, width = pair_ref.shape
    load_columns(vec, (gain_ref, 0), (bias_ref, 0))

    @first_step
    def _():
        for n in range(turned_weight.shape[0] // width):
            block = slice(n * width, (n + 1) * width)
            turned_weight[block, :] = w_ref[0, :, block].astype(F32).T.astype(BF16)

    for t in range(rows // q):
        first = pl.program_id(0) * rows + t * q
        mask = jnp.concatenate(
            [
                row_flags(first + a, device_rows, mask_smem, chain_smem, maskc_ref, chainc_ref)[0]
                for a in range(q)
            ],
            1,
        )
        here = slice(t * q * cpd, (t + 1) * q * cpd)
        emit_edges(edges_ref, here, turned(pair_ref, t, q), turned_weight, vec[0], vec[1], mask, cpd, cols)


def first_keep_kernel(
    q, device_rows, mask_smem, chain_smem, pair_ref, cot_ref, maskc_ref, chainc_ref, wt_ref, gain_ref,
    bias_ref, chain_ref, z_ref, up_ref, gate_ref, flags_ref, vec,
):
    load_columns(vec, (gain_ref, 0), (bias_ref, 0), (chain_ref, 0))
    tiles = z_ref.shape[0]
    for t in range(tiles):
        flags = [
            row_flags(
                (pl.program_id(0) * tiles + t) * q + a, device_rows, mask_smem, chain_smem, maskc_ref, chainc_ref
            )
            for a in range(q)
        ]
        mask = jnp.concatenate([f[0] for f in flags], 1)
        same = jnp.concatenate([f[1] for f in flags], 1)
        cells = turned(pair_ref, t, q)
        z_ref[t] = cells.astype(BF16)
        up_ref[t] = turned(cot_ref, t, q).astype(BF16)
        flags_ref[t] = jnp.concatenate([mask, same], 0)
        (logits,) = project(lower(cells, vec[0], vec[1])[2], wt_ref, 4, 5)
        gate_ref[t] = sigmoid(logits + same * vec[2]).astype(BF16)


def keep_kernel(layer, z_ref, flags_ref, wt_ref, gain_ref, bias_ref, chain_ref, fac_ref, low_ref, nrm_ref, inv_ref, *rest):
    vec = rest[-1]
    hidden = wt_ref.shape[0] // 5
    load_columns(vec, (gain_ref, layer), (bias_ref, layer), (chain_ref, layer))
    for t in range(z_ref.shape[0]):
        mask, same = flags_ref[t, 0:1, :], flags_ref[t, 1:2, :]
        normed, inv_ref[t], lowered = lower(z_ref[t].astype(F32), vec[0], vec[1])
        low_ref[t] = lowered
        nrm_ref[t] = normed.astype(BF16)
        part = project(lowered, wt_ref, 0, 3 + len(rest))
        for n in (0, 2):
            sig = sigmoid(part[n + 1]) * mask
            fac_ref[t, n * hidden : (n + 1) * hidden, :] = sig.astype(BF16)
            fac_ref[t, (n + 1) * hidden : (n + 2) * hidden, :] = (
                part[n] * sig * (1.0 - sig)
            ).astype(BF16)
        for gate_ref in rest[:-1]:
            gate_ref[t] = sigmoid(part[4] + same * vec[2]).astype(BF16)


def keep_product_kernel(cpd, q, prod_ref, nrm_ref, inv_ref):
    rows = q * cpd
    for t in range(nrm_ref.shape[0]):
        normed, inv_ref[t] = norm(unpack(prod_ref[:, t * rows : (t + 1) * rows, :], cpd))
        nrm_ref[t] = normed.astype(BF16)


def mix_edge_kernel(
    cpd, q, layer, prod_ref, z_ref, gate_ref, flags_ref, owt_ref, hgain_ref, hbias_ref, wt_ref,
    gain_ref, bias_ref, edges_ref, znext_ref, vec,
):
    tiles, _, lanes = z_ref.shape
    rows = q * cpd
    load_columns(vec, (hgain_ref, layer), (hbias_ref, layer), (gain_ref, layer + 1), (bias_ref, layer + 1))
    for t in range(tiles):
        here = slice(t * rows, (t + 1) * rows)
        hnormed, _ = norm(unpack(prod_ref[:, here, :], cpd))
        hscaled = (hnormed * vec[0] + vec[1]).astype(BF16)
        cells = z_ref[t].astype(F32) + gate_ref[t].astype(F32) * dot(owt_ref[...], hscaled, 1, 0)
        znext_ref[t] = cells
        emit_edges(
            edges_ref, here, cells, wt_ref, vec[2], vec[3], flags_ref[t, 0:1, :], cpd, lanes // q
        )


def mix_grad(upstream, hnormed, hinv, gate_ref, t, ow_ref, hgain):
    grad_mixed = (upstream * gate_ref[t].astype(F32)).astype(BF16)
    return norm_grad(dot(ow_ref[...], grad_mixed, 1, 0), hnormed, hinv, hgain)


def mix_back_kernel(cpd, q, layer, prod_ref, up_ref, gate_ref, ow_ref, hgain_ref, gp_ref, vec):
    tiles, _, lanes = up_ref.shape
    rows = q * cpd
    load_columns(vec, (hgain_ref, layer))
    for t in range(tiles):
        here = slice(t * rows, (t + 1) * rows)
        hnormed, hinv = norm(unpack(prod_ref[:, here, :], cpd))
        grad = mix_grad(up_ref[t].astype(F32), hnormed, hinv, gate_ref, t, ow_ref, vec[0])
        gp_ref[:, here, :] = pack(grad, cpd, lanes // q)


def mix_terms(upstream, product, gate, same, ow_ref, owt_ref, hgain, hbias, acc_ow, acc_hg, acc_hb, acc_ch):
    width = acc_hg.shape[1]
    hnormed, _ = norm(product)
    hscaled = (hnormed * hgain + hbias).astype(BF16)
    mixed = dot(owt_ref[...], hscaled, 1, 0)
    grad_gate = upstream * gate
    grad_logits = grad_gate * mixed * (1.0 - gate)
    grad_mixed = grad_gate.astype(BF16)
    acc_ow[...] += dot(hscaled, grad_mixed, 1, 1)
    grad_hscaled = dot(ow_ref[...], grad_mixed, 1, 0)
    acc_hg[...] += fold(grad_hscaled * hnormed, width)
    acc_hb[...] += fold(grad_hscaled, width)
    acc_ch[...] += fold(grad_logits * same, width)
    return grad_logits


def row_of(acc):
    return jnp.sum(acc.T, 0, keepdims=True)


def mix_terms_kernel(
    cpd, q, layer, prod_ref, up_ref, gate_ref, flags_ref, ow_ref, owt_ref, hgain_ref, hbias_ref,
    glog_ref, terms_ref, vec, acc_ow, acc_hg, acc_hb, acc_ch,
):
    rows = q * cpd
    load_columns(vec, (hgain_ref, layer), (hbias_ref, layer))
    clear(acc_ow, acc_hg, acc_hb, acc_ch)
    for t in range(up_ref.shape[0]):
        grad_logits = mix_terms(
            up_ref[t].astype(F32), unpack(prod_ref[:, t * rows : (t + 1) * rows, :], cpd),
            gate_ref[t].astype(F32), flags_ref[t, 1:2, :], ow_ref, owt_ref, vec[0], vec[1],
            acc_ow, acc_hg, acc_hb, acc_ch,
        )
        glog_ref[t] = grad_logits.astype(BF16)

    @last_step
    def _():
        hidden = acc_ow.shape[0]
        terms_ref[:hidden, :] = acc_ow[...]
        vectors = [row_of(acc_hg[...]), row_of(acc_hb[...]), row_of(acc_ch[...])]
        vectors.append(jnp.zeros((terms_ref.shape[0] - hidden - 3, hidden), F32))
        terms_ref[hidden:, :] = jnp.concatenate(vectors, 0)


def project_grad(left_ref, right_ref, fac_ref, glog_ref, t, cpd, rows):
    hidden = fac_ref.shape[1] // 4
    here = slice(t * rows, (t + 1) * rows)
    grads = (unpack(left_ref[:, here, :], cpd), unpack(right_ref[:, here, :], cpd))
    blocks = [
        (grads[n // 2] * fac_ref[t, n * hidden : (n + 1) * hidden, :].astype(F32)).astype(BF16)
        for n in range(4)
    ]
    return jnp.concatenate(blocks + [glog_ref[t]], 0)


def input_grad(gproj, nrm_ref, inv_ref, t, w_ref, gain):
    return norm_grad(dot(w_ref[...], gproj, 1, 0), nrm_ref[t].astype(F32), inv_ref[t], gain)


def edge_mix_back_kernel(
    cpd, q, layer, left_ref, right_ref, fac_ref, nrm_ref, inv_ref, glog_ref, up_ref, w_ref, gain_ref,
    hnrm_ref, hinv_ref, gate_ref, ow_ref, hgain_ref, upnext_ref, gp_ref, vec,
):
    tiles, _, lanes = up_ref.shape
    rows = q * cpd
    load_columns(vec, (gain_ref, layer), (hgain_ref, layer - 1))
    for t in range(tiles):
        gproj = project_grad(left_ref, right_ref, fac_ref, glog_ref, t, cpd, rows)
        upstream = up_ref[t].astype(F32) + input_grad(gproj, nrm_ref, inv_ref, t, w_ref, vec[0])
        upnext_ref[t] = upstream
        grad = mix_grad(upstream, hnrm_ref[t].astype(F32), hinv_ref[t], gate_ref, t, ow_ref, vec[1])
        gp_ref[:, t * rows : (t + 1) * rows, :] = pack(grad, cpd, lanes // q)


def edge_terms(gproj, low_ref, nrm_ref, t, acc_w):
    ones = jnp.ones((16, gproj.shape[1]), BF16)
    acc_w[...] += dot(jnp.concatenate([low_ref[t], nrm_ref[t], ones], 0), gproj, 1, 1)


def finish_edge(out_ref, acc_w, w_ref):
    width = w_ref.shape[0]
    for n in range(acc_w.shape[1] // width):
        out_ref[n * width : (n + 1) * width, :] = acc_w[:width, n * width : (n + 1) * width].astype(BF16)
    weight = w_ref[...].astype(F32)
    gain = row_of(fold(weight * acc_w[width : 2 * width, :], width))
    bias = row_of(fold(weight * acc_w[2 * width : 2 * width + 1, :], width))
    return [gain, bias]


def finish_rows(out_ref, first, vectors):
    pad = jnp.zeros((out_ref.shape[0] - first - sum(v.shape[0] for v in vectors), out_ref.shape[1]), F32)
    out_ref[first:, :] = jnp.concatenate(vectors + [pad], 0).astype(BF16)


def late_terms_kernel(
    cpd, q, layer, left_ref, right_ref, fac_ref, low_ref, nrm_ref, glog_ref, w_ref, terms_ref,
    prod_ref, up_ref, gate_ref, flags_ref, ow_ref, owt_ref, hgain_ref, hbias_ref,
    glognext_ref, all_ref, vec, acc_w, acc_ow, acc_hg, acc_hb, acc_ch,
):
    rows = q * cpd
    load_columns(vec, (hgain_ref, layer - 1), (hbias_ref, layer - 1))
    clear(acc_w, acc_ow, acc_hg, acc_hb, acc_ch)
    for t in range(up_ref.shape[0]):
        gproj = project_grad(left_ref, right_ref, fac_ref, glog_ref, t, cpd, rows)
        edge_terms(gproj, low_ref, nrm_ref, t, acc_w)
        grad_logits = mix_terms(
            up_ref[t], unpack(prod_ref[:, t * rows : (t + 1) * rows, :], cpd), gate_ref[t].astype(F32),
            flags_ref[t, 1:2, :], ow_ref, owt_ref, vec[0], vec[1], acc_ow, acc_hg, acc_hb, acc_ch,
        )
        glognext_ref[t] = grad_logits.astype(BF16)

    @last_step
    def _():
        hidden = acc_ow.shape[0]
        vectors = finish_edge(all_ref, acc_w, w_ref)
        all_ref[5 * hidden : 6 * hidden, :] = terms_ref[:hidden, :].astype(BF16)
        all_ref[6 * hidden : 7 * hidden, :] = acc_ow[...].astype(BF16)
        vectors += [terms_ref[hidden : hidden + 3, :]]
        vectors += [row_of(acc_hg[...]), row_of(acc_hb[...]), row_of(acc_ch[...])]
        finish_rows(all_ref, 7 * hidden, vectors)


def last_terms_kernel(
    cpd, q, left_ref, right_ref, fac_ref, low_ref, nrm_ref, glog_ref, w_ref, all_ref, acc_w,
):
    clear(acc_w)
    tiles = range(low_ref.shape[0])
    gproj = [project_grad(left_ref, right_ref, fac_ref, glog_ref, t, cpd, q * cpd) for t in tiles]
    ones = jnp.ones((16, low_ref.shape[2]), BF16)
    sides = [jnp.concatenate([low_ref[t], nrm_ref[t], ones], 0) for t in tiles]
    acc_w[...] += dot(jnp.concatenate(sides, 1), jnp.concatenate(gproj, 1), 1, 1)

    @last_step
    def _():
        finish_rows(all_ref, acc_w.shape[1], finish_edge(all_ref, acc_w, w_ref))


def pair_grad_kernel(
    cpd, q, layer, left_ref, right_ref, fac_ref, nrm_ref, inv_ref, glog_ref, up_ref, w_ref, gain_ref, pair_ref, vec,
):
    tiles, _, lanes = up_ref.shape
    cols = lanes // q
    load_columns(vec, (gain_ref, layer))
    for t in range(tiles):
        gproj = project_grad(left_ref, right_ref, fac_ref, glog_ref, t, cpd, q * cpd)
        upstream = up_ref[t] + input_grad(gproj, nrm_ref, inv_ref, t, w_ref, vec[0])
        for a in range(q):
            pair_ref[t * q + a] = upstream[:, a * cols : (a + 1) * cols].T.astype(BF16)


def spread_kernel(early_ref, late_ref, out_ref):
    early = jnp.sum(early_ref[...].astype(F32), 0).astype(BF16)
    late = jnp.sum(late_ref[...].astype(F32), 0).astype(BF16)
    out_ref[...] = jnp.broadcast_to(jnp.concatenate([early, late], 0)[None], out_ref.shape)


def unpack_kernel(factor, early_rows, got_ref, proj_ref, ow_ref, inorm_ref, hnorm_ref, chain_ref):
    width = ow_ref.shape[1]
    early = got_ref[:, :early_rows, :].astype(F32).reshape(-1, width) * factor
    late = got_ref[:, early_rows:, :].astype(F32).reshape(-1, width) * factor
    for n in range(5):
        rows, lanes = slice(n * width, (n + 1) * width), slice(n * width, (n + 1) * width)
        proj_ref[0, :, lanes] = late[rows]
        proj_ref[1, :, lanes] = early[rows]
    ow_ref[1] = early[5 * width : 6 * width]
    ow_ref[0] = early[6 * width : 7 * width]
    inorm_ref[0] = late[5 * width : 5 * width + 2]
    vectors = early[7 * width : 7 * width + 8]
    inorm_ref[1] = vectors[0:2]
    hnorm_ref[1] = vectors[2:4]
    hnorm_ref[0] = vectors[5:7]
    chain_ref[...] = jnp.concatenate([vectors[7:8], vectors[4:5]], 0)


def cell_call(kernel, steps, ins, outs, scratch, prefetch=(), flops=0, vmem=CELL_VMEM):
    def spec(shape, how):
        if how is None:
            return pl.BlockSpec(shape, lambda *s: (0,) * len(shape))
        axis, first, size = how if isinstance(how, tuple) else (how, 0, shape[how] // steps)
        block = tuple(size if n == axis else length for n, length in enumerate(shape))
        moves = shape[axis] >= size * steps
        return pl.BlockSpec(
            block,
            lambda *s: tuple((s[0] if moves else 0) + first if n == axis else 0 for n in range(len(shape))),
        )

    moved = sum(a.size * a.dtype.itemsize for a, _ in ins)
    moved += sum(functools.reduce(lambda x, y: x * y, s, 1) * jnp.dtype(t).itemsize for (s, t), _ in outs)
    return pl.pallas_call(
        kernel,
        grid_spec=pltpu.PrefetchScalarGridSpec(
            num_scalar_prefetch=len(prefetch),
            grid=(steps,),
            in_specs=[spec(a.shape, how) for a, how in ins],
            out_specs=[spec(s, how) for (s, _), how in outs],
            scratch_shapes=scratch,
        ),
        out_shape=[jax.ShapeDtypeStruct(s, t) for (s, t), _ in outs],
        compiler_params=pltpu.CompilerParams(vmem_limit_bytes=vmem),
        cost_estimate=pl.CostEstimate(flops=flops, bytes_accessed=int(moved), transcendentals=0),
    )(*prefetch, *[a for a, _ in ins])


def widen(src_ref, dst):
    devices, cols = src_ref.shape[0], src_ref.shape[-1]
    per = dst.shape[0] // devices
    for d in range(devices):
        dst[d * per : (d + 1) * per, :] = src_ref[d].astype(F32).reshape(per, cols)


def narrow(src, dst_ref):
    devices = dst_ref.shape[0]
    per = src.shape[0] // devices
    for d in range(devices):
        dst_ref[d, :per, :] = src[d * per : (d + 1) * per, :].astype(BF16)


def get_channel(src, ch, sub, subs, dims):
    row_devs, col_devs, rows, cpd, cols = dims
    halves = []
    for s in range(col_devs):
        parts = []
        for r in range(row_devs):
            base = ((r * col_devs + s) * subs + sub) * rows * cpd
            parts.append(src[pl.ds(base + ch, rows, stride=cpd), :])
        halves.append(jnp.concatenate(parts, 0))
    return jnp.concatenate(halves, 1).astype(BF16)


def put_channel(dst, value, ch, sub, subs, dims):
    row_devs, col_devs, rows, cpd, cols = dims
    for s in range(col_devs):
        for r in range(row_devs):
            base = ((r * col_devs + s) * subs + sub) * rows * cpd
            dst[pl.ds(base + ch, rows, stride=cpd), :] = value[
                r * rows : (r + 1) * rows, s * cols : (s + 1) * cols
            ]


def product_kernel(dims, outgoing, edges_ref, out_ref, edges, result):
    widen(edges_ref, edges)
    for ch in range(dims[3]):
        left = get_channel(edges, ch, 0, 2, dims)
        right = get_channel(edges, ch, 1, 2, dims)
        value = dot(left, right, 1, 1) if outgoing else dot(left, right, 0, 0)
        put_channel(result, value, ch, 0, 1, dims)
    narrow(result, out_ref)


def assemble_kernel(dims, edges_ref, out_ref, edges):
    widen(edges_ref, edges)
    for ch in range(dims[3]):
        for sub in range(2):
            out_ref[ch, sub] = get_channel(edges, ch, sub, 2, dims)


def product_grad_kernel(dims, outgoing, sides_ref, grad_ref, *rest):
    out_ref, grad, result = rest[-3:]
    widen(grad_ref, grad)
    for ch in range(dims[3]):
        left, right = sides_ref[ch, 0], sides_ref[ch, 1]
        gp = get_channel(grad, ch, 0, 1, dims)
        if outgoing:
            grad_left = dot(gp, right, 1, 0)
            grad_right = dot(gp, left, 0, 0)
        else:
            grad_left = dot(right, gp, 1, 1)
            grad_right = dot(left, gp, 1, 0)
        put_channel(result, grad_left, ch, 0, 2, dims)
        put_channel(result, grad_right, ch, 1, 2, dims)
    narrow(result, out_ref)
    for terms_ref in rest[:-3]:
        out_ref[:, out_ref.shape[1] - terms_ref.shape[1] :, :] = terms_ref[...]


def whole_call(kernel, ins, outs, scratch, flops, vmem=CHANNEL_VMEM):
    moved = sum(a.size * a.dtype.itemsize for a in ins)
    moved += sum(functools.reduce(lambda x, y: x * y, s, 1) * jnp.dtype(t).itemsize for s, t in outs)
    specs = [pl.BlockSpec(memory_space=pltpu.VMEM)] * len(outs)
    shapes = [jax.ShapeDtypeStruct(s, t) for s, t in outs]
    return pl.pallas_call(
        kernel,
        in_specs=[pl.BlockSpec(memory_space=pltpu.VMEM)] * len(ins),
        out_specs=specs if len(outs) > 1 else specs[0],
        out_shape=shapes if len(outs) > 1 else shapes[0],
        scratch_shapes=scratch,
        compiler_params=pltpu.CompilerParams(vmem_limit_bytes=vmem),
        cost_estimate=pl.CostEstimate(flops=flops, bytes_accessed=int(moved), transcendentals=0),
    )(*ins)


def exchange(array):
    return lax.all_to_all(array, AXES, split_axis=0, concat_axis=0, tiled=True)


def after(array, *others):
    return lax.optimization_barrier((array, *others))[0]


def shards(
    pair_rep, cotangent, residue_mask, chain_ids, proj_weight, out_weight,
    input_gain, input_bias, hidden_gain, hidden_bias, chain_bias,
):
    rows, cols, width = pair_rep.shape
    hidden = out_weight.shape[1]
    row_devs, col_devs = lax.axis_size("row"), lax.axis_size("col")
    devices = row_devs * col_devs
    length = rows * row_devs
    cpd = hidden // devices
    q = max(1, 16 // cpd)
    tiles = rows // q
    lanes = q * cols
    steps = max(1, tiles // 4)
    dims = (row_devs, col_devs, rows, cpd, cols)
    side = rows * cpd

    wt = [proj_weight[n].T for n in range(2)]
    owt = [out_weight[n].T for n in range(2)]
    weight = [proj_weight[n] for n in range(2)]
    mixer = [out_weight[n] for n in range(2)]
    mask_cols, chain_cols = residue_mask.reshape(col_devs, cols), chain_ids.reshape(col_devs, cols)
    scalars = (residue_mask, chain_ids)
    tile = (tiles, width, lanes)
    fac_tile = (tiles, 4 * hidden, lanes)
    edge_shape = (devices, 2, side, cols)
    cell_shape = (devices, side, cols)
    vec = lambda n: pltpu.VMEM((n, width, lanes), F32)
    acc = lambda n, m=width: pltpu.VMEM((m, n), F32)
    wide = lambda n: pltpu.VMEM((n * devices * side, cols), F32)
    cell_flops = 2 * rows * cols * width * hidden
    tri_flops = 2 * cpd * length**3
    rows_for = lambda n: -(-n // (devices * 16)) * 16
    early_rows, late_rows = rows_for(7 * hidden + 8), rows_for(5 * hidden + 2)
    terms_shape = (hidden + 8, hidden)

    def product(edges, outgoing):
        return whole_call(
            functools.partial(product_kernel, dims, outgoing), [edges], [(cell_shape, BF16)],
            [wide(2), wide(1)], tri_flops,
        )

    def assemble(edges):
        return whole_call(
            functools.partial(assemble_kernel, dims), [edges], [((cpd, 2, length, length), BF16)], [wide(2)], 0
        )

    def product_grad(sides, grad, outgoing, *terms):
        out_rows = 2 * side + sum(t.shape[1] for t in terms)
        return whole_call(
            functools.partial(product_grad_kernel, dims, outgoing), [sides, grad, *terms],
            [((devices, out_rows, cols), BF16)], [wide(1), wide(2)], 2 * tri_flops, 24 * 1024 * 1024,
        )

    def halves(grads):
        per = side // steps
        return [(grads, (1, 0, per)), (grads, (1, steps, per))]

    def keep(layer, z, with_gate):
        norm_outs = [((tile, BF16), 0), ((tile, BF16), 0), (((tiles, 1, lanes), F32), 0)]
        return cell_call(
            functools.partial(keep_kernel, layer), steps,
            [
                (z, 0), (flags, 0), (wt[layer], None), (input_gain, None), (input_bias, None), (chain_bias, None),
            ],
            [((fac_tile, BF16), 0)] + norm_outs + [((tile, BF16), 0)] * with_gate,
            [vec(3)], flops=5 * cell_flops,
        )

    (edges0,) = cell_call(
        functools.partial(edge_first_kernel, cpd, q, rows), steps,
        [
            (pair_rep, 0), (mask_cols, None), (chain_cols, None), (proj_weight, (0, 0, 1)),
            (input_gain, None), (input_bias, None),
        ],
        [((edge_shape, BF16), 2)], [vec(2), pltpu.VMEM((4 * hidden, width), BF16)],
        prefetch=scalars, flops=4 * cell_flops, vmem=ALL_VMEM,
    )
    got0 = exchange(edges0)
    z0, up, gate0, flags = cell_call(
        functools.partial(first_keep_kernel, q, rows), steps,
        [
            (after(pair_rep, edges0), 0), (cotangent, 0), (mask_cols, None), (chain_cols, None), (wt[0], None),
            (input_gain, None), (input_bias, None), (chain_bias, None),
        ],
        [((tile, BF16), 0), ((tile, BF16), 0), ((tile, BF16), 0), (((tiles, 2, lanes), F32), 0)],
        [vec(3)], prefetch=scalars, flops=2 * cell_flops,
    )
    made0 = product(after(got0, z0), True)
    prod0 = exchange(made0)
    sides0 = assemble(after(got0, made0))
    edges1, z1 = cell_call(
        functools.partial(mix_edge_kernel, cpd, q, 0), steps,
        [
            (after(prod0, sides0), 1), (z0, 0), (gate0, 0), (flags, 0), (owt[0], None), (hidden_gain, None),
            (hidden_bias, None), (wt[1], None), (input_gain, None), (input_bias, None),
        ],
        [((edge_shape, BF16), 2), ((tile, F32), 0)], [vec(4)], flops=5 * cell_flops,
    )
    got1 = exchange(edges1)
    fac1, low1, nrm1, inv1, gate1 = keep(1, after(z1, edges1), True)
    made1 = product(after(got1, gate1), False)
    prod1 = exchange(made1)
    sides1 = assemble(after(got1, made1))

    (grad1,) = cell_call(
        functools.partial(mix_back_kernel, cpd, q, 1), steps,
        [(after(prod1, sides1), 1), (up, 0), (gate1, 0), (mixer[1], None), (hidden_gain, None)],
        [((cell_shape, BF16), 1)], [vec(1)], flops=cell_flops,
    )
    got_grad1 = exchange(grad1)
    hnrm0, hinv0 = cell_call(
        functools.partial(keep_product_kernel, cpd, q), steps, [(after(prod0, grad1), 1)],
        [((tile, BF16), 0), (((tiles, 1, lanes), F32), 0)], [],
    )
    made_grads1 = product_grad(sides1, after(got_grad1, hnrm0), False)
    grads1 = exchange(made_grads1)
    glog1, terms1 = cell_call(
        functools.partial(mix_terms_kernel, cpd, q, 1), steps,
        [
            (after(prod1, made_grads1), 1), (up, 0), (gate1, 0), (flags, 0), (mixer[1], None), (owt[1], None),
            (hidden_gain, None), (hidden_bias, None),
        ],
        [((tile, BF16), 0), ((terms_shape, F32), None)],
        [vec(2), acc(hidden), acc(cols), acc(cols), acc(cols)], flops=3 * cell_flops,
    )
    up0, grad0 = cell_call(
        functools.partial(edge_mix_back_kernel, cpd, q, 1), steps,
        halves(after(grads1, glog1))
        + [
            (fac1, 0), (nrm1, 0), (inv1, 0), (glog1, 0), (up, 0), (weight[1], None), (input_gain, None),
            (hnrm0, 0), (hinv0, 0), (gate0, 0), (mixer[0], None), (hidden_gain, None),
        ],
        [((tile, F32), 0), ((cell_shape, BF16), 1)],
        [vec(2)], flops=6 * cell_flops,
    )
    got_grad0 = exchange(grad0)
    glog0, early = cell_call(
        functools.partial(late_terms_kernel, cpd, q, 1), steps,
        halves(after(grads1, grad0))
        + [
            (fac1, 0), (low1, 0), (nrm1, 0), (glog1, 0), (weight[1], None), (terms1, None), (prod0, 1),
            (up0, 0), (gate0, 0), (flags, 0), (mixer[0], None), (owt[0], None), (hidden_gain, None),
            (hidden_bias, None),
        ],
        [((tile, BF16), 0), (((devices * early_rows, hidden), BF16), None)],
        [vec(2), acc(5 * hidden, 2 * width + 16), acc(hidden), acc(cols), acc(cols), acc(cols)],
        flops=13 * cell_flops,
    )

    made_grads0 = product_grad(sides0, got_grad0, True, early.reshape(devices, early_rows, hidden))
    grads0 = exchange(made_grads0)
    fac0, low0, nrm0, inv0 = keep(0, after(z0, made_grads0), False)
    grads0 = after(grads0, nrm0)
    (late,) = cell_call(
        functools.partial(last_terms_kernel, cpd, q), steps,
        halves(grads0) + [(fac0, 0), (low0, 0), (nrm0, 0), (glog0, 0), (weight[0], None)],
        [(((devices * late_rows, hidden), BF16), None)],
        [acc(5 * hidden, 2 * width + 16)], flops=10 * cell_flops, vmem=ALL_VMEM,
    )
    got_late = exchange(late.reshape(devices, late_rows, hidden))
    (grad_pair,) = cell_call(
        functools.partial(pair_grad_kernel, cpd, q, 0), steps,
        halves(after(grads0, late))
        + [(fac0, 0), (nrm0, 0), (inv0, 0), (glog0, 0), (up0, 0), (weight[0], None), (input_gain, None)],
        [((pair_rep.shape, BF16), 0)], [vec(1)], flops=5 * cell_flops, vmem=ALL_VMEM,
    )
    (spread,) = cell_call(
        spread_kernel, 1,
        [(grads0, (1, 2 * side // early_rows, early_rows)), (after(got_late, grad_pair), None)],
        [(((devices, early_rows + late_rows, hidden), BF16), None)], [], vmem=ALL_VMEM,
    )
    proj, out, inorm, hnorm, chain = whole_call(
        functools.partial(unpack_kernel, 1.0 / length, early_rows), [exchange(spread)],
        [
            ((2, width, 5 * hidden), F32), ((2, hidden, hidden), F32), ((2, 2, hidden), F32),
            ((2, 2, hidden), F32), ((2, hidden), F32),
        ],
        [], 0,
    )
    return grad_pair, proj, out, inorm, hnorm, chain


def solution(mesh):
    cells = P(("grp", "row"), "col", None)
    return jax.shard_map(
        shards,
        mesh=mesh,
        in_specs=(cells, cells, P("grp"), P("grp")) + (P(),) * 7,
        out_specs=(
            cells, P("grp", None, None), P("grp", None, None), P("grp", None, None),
            P("grp", None, None), P("grp", None),
        ),
        check_vma=False,
    )
```
